32 devices in a mesh: groups: 2 (over x), frames: 16 (over z, y, core).
Axes of the slice: x: 2, y: 2, z: 4, core: 2. Of those that a mesh axis runs over, the one named last changes fastest.
Arguments:
- latents: bfloat16 [256, 32, 512], P(('groups', 'frames')), parts along dimension 0, may hold values from -6 to 6
- timestep: int32 [256], P(('groups', 'frames')), parts along dimension 0, may hold values from 0 to 49, as said below
- lookback: int32 [256], P(('groups', 'frames')), parts along dimension 0, may hold values from 1 to 8, as said below
- modulation: bfloat16 [2, 50, 4, 512], replicated, may hold values from -2.390625 to 2.390625
- input_weight: bfloat16 [2, 512, 2304], replicated, may hold values from -0.25 to 0.25
- step_weight: bfloat16 [2, 512, 16], replicated, may hold values from -0.25 to 0.25
- conv_weight: float32 [2, 4, 1280], replicated, may hold values from -3 to 3
- step_bias: float32 [2, 50, 16], replicated, may hold values from -3 to 2
- decay_log: float32 [2, 16], replicated
- skip_gain: float32 [2, 16], replicated, may hold values from -2 to 2
- norm_gain: float32 [2, 1024], replicated, may hold values from 0.1 to 1.9
- output_weight: bfloat16 [2, 1024, 512], replicated, may hold values from -0.1875 to 0.1875
- query_weight: bfloat16 [2, 512, 512], replicated
- memory_weight: bfloat16 [2, 512, 1024], replicated
- merge_weight: bfloat16 [2, 512, 512], replicated, may hold values from -0.25 to 0.25
Outputs:
- denoised: float32 [256, 32, 512], P(('groups', 'frames')), parts along dimension 0
The draws below stay inside these ranges and needn't reach their ends.
There are 2 independent parts, one for each index of `groups`. The reference program is written for one: setup_inputs(seed, part) draws one part's arguments, and reference() takes and returns one part's arrays. A program takes and returns all parts, laid end to end along the dimension named above; an argument that names none is the same for every part. Nothing has to cross between parts.
Inputs may be any that keep to these rules, and one draw needn't show every extreme that they name: timestep is the same for all frames of each aligned run of 8 frames. lookback[f] counts the preceding frames that frame f attends to; 8 occurs in every draw.
All inputs are finite; a program needn't handle non-finite values.
Results may differ from the reference program's by a relative error of at most 0.01.
Values may be sent and summed in bfloat16 or wider, within the bound.
No kernel may reach another device: no remote copies, remote signals or barrier semaphores. Data moves between devices by JAX's collectives and lax.ppermute only.
A program may use at most 128 MiB of HBM per device.

```python
import math
import jax
import jax.numpy as jnp
from jax import lax

D = 512
HEADS = 16
HEAD_DIM = 64
STATE = 128
ATT_HEADS = 8
NSTEPS = 50
LAYERS = 2
CONV = 4
SPAN = 128
WINDOW = 8
TPF = 32
INNER = 1024
ATTN = 512
FRAMES = 128
TOKENS = 4096


def draw_timestep(key, part):
    groups = jax.random.randint(key, (FRAMES // WINDOW,), 0, NSTEPS)
    return jnp.repeat(groups, WINDOW).astype(jnp.int32)


def draw_lookback(key, part):
    first_key, second_key = jax.random.split(key)
    counts = jax.random.randint(first_key, (FRAMES,), 1, WINDOW + 1)
    where_full = jax.random.randint(second_key, (), 0, FRAMES)
    return counts.at[where_full].set(WINDOW).astype(jnp.int32)


def draw_decay_log(key, part):
    ranks = jnp.stack([jax.random.permutation(jax.random.fold_in(key, 11 + layer), HEADS) for layer in range(LAYERS)])
    fast_count = HEADS // 2
    slow_rate = jnp.exp(jax.random.uniform(jax.random.fold_in(key, 1), (LAYERS, HEADS), jnp.float32, math.log(0.7), math.log(2.5))) / TOKENS
    fast_rate = jax.random.uniform(jax.random.fold_in(key, 2), (LAYERS, HEADS), jnp.float32, 0.6, 1.5) / 32.0
    return jnp.log(jnp.where(ranks < fast_count, fast_rate, slow_rate)).astype(jnp.float32)


def key_columns(key):
    return jax.random.normal(jax.random.fold_in(key, 7), (LAYERS, D, ATT_HEADS * HEAD_DIM), jnp.float32) * D ** (-0.5)


def draw_memory_weight(key, part):
    value_part = jax.random.normal(jax.random.fold_in(key, 8), (LAYERS, D, ATT_HEADS * HEAD_DIM), jnp.float32) * D ** (-0.5)
    return jnp.concatenate([key_columns(key), value_part], axis=2).astype(jnp.bfloat16)


def draw_query_weight(key, part):
    values = jax.random.normal(jax.random.fold_in(key, 9), (LAYERS, D, ATT_HEADS * HEAD_DIM), jnp.float32) * D ** (-0.5)
    return values.astype(jnp.bfloat16)


def levels(rng, dims, shards, least, largest):
    def one(dim, parts):
        steps = jax.random.uniform(jax.random.fold_in(jax.random.fold_in(rng, 6), dim), (parts,), jnp.float32, least / len(shards), largest / len(shards))
        return jnp.repeat(jnp.exp(steps), dims[dim] // parts).reshape((-1,) + (1,) * (len(dims) - dim - 1))

    level = one(*shards[0])
    for cut in shards[1:]:
        level = level * one(*cut)
    return level


def normal_values(rng, extent, scale, most, pieces=(), kind=jnp.bfloat16):
    level = levels(rng, extent, pieces, -0.22, 0.18) if pieces else 1.0
    drawn = jax.random.normal(rng, extent, jnp.float32) * scale * level
    return jnp.minimum(jnp.maximum(drawn, -most), most).astype(kind)


def setup_inputs(seed: int = 0, part: int = 0) -> dict:
    streams_of = jax.random.split(jax.random.key(seed), 16)
    part_splits = jax.random.split(jax.random.fold_in(streams_of[15], part), 16)
    return {
        "latents": normal_values(part_splits[0], (FRAMES, TPF, D), 1.0, 6.0, ((0, 16),)),
        "timestep": draw_timestep(jax.random.fold_in(jax.random.fold_in(streams_of[15], part), 71), part),
        "lookback": draw_lookback(jax.random.fold_in(jax.random.fold_in(streams_of[15], part), 71), part),
        "modulation": normal_values(streams_of[3], (LAYERS, NSTEPS, 4, D), 0.4, 2.390625),
        "input_weight": normal_values(streams_of[4], (LAYERS, D, 2 * INNER + 2 * STATE), D ** -0.5, 0.25),
        "step_weight": normal_values(streams_of[5], (LAYERS, D, HEADS), D ** -0.5, 0.25),
        "conv_weight": normal_values(streams_of[6], (LAYERS, CONV, INNER + 2 * STATE), 0.5, 3.0, (), jnp.float32),
        "step_bias": jnp.clip(jax.random.uniform(streams_of[7], (LAYERS, NSTEPS, HEADS), jnp.float32, -3.0, 2.0), -3.0, 2.0),
        "decay_log": draw_decay_log(jax.random.fold_in(streams_of[15], 71), part),
        "skip_gain": jnp.clip(jax.random.uniform(streams_of[9], (LAYERS, HEADS), jnp.float32, -2.0, 2.0), -2.0, 2.0),
        "norm_gain": jnp.clip(1.0 + 0.18 * jax.random.normal(streams_of[10], (LAYERS, INNER), jnp.float32), 0.1, 1.9),
        "output_weight": normal_values(streams_of[11], (LAYERS, INNER, D), INNER ** -0.5, 0.1875),
        "query_weight": draw_query_weight(jax.random.fold_in(streams_of[15], 71), part),
        "memory_weight": draw_memory_weight(jax.random.fold_in(streams_of[15], 71), part),
        "merge_weight": normal_values(streams_of[14], (LAYERS, ATTN, D), ATTN ** -0.5, 0.25),
    }


EPS = 1e-06
HEAD_EPS = 1e-05

def rms_rows(values):
    return values * lax.rsqrt(lax.optimization_barrier(jnp.mean(values * values, axis=-1, keepdims=True)) + EPS)

def modulated(resid, shift, scale):
    normed = rms_rows(resid.astype(jnp.float32))
    return (normed * (1.0 + scale[:, None, :]) + shift[:, None, :]).astype(jnp.bfloat16)

def conv_silu(extended, weights, count):
    total = weights[0][None, :] * extended[0:count].astype(jnp.float32)
    for offset in range(1, CONV):
        total = total + weights[offset][None, :] * extended[offset:offset + count].astype(jnp.float32)
    return jax.nn.silu(total).astype(jnp.bfloat16)

def span_terms(values, input_map, output_map, log_decay, step_size):
    count = values.shape[0] // SPAN
    by_head = values.reshape(count, SPAN, HEADS, HEAD_DIM).astype(jnp.float32)
    in_blocks = input_map.reshape(count, SPAN, STATE).astype(jnp.float32)
    out_blocks = output_map.reshape(count, SPAN, STATE).astype(jnp.float32)
    cumulated = jnp.cumsum(log_decay.reshape(count, SPAN, HEADS), axis=1).transpose(0, 2, 1)
    steps = step_size.reshape(count, SPAN, HEADS).transpose(0, 2, 1)
    affinity = jnp.einsum('cqn,csn->cqs', out_blocks, in_blocks)
    position = jnp.arange(SPAN)
    lower = position[:, None] >= position[None, :]
    gaps = cumulated[:, :, :, None] - cumulated[:, :, None, :]
    gaps = jnp.where(lower[None, None], gaps, -jnp.inf)
    mixing = (affinity[:, None] * jnp.exp(gaps) * steps[:, :, None, :]).astype(jnp.bfloat16)
    y_local = jnp.einsum('chqs,cshp->cqhp', mixing.astype(jnp.float32), by_head)
    edge = jnp.exp(cumulated[:, :, -1:] - cumulated) * steps
    weighted = (in_blocks[:, None, :, :] * edge[:, :, :, None]).astype(jnp.bfloat16)
    states = jnp.einsum('cshp,chsn->chpn', by_head, weighted.astype(jnp.float32))
    return (y_local, states, cumulated, out_blocks)

def finish_mixer(resid, y_total, values, gate_half, skip, gain, weight):
    rows = values.shape[0]
    mixed = y_total.reshape(rows, HEADS * HEAD_DIM) + jnp.repeat(skip, HEAD_DIM)[None, :] * values.astype(jnp.float32)
    gated = (mixed * jax.nn.silu(gate_half.astype(jnp.float32))).reshape(rows, HEADS, HEAD_DIM)
    gated = gated * lax.rsqrt(lax.optimization_barrier(jnp.mean(gated * gated, axis=-1, keepdims=True)) + HEAD_EPS)
    normed = (gated.reshape(rows, HEADS * HEAD_DIM) * gain[None, :]).astype(jnp.bfloat16)
    update = jnp.dot(normed, weight, preferred_element_type=jnp.float32)
    return resid + update.reshape(resid.shape)

def attend(query_block, key_block, query_frame, key_frame, reach):
    count, tok_frame, attn = query_block.shape
    heads = attn // HEAD_DIM
    queries = query_block.reshape(count * tok_frame, heads, HEAD_DIM).astype(jnp.float32)
    key_rows = key_block[:, :, :attn].reshape(-1, heads, HEAD_DIM).astype(jnp.float32)
    value_rows = key_block[:, :, attn:].reshape(-1, heads, HEAD_DIM).astype(jnp.float32)
    scores = jnp.einsum('qhd,khd->hqk', queries, key_rows) * HEAD_DIM ** (-0.5)
    allowed = (key_frame[None, :] >= 0) & (key_frame[None, :] <= query_frame[:, None]) & (key_frame[None, :] >= query_frame[:, None] - reach[:, None])
    allowed = jnp.repeat(jnp.repeat(allowed, tok_frame, axis=0), tok_frame, axis=1)
    scores = jnp.where(allowed[None], scores, -1e+30)
    top = lax.optimization_barrier(jnp.max(scores, axis=-1, keepdims=True))
    weights = jnp.exp(scores - top)
    probs = (weights / lax.optimization_barrier(jnp.sum(weights, axis=-1, keepdims=True))).astype(jnp.bfloat16)
    mixed = jnp.einsum('hqk,khd->qhd', probs.astype(jnp.float32), value_rows)
    return mixed.astype(jnp.bfloat16).reshape(count, tok_frame, attn)

def reference(latents, timestep, lookback, modulation, input_weight, step_weight, conv_weight, step_bias, decay_log, skip_gain, norm_gain, output_weight, query_weight, memory_weight, merge_weight):
    inner = HEADS * HEAD_DIM
    attn = ATT_HEADS * HEAD_DIM
    resid = latents.astype(jnp.float32)
    for layer in range(LAYERS):
        mods = modulation[layer][timestep].astype(jnp.float32)
        frame_bias = step_bias[layer][timestep]
        u_rows = modulated(resid, mods[:, 0], mods[:, 1]).reshape(-1, D)
        projected = jnp.dot(u_rows, input_weight[layer], preferred_element_type=jnp.float32).astype(jnp.bfloat16)
        gate_half = projected[:, :inner]
        mixed_in = projected[:, inner:]
        step_raw = jnp.dot(u_rows, step_weight[layer], preferred_element_type=jnp.float32)
        step_raw = (step_raw.reshape(FRAMES, TPF, HEADS) + frame_bias[:, None, :]).reshape(-1, HEADS)
        extended = jnp.concatenate([jnp.zeros((CONV - 1, mixed_in.shape[1]), jnp.bfloat16), mixed_in], axis=0)
        act = conv_silu(extended, conv_weight[layer], mixed_in.shape[0])
        values = act[:, :inner]
        input_map = act[:, inner:inner + STATE]
        output_map = act[:, inner + STATE:]
        step_size = jax.nn.softplus(step_raw)
        log_decay = -jnp.exp(decay_log[layer])[None, :] * step_size
        y_local, states, cumulated, out_blocks = span_terms(values, input_map, output_map, log_decay, step_size)

        def walk(carry, item):
            state, ends = item
            return (jnp.exp(ends)[:, None, None] * carry + state, carry)
        final_state, before = lax.scan(walk, jnp.zeros((HEADS, HEAD_DIM, STATE), jnp.float32), (states, cumulated[:, :, -1]))
        y_carry = jnp.einsum('cqn,chpn->cqhp', out_blocks, before, precision=lax.Precision.HIGHEST)
        y_carry = y_carry * jnp.exp(cumulated).transpose(0, 2, 1)[:, :, :, None]
        hidden = finish_mixer(resid, y_local + y_carry, values, gate_half, skip_gain[layer], norm_gain[layer], output_weight[layer])
        a_rows = modulated(hidden, mods[:, 2], mods[:, 3]).reshape(-1, D)
        queries = jnp.dot(a_rows, query_weight[layer], preferred_element_type=jnp.float32).astype(jnp.bfloat16).reshape(FRAMES, TPF, attn)
        memory = jnp.dot(a_rows, memory_weight[layer], preferred_element_type=jnp.float32).astype(jnp.bfloat16).reshape(FRAMES, TPF, 2 * attn)
        padded = jnp.concatenate([jnp.zeros((WINDOW, TPF, 2 * attn), jnp.bfloat16), memory], axis=0)

        def one_block(block):
            start = (block * WINDOW).astype(jnp.int32)
            query_block = lax.dynamic_slice_in_dim(queries, start, WINDOW, 0)
            key_block = lax.dynamic_slice_in_dim(padded, start, 2 * WINDOW, 0)
            reach = lax.dynamic_slice_in_dim(lookback, start, WINDOW, 0)
            query_frame = start + jnp.arange(WINDOW, dtype=jnp.int32)
            key_frame = start - WINDOW + jnp.arange(2 * WINDOW, dtype=jnp.int32)
            return attend(query_block, key_block, query_frame, key_frame, reach)
        attended = lax.map(one_block, jnp.arange(FRAMES // WINDOW, dtype=jnp.int32)).reshape(-1, attn)
        update = jnp.dot(attended, merge_weight[layer], preferred_element_type=jnp.float32)
        resid = hidden + update.reshape(hidden.shape)
    return resid
```

```python
import functools

import jax
import jax.numpy as jnp
from jax import lax
from jax.experimental import pallas as pl
from jax.experimental.pallas import tpu as pltpu
from jax.sharding import PartitionSpec as P

HEADS = 16
HEAD_DIM = 64
STATE = 128
ATT_HEADS = 8
LAYERS = 2
CONV = 4
SPAN = 128
WINDOW = 8
EPS = 1e-06
HEAD_EPS = 1e-05
INNER = HEADS * HEAD_DIM
ATTN = ATT_HEADS * HEAD_DIM
PAD = 16
LANES = 128
TAIL = 16
F32 = jnp.float32
BF16 = jnp.bfloat16


def dot(a, b, dims=((1,), (0,)), precision=None):
    return lax.dot_general(a, b, (dims, ((), ())), precision=precision, preferred_element_type=F32)


def rms_mod(x, shift, scale):
    normed = x * lax.rsqrt(jnp.mean(x * x, axis=-1, keepdims=True) + EPS)
    return (normed * (1.0 + scale) + shift).astype(BF16)


def spread(per_head):
    high = per_head.astype(BF16)
    rest = per_head - high.astype(F32)
    middle = rest.astype(BF16)
    low = (rest - middle.astype(F32)).astype(BF16)
    row = lax.broadcasted_iota(jnp.int32, (HEADS, INNER), 0)
    head = lax.broadcasted_iota(jnp.int32, (HEADS, INNER), 1) // HEAD_DIM
    sel = jnp.where(row == head, 1.0, 0.0).astype(BF16)
    return dot(high, sel) + dot(middle, sel) + dot(low, sel)


def first_kernel(x_ref, mods_ref, u_ref, tail_ref):
    rows = x_ref.shape[0]
    u = rms_mod(x_ref[...].astype(F32), mods_ref[0:1, :], mods_ref[1:2, :])
    u_ref[...] = u
    tail_ref[...] = u[rows - TAIL :]


def local_kernel(
    parts,
    u_ref,
    tail_ref,
    w_ref,
    sw_ref,
    conv_ref,
    bias_ref,
    decay_ref,
    skip_ref,
    gate_ref,
    y_ref,
    out_map_ref,
    cum_ref,
    send_ref,
    ext_ref,
    act_ref,
):
    rows = u_ref.shape[0]
    u = u_ref[...]
    tail = tail_ref[...]
    chunk = 256
    for c in range(0, INNER, chunk):
        gate_ref[:, c : c + chunk] = dot(u, w_ref[:, c : c + chunk]).astype(BF16)
    for c in range(0, INNER + 2 * STATE, chunk):
        w = w_ref[:, INNER + c : INNER + c + chunk]
        ext_ref[0:TAIL, :] = dot(tail, w).astype(BF16).astype(F32)
        ext_ref[TAIL:, :] = dot(u, w).astype(BF16).astype(F32)
        total = None
        for k in range(CONV):
            start = TAIL - (CONV - 1) + k
            term = conv_ref[k : k + 1, c : c + chunk] * ext_ref[start : start + rows, :]
            total = term if total is None else total + term
        act_ref[:, c : c + chunk] = (total * jax.nn.sigmoid(total)).astype(BF16)

    raw = dot(u, sw_ref[...]) + bias_ref[...]
    step = jnp.maximum(raw, 0.0) + jnp.log1p(jnp.exp(-jnp.abs(raw)))
    log_decay = -jnp.exp(decay_ref[...]) * step
    log_step = jnp.log(step)

    q_pos = lax.broadcasted_iota(jnp.int32, (SPAN, SPAN), 0)
    s_pos = lax.broadcasted_iota(jnp.int32, (SPAN, SPAN), 1)
    lower = q_pos >= s_pos
    lower_f = jnp.where(lower, 1.0, 0.0).astype(F32)
    lane = lax.broadcasted_iota(jnp.int32, (SPAN, LANES), 1)
    left = lane < HEAD_DIM
    zero = jnp.zeros((SPAN, LANES), BF16)
    skip = skip_ref[...]

    before = jnp.zeros((1, HEADS), F32)
    state = None
    for b in range(rows // SPAN):
        r = slice(b * SPAN, (b + 1) * SPAN)
        cum = dot(lower_f, log_decay[r], precision=lax.Precision.HIGHEST)
        end = cum[SPAN - 1 : SPAN, :]
        cum_ref[r, :] = cum + before
        before = before + end
        shifted = (cum - log_step[r]).T
        edge = jnp.exp(end - cum) * step[r]
        in_map = act_ref[r, INNER : INNER + STATE]
        out_map = act_ref[r, INNER + STATE :]
        out_map_ref[r, :] = out_map
        affinity = dot(out_map, in_map, ((1,), (1,)))
        if state is not None:
            entering = dot(out_map, state.astype(BF16)) * spread(jnp.exp(cum))
        for pair in range(HEADS // 2):
            cols = slice(pair * LANES, (pair + 1) * LANES)
            values = act_ref[r, cols]
            mixing = []
            for h in (2 * pair, 2 * pair + 1):
                gap = cum[:, h : h + 1] - shifted[h : h + 1, :]
                mixing.append(jnp.where(lower, affinity * jnp.exp(gap), 0.0).astype(BF16))
            both = jnp.concatenate(mixing, axis=1)
            stacked = jnp.concatenate(
                [jnp.where(left, values, zero), jnp.where(left, zero, values)], axis=0
            )
            y = dot(both, stacked) + skip[:, cols] * values.astype(F32)
            if state is not None:
                y = y + entering[:, cols]
            y_ref[r, cols] = y
        scaled = (act_ref[r, 0:INNER].astype(F32) * spread(edge)).astype(BF16)
        term = dot(in_map, scaled, ((0,), (0,)))
        if state is None:
            state = term
        else:
            state = spread(jnp.broadcast_to(jnp.exp(end), (8, HEADS)))[0:1, :] * state + term

    part_rows = INNER // parts
    held = max(1, part_rows // HEAD_DIM)
    pad_row = lax.broadcasted_iota(jnp.int32, (PAD, LANES), 0)
    for pair in range(HEADS // 2):
        turned = state[:, pair * LANES : (pair + 1) * LANES].T.astype(BF16)
        for k in range(LANES // min(part_rows, LANES)):
            first = pair * LANES + k * min(part_rows, LANES)
            part, at = first // part_rows, first % part_rows
            size = min(part_rows, LANES)
            send_ref[part, at : at + size, :] = turned[k * size : (k + 1) * size, :]
    for part in range(parts):
        pad = jnp.zeros((PAD, LANES), F32)
        for i in range(held):
            h = part * part_rows // HEAD_DIM + i
            decay = jnp.broadcast_to(before[:, h : h + 1], (PAD, LANES))
            high = decay.astype(BF16).astype(F32)
            pad = jnp.where(pad_row == 2 * i, high, jnp.where(pad_row == 2 * i + 1, decay - high, pad))
        send_ref[part, part_rows:, :] = pad.astype(BF16)


def scan_kernel(got_ref, back_ref):
    parts, padded, _ = got_ref.shape
    part_rows = padded - PAD
    held = max(1, part_rows // HEAD_DIM)
    size = part_rows // held
    carry = [jnp.zeros((size, LANES), F32) for _ in range(held)]
    for d in range(parts):
        pad = got_ref[d, part_rows:, :].astype(F32)
        for i in range(held):
            rows = slice(i * size, (i + 1) * size)
            back_ref[d, rows, :] = carry[i].astype(BF16)
            decay = jnp.exp(pad[2 * i : 2 * i + 1, :] + pad[2 * i + 1 : 2 * i + 2, :])
            carry[i] = decay * carry[i] + got_ref[d, rows, :].astype(F32)


def finish_kernel(
    enter_ref,
    out_map_ref,
    cum_ref,
    y_ref,
    gate_ref,
    resid_ref,
    w_ref,
    gain_ref,
    mods_ref,
    hidden_ref,
    a_ref,
    normed_ref,
):
    out_map = out_map_ref[...]
    scale = jnp.exp(cum_ref[...])
    chunk = 256
    row = lax.broadcasted_iota(jnp.int32, (chunk, chunk), 0) // HEAD_DIM
    col = lax.broadcasted_iota(jnp.int32, (chunk, chunk), 1) // HEAD_DIM
    same = jnp.where(row == col, 1.0 / HEAD_DIM, 0.0).astype(BF16)
    wide = spread(scale)
    for c in range(0, INNER, chunk):
        cols = slice(c, c + chunk)
        carried = dot(out_map, enter_ref[cols, :], ((1,), (1,)))
        gate = gate_ref[:, cols].astype(F32)
        total = (y_ref[:, cols] + carried * wide[:, cols]) * (gate * jax.nn.sigmoid(gate))
        square = total * total
        high = square.astype(BF16)
        low = (square - high.astype(F32)).astype(BF16)
        mean = dot(high, same) + dot(low, same)
        normed_ref[:, cols] = (total * lax.rsqrt(mean + HEAD_EPS) * gain_ref[:, cols]).astype(BF16)
    hidden = resid_ref[...].astype(F32) + dot(normed_ref[...], w_ref[...])
    hidden_ref[...] = hidden
    a_ref[...] = rms_mod(hidden, mods_ref[2:3, :], mods_ref[3:4, :])


def memory_kernel(a_ref, wq_ref, wm_ref, q_ref, kv_ref):
    a = a_ref[...]
    q_ref[...] = (dot(a, wq_ref[...]).astype(BF16).astype(F32) * HEAD_DIM**-0.5).astype(BF16)
    kv_ref[...] = dot(a, wm_ref[...]).astype(BF16)


def attend_kernel(
    last,
    tok_frame,
    base_ref,
    reach_ref,
    q_ref,
    kv_ref,
    prev_ref,
    wm_ref,
    merge_ref,
    hidden_ref,
    mods_ref,
    *rest,
):
    if last:
        resid_ref, keyed_ref, bias_ref, out_ref = rest
    else:
        resid_ref, u_ref, tail_ref, keyed_ref, bias_ref, out_ref = rest
    rows = q_ref.shape[0]
    keyed_ref[0:rows, :] = dot(prev_ref[...], wm_ref[...]).astype(BF16)
    keyed_ref[rows:, :] = kv_ref[...]
    key_frame = lax.broadcasted_iota(jnp.int32, (tok_frame, 2 * rows), 1) // tok_frame
    first = WINDOW - base_ref[0]
    for f in range(WINDOW):
        low = jnp.maximum(first, f + WINDOW - reach_ref[f])
        seen = (key_frame >= low) & (key_frame <= f + WINDOW)
        bias_ref[f * tok_frame : (f + 1) * tok_frame, :] = jnp.where(seen, 0.0, -1e30)
    half = rows // 2
    span = rows + half
    q_left = lax.broadcasted_iota(jnp.int32, (half, LANES), 1) < HEAD_DIM
    k_left = lax.broadcasted_iota(jnp.int32, (span, LANES), 1) < HEAD_DIM
    one = jnp.ones((span, LANES), BF16)
    zero = jnp.zeros((half, LANES), BF16)
    for part in range(2):
        r = slice(part * half, (part + 1) * half)
        k_rows = slice(part * half, part * half + span)
        bias = bias_ref[r, k_rows]
        for pair in range(ATT_HEADS // 2):
            cols = slice(pair * LANES, (pair + 1) * LANES)
            query = q_ref[r, cols]
            keys = keyed_ref[k_rows, cols]
            values = keyed_ref[k_rows, ATTN + pair * LANES : ATTN + (pair + 1) * LANES]
            sides = []
            for side in range(2):
                mine = q_left if side == 0 else ~q_left
                own = k_left if side == 0 else ~k_left
                scores = dot(jnp.where(mine, query, zero), keys, ((1,), (1,))) + bias
                top = jnp.max(scores, axis=-1, keepdims=True)
                weights = jnp.exp(scores - top).astype(BF16)
                sides.append(dot(weights, jnp.where(own, values, one)))
            number = jnp.where(q_left, sides[0], sides[1])
            total = pltpu.roll(jnp.where(q_left, sides[1], sides[0]), HEAD_DIM, 1)
            out_ref[r, cols] = (number / total).astype(BF16)
    resid = hidden_ref[...] + dot(out_ref[...], merge_ref[...])
    resid_ref[...] = resid
    if not last:
        u = rms_mod(resid, mods_ref[0:1, :], mods_ref[1:2, :])
        u_ref[...] = u
        tail_ref[...] = u[rows - TAIL :]


def whole(array):
    zeros = (0,) * array.ndim
    return pl.BlockSpec(array.shape, lambda i: zeros)


def layer_of(array, layer):
    zeros = (0,) * (array.ndim - 1)
    return pl.BlockSpec((None,) + array.shape[1:], lambda i: (layer,) + zeros)


SCALARS = pl.BlockSpec(memory_space=pltpu.SMEM)


def run(kernel, specs, operands, outs, scratch=(), name=None):
    return pl.pallas_call(
        kernel,
        grid=(1,),
        in_specs=specs,
        out_specs=[whole(o) for o in outs],
        out_shape=list(outs),
        scratch_shapes=list(scratch),
        compiler_params=pltpu.CompilerParams(vmem_limit_bytes=40 * 1024 * 1024),
        name=name,
    )(*operands)


def shape(dims, dtype):
    return jax.ShapeDtypeStruct(dims, dtype)


def from_behind(value, axis):
    count = lax.axis_size(axis)
    return lax.ppermute(value, axis, [(i, i + 1) for i in range(count - 1)])


def shards(
    latents,
    timestep,
    lookback,
    modulation,
    input_weight,
    step_weight,
    conv_weight,
    step_bias,
    decay_log,
    skip_gain,
    norm_gain,
    output_weight,
    query_weight,
    memory_weight,
    merge_weight,
):
    frames_dev, tok_frame, width = latents.shape
    rows = frames_dev * tok_frame
    parts = lax.axis_size("frames")
    part_rows = INNER // parts
    base = (lax.axis_index("frames") * frames_dev).astype(jnp.int32).reshape(1)
    mods = modulation[:, timestep[0]].astype(F32)
    bias = step_bias[:, timestep[0]][:, None, :]
    decay_log = decay_log[:, None, :]
    skip = jnp.repeat(skip_gain, HEAD_DIM, axis=1)[:, None, :]
    gain = norm_gain[:, None, :]
    resid = latents.reshape(rows, width)
    u, tail = run(
        first_kernel,
        [whole(resid), layer_of(mods, 0)],
        (resid, mods),
        [shape((rows, width), BF16), shape((TAIL, width), BF16)],
        name="first",
    )
    for layer in range(LAYERS):
        tail = from_behind(tail, "frames")
        per_layer = (input_weight, step_weight, conv_weight, bias, decay_log, skip)
        gate, y, out_map, cum, send = run(
            functools.partial(local_kernel, parts),
            [whole(u), whole(tail)] + [layer_of(p, layer) for p in per_layer],
            (u, tail) + per_layer,
            [
                shape((rows, INNER), BF16),
                shape((rows, INNER), F32),
                shape((rows, STATE), BF16),
                shape((rows, HEADS), F32),
                shape((parts, part_rows + PAD, LANES), BF16),
            ],
            [pltpu.VMEM((rows + TAIL, 256), F32), pltpu.VMEM((rows, INNER + 2 * STATE), BF16)],
            name="local",
        )
        got = lax.all_to_all(send, "frames", 0, 0)
        (back,) = run(
            scan_kernel,
            [whole(got)],
            (got,),
            [shape((parts, part_rows, LANES), BF16)],
            name="scan",
        )
        enter = lax.all_to_all(back, "frames", 0, 0).reshape(INNER, LANES)
        hidden, a = run(
            finish_kernel,
            [whole(enter), whole(out_map), whole(cum), whole(y), whole(gate), whole(resid)]
            + [layer_of(output_weight, layer), layer_of(gain, layer), layer_of(mods, layer)],
            (enter, out_map, cum, y, gate, resid, output_weight, gain, mods),
            [shape((rows, width), F32), shape((rows, width), BF16)],
            [pltpu.VMEM((rows, INNER), BF16)],
            name="finish",
        )
        prev = from_behind(a, "frames")
        q, kv = run(
            memory_kernel,
            [whole(a), layer_of(query_weight, layer), layer_of(memory_weight, layer)],
            (a, query_weight, memory_weight),
            [shape((rows, ATTN), BF16), shape((rows, 2 * ATTN), BF16)],
            name="memory",
        )
        last = layer == LAYERS - 1
        outs = [shape((rows, width), F32)]
        if not last:
            outs += [shape((rows, width), BF16), shape((TAIL, width), BF16)]
        result = run(
            functools.partial(attend_kernel, last, tok_frame),
            [SCALARS, SCALARS, whole(q), whole(kv), whole(prev)]
            + [layer_of(memory_weight, layer), layer_of(merge_weight, layer), whole(hidden)]
            + [layer_of(mods, min(layer + 1, LAYERS - 1))],
            (base, lookback, q, kv, prev, memory_weight, merge_weight, hidden, mods),
            outs,
            [
                pltpu.VMEM((2 * rows, 2 * ATTN), BF16),
                pltpu.VMEM((rows, 2 * rows), F32),
                pltpu.VMEM((rows, ATTN), BF16),
            ],
            name="attend",
        )
        resid = result[0]
        if not last:
            u, tail = result[1:]
    return resid.reshape(latents.shape)


def solution(mesh):
    sharded = P(("groups", "frames"))
    return jax.shard_map(
        shards,
        mesh=mesh,
        in_specs=(P(("groups", "frames"), None, None), sharded, sharded) + (P(),) * 12,
        out_specs=P(("groups", "frames"), None, None),
        check_vma=False,
    )
```

```python
import functools

import jax
import jax.numpy as jnp
from jax import lax
from jax.experimental import pallas as pl
from jax.experimental.pallas import tpu as pltpu
from jax.sharding import PartitionSpec as P

HEADS = 16
HEAD_DIM = 64
STATE = 128
ATT_HEADS = 8
LAYERS = 2
CONV = 4
SPAN = 128
WINDOW = 8
EPS = 1e-06
HEAD_EPS = 1e-05
INNER = HEADS * HEAD_DIM
ATTN = ATT_HEADS * HEAD_DIM
PAD = 16
LANES = 128
TAIL = 16
F32 = jnp.float32
BF16 = jnp.bfloat16


def dot(a, b, dims=((1,), (0,)), precision=None):
    return lax.dot_general(a, b, (dims, ((), ())), precision=precision, preferred_element_type=F32)


def rms_mod(x, shift, scale):
    normed = x * lax.rsqrt(jnp.mean(x * x, axis=-1, keepdims=True) + EPS)
    return (normed * (1.0 + scale) + shift).astype(BF16)


def spread(per_head):
    high = per_head.astype(BF16)
    low = (per_head - high.astype(F32)).astype(BF16)
    row = lax.broadcasted_iota(jnp.int32, (2 * HEADS, INNER), 0) % HEADS
    head = lax.broadcasted_iota(jnp.int32, (2 * HEADS, INNER), 1) // HEAD_DIM
    sel = jnp.where(row == head, 1.0, 0.0).astype(BF16)
    return dot(jnp.concatenate([high, low], axis=1), sel)


def spread_row(per_head):
    return spread(jnp.broadcast_to(per_head, (16, HEADS)))[0:1, :]


def mod_rows(mods_ref, layer, step, which):
    mods = mods_ref[layer, step].astype(F32)
    return mods[which : which + 1, :], mods[which + 1 : which + 2, :]


def first_kernel(step_ref, x_ref, mods_ref, u_ref, tail_ref):
    rows = x_ref.shape[0]
    u = rms_mod(x_ref[...].astype(F32), *mod_rows(mods_ref, 0, step_ref[0], 0))
    u_ref[...] = u
    tail_ref[...] = u[rows - TAIL :]


def local_kernel(
    layer,
    parts,
    step_ref,
    u_ref,
    tail_ref,
    w_ref,
    sw_ref,
    conv_ref,
    bias_ref,
    decay_ref,
    act_ref,
    cum_ref,
    shifted_ref,
    state_ref,
    send_ref,
    ext_ref,
):
    rows = u_ref.shape[0]
    u = u_ref[...]
    tail = tail_ref[...]
    nsteps = bias_ref.shape[-1]
    chosen = lax.broadcasted_iota(jnp.int32, (8, nsteps), 1) == step_ref[0]
    bias = dot(
        jnp.where(chosen, 1.0, 0.0).astype(F32),
        bias_ref[layer],
        ((1,), (1,)),
        precision=lax.Precision.HIGHEST,
    )[0:1, :]
    raw = dot(u, sw_ref[layer], ((1,), (1,))) + bias
    step = jnp.maximum(raw, 0.0) + jnp.log1p(jnp.exp(-jnp.abs(raw)))
    log_decay = -jnp.exp(decay_ref[layer : layer + 1, :]) * step
    log_step = jnp.log(step)
    q_pos = lax.broadcasted_iota(jnp.int32, (SPAN, SPAN), 0)
    s_pos = lax.broadcasted_iota(jnp.int32, (SPAN, SPAN), 1)
    lower = jnp.where(q_pos >= s_pos, 1.0, 0.0).astype(F32)
    ends, edges = [], []
    for b in range(rows // SPAN):
        r = slice(b * SPAN, (b + 1) * SPAN)
        cum = dot(lower, log_decay[r], precision=lax.Precision.HIGHEST)
        end = cum[SPAN - 1 : SPAN, :]
        cum_ref[r, :] = cum
        shifted_ref[:, r] = (cum - log_step[r]).T
        ends.append(end)
        edges.append(spread(jnp.exp(end - cum) * step[r]))

    chunk = 256
    for c in [INNER] + list(range(0, INNER, chunk)):
        w = w_ref[layer, :, INNER + c : INNER + c + chunk]
        slot = c // chunk % 2
        ext_ref[slot, 0:TAIL, :] = dot(tail, w).astype(BF16).astype(F32)
        ext_ref[slot, TAIL:, :] = dot(u, w).astype(BF16).astype(F32)
        total = None
        for k in range(CONV):
            start = TAIL - (CONV - 1) + k
            term = conv_ref[layer, k : k + 1, c : c + chunk] * ext_ref[slot, start : start + rows, :]
            total = term if total is None else total + term
        act_ref[:, c : c + chunk] = (total * jax.nn.sigmoid(total)).astype(BF16)

    state = None
    for b in range(rows // SPAN):
        r = slice(b * SPAN, (b + 1) * SPAN)
        in_map = act_ref[r, INNER : INNER + STATE]
        scaled = (act_ref[r, 0:INNER].astype(F32) * edges[b]).astype(BF16)
        term = dot(in_map, scaled, ((0,), (0,)))
        if state is None:
            state = term
        else:
            state_ref[(b - 1) * STATE : b * STATE, :] = state.astype(BF16)
            state = spread_row(jnp.exp(ends[b])) * state + term

    part_rows = INNER // parts
    held = max(1, part_rows // HEAD_DIM)
    size = min(part_rows, LANES)
    for pair in range(HEADS // 2):
        turned = state[:, pair * LANES : (pair + 1) * LANES].T.astype(BF16)
        for k in range(LANES // size):
            first = pair * LANES + k * size
            part, at = first // part_rows, first % part_rows
            send_ref[part, at : at + size, :] = turned[k * size : (k + 1) * size, :]
    pad_row = lax.broadcasted_iota(jnp.int32, (PAD, LANES), 0)
    over = sum(ends[1:], ends[0])
    for part in range(parts):
        pad = jnp.zeros((PAD, LANES), F32)
        for i in range(held):
            h = part * part_rows // HEAD_DIM + i
            decay = jnp.broadcast_to(over[:, h : h + 1], (PAD, LANES))
            high = decay.astype(BF16).astype(F32)
            pad = jnp.where(pad_row == 2 * i, high, jnp.where(pad_row == 2 * i + 1, decay - high, pad))
        send_ref[part, part_rows:, :] = pad.astype(BF16)


def mix_kernel(
    layer, u_ref, w_ref, act_ref, cum_ref, shifted_ref, state_ref, skip_ref, y_ref, wide_ref
):
    rows = u_ref.shape[0]
    u = u_ref[...]
    q_pos = lax.broadcasted_iota(jnp.int32, (SPAN, SPAN), 0)
    s_pos = lax.broadcasted_iota(jnp.int32, (SPAN, SPAN), 1)
    lower = q_pos >= s_pos
    lane = lax.broadcasted_iota(jnp.int32, (SPAN, LANES), 1)
    left = lane < HEAD_DIM
    zero = jnp.zeros((SPAN, LANES), BF16)
    skip = spread_row(skip_ref[layer : layer + 1, :])
    before = jnp.zeros((1, HEADS), F32)
    for b in range(rows // SPAN):
        r = slice(b * SPAN, (b + 1) * SPAN)
        cum = cum_ref[r, :]
        in_map = act_ref[r, INNER : INNER + STATE]
        out_map = act_ref[r, INNER + STATE :]
        affinity = dot(out_map, in_map, ((1,), (1,)))
        wide_ref[r, :] = spread(jnp.exp(cum + before))
        before = before + cum[SPAN - 1 : SPAN, :]
        if b:
            y_ref[r, :] = dot(out_map, state_ref[(b - 1) * STATE : b * STATE, :]) * spread(jnp.exp(cum))
        for pair in range(HEADS // 2):
            cols = slice(pair * LANES, (pair + 1) * LANES)
            values = act_ref[r, cols]
            mixing = []
            for h in (2 * pair, 2 * pair + 1):
                gap = cum[:, h : h + 1] - shifted_ref[h : h + 1, r]
                mixing.append(jnp.where(lower, affinity * jnp.exp(gap), 0.0).astype(BF16))
            both = jnp.concatenate(mixing, axis=1)
            stacked = jnp.concatenate(
                [jnp.where(left, values, zero), jnp.where(left, zero, values)], axis=0
            )
            y = dot(both, stacked) + skip[:, cols] * values.astype(F32)
            if b:
                y = y + y_ref[r, cols]
            gate = dot(u[r], w_ref[layer, :, cols]).astype(BF16).astype(F32)
            gate = gate * jax.nn.sigmoid(gate)
            y_ref[r, cols] = y * gate
            wide_ref[r, cols] = wide_ref[r, cols] * gate


def scan_kernel(got_ref, back_ref):
    parts, padded, _ = got_ref.shape
    part_rows = padded - PAD
    held = max(1, part_rows // HEAD_DIM)
    size = part_rows // held
    carry = [jnp.zeros((size, LANES), F32) for _ in range(held)]
    for d in range(parts):
        pad = got_ref[d, part_rows:, :].astype(F32)
        for i in range(held):
            rows = slice(i * size, (i + 1) * size)
            back_ref[d, rows, :] = carry[i].astype(BF16)
            decay = jnp.exp(pad[2 * i : 2 * i + 1, :] + pad[2 * i + 1 : 2 * i + 2, :])
            carry[i] = decay * carry[i] + got_ref[d, rows, :].astype(F32)


def finish_kernel(
    layer,
    step_ref,
    enter_ref,
    act_ref,
    y_ref,
    wide_ref,
    resid_ref,
    w_ref,
    gain_ref,
    mods_ref,
    hidden_ref,
    a_ref,
    normed_ref,
):
    out_map = act_ref[:, INNER + STATE :]
    chunk = 256
    row = lax.broadcasted_iota(jnp.int32, (chunk, chunk), 0) // HEAD_DIM
    col = lax.broadcasted_iota(jnp.int32, (chunk, chunk), 1) // HEAD_DIM
    same = jnp.where(row == col, 1.0 / HEAD_DIM, 0.0).astype(BF16)
    for c in range(0, INNER, chunk):
        cols = slice(c, c + chunk)
        carried = dot(out_map, enter_ref[cols, :], ((1,), (1,)))
        total = y_ref[:, cols] + carried * wide_ref[:, cols]
        square = total * total
        high = square.astype(BF16)
        low = (square - high.astype(F32)).astype(BF16)
        mean = dot(high, same) + dot(low, same)
        gain = gain_ref[layer : layer + 1, cols]
        normed_ref[:, cols] = (total * lax.rsqrt(mean + HEAD_EPS) * gain).astype(BF16)
    hidden = resid_ref[...].astype(F32) + dot(normed_ref[...], w_ref[layer])
    hidden_ref[...] = hidden
    a_ref[...] = rms_mod(hidden, *mod_rows(mods_ref, layer, step_ref[0], 2))


def memory_kernel(
    layer, tok_frame, base_ref, reach_ref, a_ref, wq_ref, wm_ref, q_ref, kv_ref, bias_ref
):
    rows = a_ref.shape[0]
    a = a_ref[...]
    q_ref[...] = (dot(a, wq_ref[layer]).astype(BF16).astype(F32) * HEAD_DIM**-0.5).astype(BF16)
    kv_ref[...] = dot(a, wm_ref[layer]).astype(BF16)
    key_frame = lax.broadcasted_iota(jnp.int32, (tok_frame, 2 * rows), 1) // tok_frame
    first = WINDOW - base_ref[0]
    for f in range(WINDOW):
        low = jnp.maximum(first, f + WINDOW - reach_ref[f])
        seen = (key_frame >= low) & (key_frame <= f + WINDOW)
        bias_ref[f * tok_frame : (f + 1) * tok_frame, :] = jnp.where(seen, 0.0, -1e30)


def attend_kernel(
    layer,
    last,
    step_ref,
    q_ref,
    kv_ref,
    bias_ref,
    prev_ref,
    wm_ref,
    merge_ref,
    hidden_ref,
    mods_ref,
    *rest,
):
    if last:
        resid_ref, keyed_ref, out_ref = rest
    else:
        resid_ref, u_ref, tail_ref, keyed_ref, out_ref = rest
    rows = q_ref.shape[0]
    keyed_ref[0:rows, :] = dot(prev_ref[...], wm_ref[layer]).astype(BF16)
    keyed_ref[rows:, :] = kv_ref[...]
    half = rows // 2
    span = rows + half
    left = lax.broadcasted_iota(jnp.int32, (half, LANES), 1) < HEAD_DIM
    one = jnp.ones((span, LANES), BF16)
    zero = jnp.zeros((half, LANES), BF16)
    together = 2
    for part in range(2):
        r = slice(part * half, (part + 1) * half)
        k_rows = slice(part * half, part * half + span)
        bias = bias_ref[r, k_rows]
        bias = jnp.concatenate([bias, bias], axis=0)
        for group in range(0, ATT_HEADS // 2, together):
            pairs = range(group, group + together)
            scores = []
            for pair in pairs:
                cols = slice(pair * LANES, (pair + 1) * LANES)
                query = q_ref[r, cols]
                sides = jnp.concatenate(
                    [jnp.where(left, query, zero), jnp.where(left, zero, query)], axis=0
                )
                scores.append(dot(sides, keyed_ref[k_rows, cols], ((1,), (1,))) + bias)
            tops = [jnp.max(s, axis=-1, keepdims=True) for s in scores]
            weights = [jnp.exp(s - t).astype(BF16) for s, t in zip(scores, tops)]
            for pair, weight in zip(pairs, weights):
                values = keyed_ref[k_rows, ATTN + pair * LANES : ATTN + (pair + 1) * LANES]
                both = dot(weight, jnp.concatenate([values, one], axis=1))
                number = jnp.where(left, both[:half, :LANES], both[half:, :LANES])
                total = jnp.where(left, both[:half, LANES:], both[half:, LANES:])
                out_ref[r, pair * LANES : (pair + 1) * LANES] = (number / total).astype(BF16)
    resid = hidden_ref[...] + dot(out_ref[...], merge_ref[layer])
    resid_ref[...] = resid
    if not last:
        u = rms_mod(resid, *mod_rows(mods_ref, layer + 1, step_ref[0], 0))
        u_ref[...] = u
        tail_ref[...] = u[rows - TAIL :]


SCALARS = pl.BlockSpec(memory_space=pltpu.SMEM)
WHOLE = pl.BlockSpec(memory_space=pltpu.VMEM)


def run(kernel, scalars, operands, outs, scratch=(), name=None, flops=0):
    moved = sum(o.size * o.dtype.itemsize for o in list(operands) + list(outs))
    return pl.pallas_call(
        kernel,
        in_specs=[SCALARS] * len(scalars) + [WHOLE] * len(operands),
        out_specs=[WHOLE] * len(outs),
        out_shape=list(outs),
        scratch_shapes=list(scratch),
        compiler_params=pltpu.CompilerParams(vmem_limit_bytes=20 * 1024 * 1024),
        cost_estimate=pl.CostEstimate(flops=flops, bytes_accessed=moved, transcendentals=0),
        name=name,
    )(*scalars, *operands)


def shape(dims, dtype):
    return jax.ShapeDtypeStruct(dims, dtype)


def from_behind(value, axis):
    count = lax.axis_size(axis)
    return lax.ppermute(value, axis, [(i, i + 1) for i in range(count - 1)])


def shards(
    latents,
    timestep,
    lookback,
    modulation,
    input_weight,
    step_weight,
    conv_weight,
    step_bias,
    decay_log,
    skip_gain,
    norm_gain,
    output_weight,
    query_weight,
    memory_weight,
    merge_weight,
):
    frames_dev, tok_frame, width = latents.shape
    rows = frames_dev * tok_frame
    spans = rows // SPAN
    parts = lax.axis_size("frames")
    part_rows = INNER // parts
    base = (lax.axis_index("frames") * frames_dev).astype(jnp.int32).reshape(1)
    step_weight = jnp.swapaxes(step_weight, 1, 2)
    step_bias = jnp.swapaxes(step_bias, 1, 2)
    resid = latents.reshape(rows, width)
    u, tail = run(
        first_kernel,
        (timestep,),
        (resid, modulation),
        [shape((rows, width), BF16), shape((TAIL, width), BF16)],
        name="first",
    )
    for layer in range(LAYERS):
        tail = from_behind(tail, "frames")
        act, cum, shifted, state, send = run(
            functools.partial(local_kernel, layer, parts),
            (timestep,),
            (u, tail, input_weight, step_weight, conv_weight, step_bias, decay_log),
            [
                shape((rows, INNER + 2 * STATE), BF16),
                shape((rows, HEADS), F32),
                shape((HEADS, rows), F32),
                shape((max(spans - 1, 1) * STATE, INNER), BF16),
                shape((parts, part_rows + PAD, LANES), BF16),
            ],
            [pltpu.VMEM((2, rows + TAIL, 256), F32)],
            name="local",
            flops=2 * rows * width * (INNER + 2 * STATE),
        )
        got = lax.all_to_all(send, "frames", 0, 0)
        y, wide = run(
            functools.partial(mix_kernel, layer),
            (),
            (u, input_weight, act, cum, shifted, state, skip_gain),
            [shape((rows, INNER), F32), shape((rows, INNER), F32)],
            name="mix",
            flops=2 * rows * width * INNER,
        )
        (back,) = run(
            scan_kernel,
            (),
            (got,),
            [shape((parts, part_rows, LANES), BF16)],
            name="scan",
        )
        enter = lax.all_to_all(back, "frames", 0, 0).reshape(INNER, LANES)
        hidden, a = run(
            functools.partial(finish_kernel, layer),
            (timestep,),
            (enter, act, y, wide, resid, output_weight, norm_gain, modulation),
            [shape((rows, width), F32), shape((rows, width), BF16)],
            [pltpu.VMEM((rows, INNER), BF16)],
            name="finish",
        )
        prev = from_behind(a, "frames")
        q, kv, bias = run(
            functools.partial(memory_kernel, layer, tok_frame),
            (base, lookback),
            (a, query_weight, memory_weight),
            [
                shape((rows, ATTN), BF16),
                shape((rows, 2 * ATTN), BF16),
                shape((rows, 2 * rows), F32),
            ],
            name="memory",
            flops=2 * rows * width * 3 * ATTN,
        )
        last = layer == LAYERS - 1
        outs = [shape((rows, width), F32)]
        if not last:
            outs += [shape((rows, width), BF16), shape((TAIL, width), BF16)]
        result = run(
            functools.partial(attend_kernel, layer, last),
            (timestep,),
            (q, kv, bias, prev, memory_weight, merge_weight, hidden, modulation),
            outs,
            [pltpu.VMEM((2 * rows, 2 * ATTN), BF16), pltpu.VMEM((rows, ATTN), BF16)],
            name="attend",
        )
        resid = result[0]
        if not last:
            u, tail = result[1:]
    return resid.reshape(latents.shape)


def solution(mesh):
    sharded = P(("groups", "frames"))
    return jax.shard_map(
        shards,
        mesh=mesh,
        in_specs=(P(("groups", "frames"), None, None), sharded, sharded) + (P(),) * 12,
        out_specs=P(("groups", "frames"), None, None),
        check_vma=False,
    )
```

```python
import functools

import jax
import jax.numpy as jnp
from jax import lax
from jax.experimental import pallas as pl
from jax.experimental.pallas import tpu as pltpu
from jax.sharding import PartitionSpec as P

HEADS = 16
HEAD_DIM = 64
STATE = 128
ATT_HEADS = 8
LAYERS = 2
CONV = 4
SPAN = 128
WINDOW = 8
EPS = 1e-06
HEAD_EPS = 1e-05
INNER = HEADS * HEAD_DIM
ATTN = ATT_HEADS * HEAD_DIM
PAD = 16
LANES = 128
TAIL = 16
F32 = jnp.float32
BF16 = jnp.bfloat16


def dot(a, b, dims=((1,), (0,)), precision=None):
    return lax.dot_general(a, b, (dims, ((), ())), precision=precision, preferred_element_type=F32)


def rms_mod(x, shift, scale):
    normed = x * lax.rsqrt(jnp.mean(x * x, axis=-1, keepdims=True) + EPS)
    return (normed * (1.0 + scale) + shift).astype(BF16)


def spread(per_head):
    high = per_head.astype(BF16)
    low = (per_head - high.astype(F32)).astype(BF16)
    row = lax.broadcasted_iota(jnp.int32, (2 * HEADS, INNER), 0) % HEADS
    head = lax.broadcasted_iota(jnp.int32, (2 * HEADS, INNER), 1) // HEAD_DIM
    sel = jnp.where(row == head, 1.0, 0.0).astype(BF16)
    return dot(jnp.concatenate([high, low], axis=1), sel)


def spread_row(per_head):
    return spread(jnp.broadcast_to(per_head, (16, HEADS)))[0:1, :]


def mod_rows(mods_ref, layer, step, which):
    mods = mods_ref[layer, step].astype(F32)
    return mods[which : which + 1, :], mods[which + 1 : which + 2, :]


def first_kernel(step_ref, x_ref, mods_ref, u_ref, tail_ref):
    rows = x_ref.shape[0]
    u = rms_mod(x_ref[...].astype(F32), *mod_rows(mods_ref, 0, step_ref[0], 0))
    u_ref[...] = u
    tail_ref[...] = u[rows - TAIL :]


def local_kernel(
    layer,
    parts,
    step_ref,
    u_ref,
    tail_ref,
    w_ref,
    sw_ref,
    conv_ref,
    bias_ref,
    decay_ref,
    act_ref,
    cum_ref,
    shifted_ref,
    state_ref,
    send_ref,
    ext_ref,
):
    rows = u_ref.shape[0]
    u = u_ref[...]
    tail = tail_ref[...]
    nsteps = bias_ref.shape[-1]
    chosen = lax.broadcasted_iota(jnp.int32, (8, nsteps), 1) == step_ref[0]
    bias = dot(
        jnp.where(chosen, 1.0, 0.0).astype(F32),
        bias_ref[layer],
        ((1,), (1,)),
        precision=lax.Precision.HIGHEST,
    )[0:1, :]
    raw = dot(u, sw_ref[layer], ((1,), (1,))) + bias
    step = jnp.maximum(raw, 0.0) + jnp.log1p(jnp.exp(-jnp.abs(raw)))
    log_decay = -jnp.exp(decay_ref[layer : layer + 1, :]) * step
    log_step = jnp.log(step)
    q_pos = lax.broadcasted_iota(jnp.int32, (SPAN, SPAN), 0)
    s_pos = lax.broadcasted_iota(jnp.int32, (SPAN, SPAN), 1)
    lower = jnp.where(q_pos >= s_pos, 1.0, 0.0).astype(F32)
    ends, edges = [], []
    for b in range(rows // SPAN):
        r = slice(b * SPAN, (b + 1) * SPAN)
        cum = dot(lower, log_decay[r], precision=lax.Precision.HIGHEST)
        end = cum[SPAN - 1 : SPAN, :]
        cum_ref[r, :] = cum
        shifted_ref[:, r] = (cum - log_step[r]).T
        ends.append(end)
        edges.append(spread(jnp.exp(end - cum) * step[r]))

    chunk = 256
    for c in [INNER] + list(range(0, INNER, chunk)):
        w = w_ref[layer, :, INNER + c : INNER + c + chunk]
        slot = c // chunk % 2
        ext_ref[slot, 0:TAIL, :] = dot(tail, w).astype(BF16).astype(F32)
        ext_ref[slot, TAIL:, :] = dot(u, w).astype(BF16).astype(F32)
        total = None
        for k in range(CONV):
            start = TAIL - (CONV - 1) + k
            term = conv_ref[layer, k : k + 1, c : c + chunk] * ext_ref[slot, start : start + rows, :]
            total = term if total is None else total + term
        act_ref[:, c : c + chunk] = (total * jax.nn.sigmoid(total)).astype(BF16)

    state = None
    for b in range(rows // SPAN):
        r = slice(b * SPAN, (b + 1) * SPAN)
        in_map = act_ref[r, INNER : INNER + STATE]
        scaled = (act_ref[r, 0:INNER].astype(F32) * edges[b]).astype(BF16)
        term = dot(in_map, scaled, ((0,), (0,)))
        if state is None:
            state = term
        else:
            state_ref[(b - 1) * STATE : b * STATE, :] = state.astype(BF16)
            state = spread_row(jnp.exp(ends[b])) * state + term

    part_rows = INNER // parts
    held = max(1, part_rows // HEAD_DIM)
    size = min(part_rows, LANES)
    for pair in range(HEADS // 2):
        turned = state[:, pair * LANES : (pair + 1) * LANES].T.astype(BF16)
        for k in range(LANES // size):
            first = pair * LANES + k * size
            part, at = first // part_rows, first % part_rows
            send_ref[part, at : at + size, :] = turned[k * size : (k + 1) * size, :]
    pad_row = lax.broadcasted_iota(jnp.int32, (PAD, LANES), 0)
    over = sum(ends[1:], ends[0])
    for part in range(parts):
        pad = jnp.zeros((PAD, LANES), F32)
        for i in range(held):
            h = part * part_rows // HEAD_DIM + i
            decay = jnp.broadcast_to(over[:, h : h + 1], (PAD, LANES))
            high = decay.astype(BF16).astype(F32)
            pad = jnp.where(pad_row == 2 * i, high, jnp.where(pad_row == 2 * i + 1, decay - high, pad))
        send_ref[part, part_rows:, :] = pad.astype(BF16)


def mix_kernel(
    layer, u_ref, w_ref, act_ref, cum_ref, shifted_ref, state_ref, skip_ref, y_ref, wide_ref
):
    rows = u_ref.shape[0]
    u = u_ref[...]
    q_pos = lax.broadcasted_iota(jnp.int32, (SPAN, SPAN), 0)
    s_pos = lax.broadcasted_iota(jnp.int32, (SPAN, SPAN), 1)
    lower = q_pos >= s_pos
    lane = lax.broadcasted_iota(jnp.int32, (SPAN, LANES), 1)
    left = lane < HEAD_DIM
    zero = jnp.zeros((SPAN, LANES), BF16)
    skip = spread_row(skip_ref[layer : layer + 1, :])
    before = jnp.zeros((1, HEADS), F32)
    for b in range(rows // SPAN):
        r = slice(b * SPAN, (b + 1) * SPAN)
        cum = cum_ref[r, :]
        in_map = act_ref[r, INNER : INNER + STATE]
        out_map = act_ref[r, INNER + STATE :]
        affinity = dot(out_map, in_map, ((1,), (1,)))
        wide_ref[r, :] = spread(jnp.exp(cum + before))
        before = before + cum[SPAN - 1 : SPAN, :]
        if b:
            y_ref[r, :] = dot(out_map, state_ref[(b - 1) * STATE : b * STATE, :]) * spread(jnp.exp(cum))
        for pair in range(HEADS // 2):
            cols = slice(pair * LANES, (pair + 1) * LANES)
            values = act_ref[r, cols]
            mixing = []
            for h in (2 * pair, 2 * pair + 1):
                gap = cum[:, h : h + 1] - shifted_ref[h : h + 1, r]
                mixing.append(jnp.where(lower, affinity * jnp.exp(gap), 0.0).astype(BF16))
            both = jnp.concatenate(mixing, axis=1)
            stacked = jnp.concatenate(
                [jnp.where(left, values, zero), jnp.where(left, zero, values)], axis=0
            )
            y = dot(both, stacked) + skip[:, cols] * values.astype(F32)
            if b:
                y = y + y_ref[r, cols]
            gate = dot(u[r], w_ref[layer, :, cols]).astype(BF16).astype(F32)
            gate = gate * jax.nn.sigmoid(gate)
            y_ref[r, cols] = y * gate
            wide_ref[r, cols] = wide_ref[r, cols] * gate


def scan_kernel(got_ref, back_ref):
    parts, padded, _ = got_ref.shape
    part_rows = padded - PAD
    held = max(1, part_rows // HEAD_DIM)
    size = part_rows // held
    carry = [jnp.zeros((size, LANES), F32) for _ in range(held)]
    for d in range(parts):
        pad = got_ref[d, part_rows:, :].astype(F32)
        for i in range(held):
            rows = slice(i * size, (i + 1) * size)
            back_ref[d, rows, :] = carry[i].astype(BF16)
            decay = jnp.exp(pad[2 * i : 2 * i + 1, :] + pad[2 * i + 1 : 2 * i + 2, :])
            carry[i] = decay * carry[i] + got_ref[d, rows, :].astype(F32)


def finish_kernel(
    layer,
    step_ref,
    enter_ref,
    act_ref,
    y_ref,
    wide_ref,
    resid_ref,
    w_ref,
    gain_ref,
    mods_ref,
    hidden_ref,
    a_ref,
    normed_ref,
):
    out_map = act_ref[:, INNER + STATE :]
    chunk = 256
    row = lax.broadcasted_iota(jnp.int32, (chunk, chunk), 0) // HEAD_DIM
    col = lax.broadcasted_iota(jnp.int32, (chunk, chunk), 1) // HEAD_DIM
    same = jnp.where(row == col, 1.0 / HEAD_DIM, 0.0).astype(BF16)
    for c in range(0, INNER, chunk):
        cols = slice(c, c + chunk)
        carried = dot(out_map, enter_ref[cols, :], ((1,), (1,)))
        total = y_ref[:, cols] + carried * wide_ref[:, cols]
        square = total * total
        high = square.astype(BF16)
        low = (square - high.astype(F32)).astype(BF16)
        mean = dot(high, same) + dot(low, same)
        gain = gain_ref[layer : layer + 1, cols]
        normed_ref[:, cols] = (total * lax.rsqrt(mean + HEAD_EPS) * gain).astype(BF16)
    hidden = resid_ref[...].astype(F32) + dot(normed_ref[...], w_ref[layer])
    hidden_ref[...] = hidden
    a_ref[...] = rms_mod(hidden, *mod_rows(mods_ref, layer, step_ref[0], 2))


def memory_kernel(
    layer, tok_frame, base_ref, reach_ref, a_ref, wq_ref, wm_ref, q_ref, kv_ref, bias_ref
):
    rows = a_ref.shape[0]
    a = a_ref[...]
    q_ref[...] = (dot(a, wq_ref[layer]).astype(BF16).astype(F32) * HEAD_DIM**-0.5).astype(BF16)
    kv_ref[...] = dot(a, wm_ref[layer]).astype(BF16)
    key_frame = lax.broadcasted_iota(jnp.int32, (tok_frame, 2 * rows), 1) // tok_frame
    first = WINDOW - base_ref[0]
    for f in range(WINDOW):
        low = jnp.maximum(first, f + WINDOW - reach_ref[f])
        seen = (key_frame >= low) & (key_frame <= f + WINDOW)
        bias_ref[f * tok_frame : (f + 1) * tok_frame, :] = jnp.where(seen, 0.0, -1e30)


def attend_kernel(
    layer,
    last,
    step_ref,
    q_ref,
    kv_ref,
    bias_ref,
    prev_ref,
    wm_ref,
    merge_ref,
    hidden_ref,
    mods_ref,
    *rest,
):
    if last:
        resid_ref, keyed_ref, out_ref = rest
    else:
        resid_ref, u_ref, tail_ref, keyed_ref, out_ref = rest
    rows = q_ref.shape[0]
    keyed_ref[0:rows, :] = dot(prev_ref[...], wm_ref[layer]).astype(BF16)
    keyed_ref[rows:, :] = kv_ref[...]
    half = rows // 2
    span = rows + half
    left = lax.broadcasted_iota(jnp.int32, (half, LANES), 1) < HEAD_DIM
    one = jnp.ones((span, LANES), BF16)
    zero = jnp.zeros((half, LANES), BF16)
    together = 2
    for part in range(2):
        r = slice(part * half, (part + 1) * half)
        k_rows = slice(part * half, part * half + span)
        bias = bias_ref[r, k_rows]
        bias = jnp.concatenate([bias, bias], axis=0)
        for group in range(0, ATT_HEADS // 2, together):
            pairs = range(group, group + together)
            scores = []
            for pair in pairs:
                cols = slice(pair * LANES, (pair + 1) * LANES)
                query = q_ref[r, cols]
                sides = jnp.concatenate(
                    [jnp.where(left, query, zero), jnp.where(left, zero, query)], axis=0
                )
                scores.append(dot(sides, keyed_ref[k_rows, cols], ((1,), (1,))) + bias)
            tops = [jnp.max(s, axis=-1, keepdims=True) for s in scores]
            weights = [jnp.exp(s - t).astype(BF16) for s, t in zip(scores, tops)]
            for pair, weight in zip(pairs, weights):
                values = keyed_ref[k_rows, ATTN + pair * LANES : ATTN + (pair + 1) * LANES]
                both = dot(weight, jnp.concatenate([values, one], axis=1))
                number = jnp.where(left, both[:half, :LANES], both[half:, :LANES])
                total = jnp.where(left, both[:half, LANES:], both[half:, LANES:])
                out_ref[r, pair * LANES : (pair + 1) * LANES] = (number / total).astype(BF16)
    resid = hidden_ref[...] + dot(out_ref[...], merge_ref[layer])
    resid_ref[...] = resid
    if not last:
        u = rms_mod(resid, *mod_rows(mods_ref, layer + 1, step_ref[0], 0))
        u_ref[...] = u
        tail_ref[...] = u[rows - TAIL :]


SCALARS = pl.BlockSpec(memory_space=pltpu.SMEM)
WHOLE = pl.BlockSpec(memory_space=pltpu.VMEM)


def run(kernel, scalars, operands, outs, scratch=(), name=None, flops=0):
    moved = sum(o.size * o.dtype.itemsize for o in list(operands) + list(outs))
    return pl.pallas_call(
        kernel,
        in_specs=[SCALARS] * len(scalars) + [WHOLE] * len(operands),
        out_specs=[WHOLE] * len(outs),
        out_shape=list(outs),
        scratch_shapes=list(scratch),
        compiler_params=pltpu.CompilerParams(vmem_limit_bytes=20 * 1024 * 1024),
        cost_estimate=pl.CostEstimate(flops=flops, bytes_accessed=moved, transcendentals=0),
        name=name,
    )(*scalars, *operands)


def shape(dims, dtype):
    return jax.ShapeDtypeStruct(dims, dtype)


def from_behind(value, axis):
    count = lax.axis_size(axis)
    return lax.ppermute(value, axis, [(i, i + 1) for i in range(count - 1)])


def shards(
    latents,
    timestep,
    lookback,
    modulation,
    input_weight,
    step_weight,
    conv_weight,
    step_bias,
    decay_log,
    skip_gain,
    norm_gain,
    output_weight,
    query_weight,
    memory_weight,
    merge_weight,
):
    frames_dev, tok_frame, width = latents.shape
    rows = frames_dev * tok_frame
    spans = rows // SPAN
    parts = lax.axis_size("frames")
    part_rows = INNER // parts
    base = (lax.axis_index("frames") * frames_dev).astype(jnp.int32).reshape(1)
    step_weight = jnp.swapaxes(step_weight, 1, 2)
    step_bias = jnp.swapaxes(step_bias, 1, 2)
    resid = latents.reshape(rows, width)
    u, tail = run(
        first_kernel,
        (timestep,),
        (resid, modulation),
        [shape((rows, width), BF16), shape((TAIL, width), BF16)],
        name="first",
    )
    for layer in range(LAYERS):
        tail = from_behind(tail, "frames")
        act, cum, shifted, state, send = run(
            functools.partial(local_kernel, layer, parts),
            (timestep,),
            (u, tail, input_weight, step_weight, conv_weight, step_bias, decay_log),
            [
                shape((rows, INNER + 2 * STATE), BF16),
                shape((rows, HEADS), F32),
                shape((HEADS, rows), F32),
                shape((max(spans - 1, 1) * STATE, INNER), BF16),
                shape((parts, part_rows + PAD, LANES), BF16),
            ],
            [pltpu.VMEM((2, rows + TAIL, 256), F32)],
            name="local",
            flops=2 * rows * width * (INNER + 2 * STATE),
        )
        y, wide = run(
            functools.partial(mix_kernel, layer),
            (),
            (u, input_weight, act, cum, shifted, state, skip_gain),
            [shape((rows, INNER), F32), shape((rows, INNER), F32)],
            name="mix",
            flops=2 * rows * width * INNER,
        )
        send, y, wide, act = lax.optimization_barrier((send, y, wide, act))
        got = lax.all_to_all(send, "frames", 0, 0)
        (back,) = run(
            scan_kernel,
            (),
            (got,),
            [shape((parts, part_rows, LANES), BF16)],
            name="scan",
        )
        enter = lax.all_to_all(back, "frames", 0, 0).reshape(INNER, LANES)
        hidden, a = run(
            functools.partial(finish_kernel, layer),
            (timestep,),
            (enter, act, y, wide, resid, output_weight, norm_gain, modulation),
            [shape((rows, width), F32), shape((rows, width), BF16)],
            [pltpu.VMEM((rows, INNER), BF16)],
            name="finish",
        )
        prev = from_behind(a, "frames")
        q, kv, bias = run(
            functools.partial(memory_kernel, layer, tok_frame),
            (base, lookback),
            (a, query_weight, memory_weight),
            [
                shape((rows, ATTN), BF16),
                shape((rows, 2 * ATTN), BF16),
                shape((rows, 2 * rows), F32),
            ],
            name="memory",
            flops=2 * rows * width * 3 * ATTN,
        )
        last = layer == LAYERS - 1
        outs = [shape((rows, width), F32)]
        if not last:
            outs += [shape((rows, width), BF16), shape((TAIL, width), BF16)]
        result = run(
            functools.partial(attend_kernel, layer, last),
            (timestep,),
            (q, kv, bias, prev, memory_weight, merge_weight, hidden, modulation),
            outs,
            [pltpu.VMEM((2 * rows, 2 * ATTN), BF16), pltpu.VMEM((rows, ATTN), BF16)],
            name="attend",
        )
        resid = result[0]
        if not last:
            u, tail = result[1:]
    return resid.reshape(latents.shape)


def solution(mesh):
    sharded = P(("groups", "frames"))
    return jax.shard_map(
        shards,
        mesh=mesh,
        in_specs=(P(("groups", "frames"), None, None), sharded, sharded) + (P(),) * 12,
        out_specs=P(("groups", "frames"), None, None),
        check_vma=False,
    )
```

```python
import functools

import jax
import jax.numpy as jnp
from jax import lax
from jax.experimental import pallas as pl
from jax.experimental.pallas import tpu as pltpu
from jax.sharding import PartitionSpec as P

HEADS = 16
HEAD_DIM = 64
STATE = 128
ATT_HEADS = 8
LAYERS = 2
CONV = 4
SPAN = 128
WINDOW = 8
EPS = 1e-06
HEAD_EPS = 1e-05
INNER = HEADS * HEAD_DIM
ATTN = ATT_HEADS * HEAD_DIM
PAD = 16
LANES = 128
TAIL = 16
F32 = jnp.float32
OPENING = 4 * 10**9
BF16 = jnp.bfloat16


def dot(a, b, dims=((1,), (0,)), precision=None):
    return lax.dot_general(a, b, (dims, ((), ())), precision=precision, preferred_element_type=F32)


def rms_mod(x, shift, scale):
    normed = x * lax.rsqrt(jnp.mean(x * x, axis=-1, keepdims=True) + EPS)
    return (normed * (1.0 + scale) + shift).astype(BF16)


def spread(per_head, sel):
    high = per_head.astype(BF16)
    low = (per_head - high.astype(F32)).astype(BF16)
    return dot(jnp.concatenate([high, low], axis=1), sel)


def spread_row(per_head, sel):
    return spread(jnp.broadcast_to(per_head, (16, HEADS)), sel)[0:1, :]


def select_kernel(sel_ref):
    row = lax.broadcasted_iota(jnp.int32, sel_ref.shape, 0) % HEADS
    head = lax.broadcasted_iota(jnp.int32, sel_ref.shape, 1) // HEAD_DIM
    sel_ref[...] = jnp.where(row == head, 1.0, 0.0).astype(BF16)


def first_kernel(
    step_ref,
    reach_ref,
    sel_ref,
    x_ref,
    all_mods_ref,
    all_bias_ref,
    u_ref,
    tail_ref,
    mods_ref,
    bias_ref,
    seen_ref,
):
    rows, width = u_ref.shape
    tok_frame = rows // WINDOW
    step = step_ref[0]
    for layer in range(LAYERS):
        mods_ref[layer] = all_mods_ref[layer, step].astype(F32)
    u = rms_mod(x_ref[...].astype(F32), mods_ref[0, 0:1, :], mods_ref[0, 1:2, :])
    u_ref[...] = u
    tail_ref[...] = u[rows - TAIL :]
    chosen = lax.broadcasted_iota(jnp.int32, (8, all_bias_ref.shape[-1]), 1) == step
    chosen = jnp.where(chosen, 1.0, 0.0).astype(F32)
    for layer in range(LAYERS):
        bias_ref[layer] = dot(
            chosen, all_bias_ref[layer], ((1,), (1,)), precision=lax.Precision.HIGHEST
        )
    key_frame = lax.broadcasted_iota(jnp.int32, (tok_frame, 2 * rows), 1) // tok_frame
    first = WINDOW - lax.axis_index("frames") * WINDOW
    for f in range(WINDOW):
        low = jnp.maximum(first, f + WINDOW - reach_ref[f])
        seen = (key_frame >= low) & (key_frame <= f + WINDOW)
        seen_ref[f * tok_frame : (f + 1) * tok_frame, :] = jnp.where(seen, 0.0, -1e30)


def local_kernel(
    layer,
    parts,
    u_ref,
    tail_ref,
    w_ref,
    sw_ref,
    conv_ref,
    bias_ref,
    decay_ref,
    sel_ref,
    act_ref,
    cum_ref,
    shifted_ref,
    state_ref,
    send_ref,
    ext_ref,
):
    rows = u_ref.shape[0]
    u = u_ref[...]
    tail = tail_ref[...]
    sel = sel_ref[...]
    raw = dot(u, sw_ref[layer], ((1,), (1,))) + bias_ref[layer, 0:1, :]
    step = jnp.maximum(raw, 0.0) + jnp.log1p(jnp.exp(-jnp.abs(raw)))
    log_decay = -jnp.exp(decay_ref[layer : layer + 1, :]) * step
    log_step = jnp.log(step)
    q_pos = lax.broadcasted_iota(jnp.int32, (SPAN, SPAN), 0)
    s_pos = lax.broadcasted_iota(jnp.int32, (SPAN, SPAN), 1)
    lower = jnp.where(q_pos >= s_pos, 1.0, 0.0).astype(F32)
    ends, edges = [], []
    for b in range(rows // SPAN):
        r = slice(b * SPAN, (b + 1) * SPAN)
        cum = dot(lower, log_decay[r], precision=lax.Precision.HIGHEST)
        end = cum[SPAN - 1 : SPAN, :]
        cum_ref[r, :] = cum
        shifted_ref[:, r] = (cum - log_step[r]).T
        ends.append(end)
        edges.append(spread(jnp.exp(end - cum) * step[r], sel))

    chunk = 256
    for c in [INNER] + list(range(0, INNER, chunk)):
        w = w_ref[layer, :, INNER + c : INNER + c + chunk]
        slot = c // chunk % 2
        ext_ref[slot, 0:TAIL, :] = dot(tail, w).astype(BF16).astype(F32)
        ext_ref[slot, TAIL:, :] = dot(u, w).astype(BF16).astype(F32)
        total = None
        for k in range(CONV):
            start = TAIL - (CONV - 1) + k
            term = conv_ref[layer, k : k + 1, c : c + chunk] * ext_ref[slot, start : start + rows, :]
            total = term if total is None else total + term
        act_ref[:, c : c + chunk] = (total * jax.nn.sigmoid(total)).astype(BF16)

    state = None
    for b in range(rows // SPAN):
        r = slice(b * SPAN, (b + 1) * SPAN)
        in_map = act_ref[r, INNER : INNER + STATE]
        scaled = (act_ref[r, 0:INNER].astype(F32) * edges[b]).astype(BF16)
        term = dot(in_map, scaled, ((0,), (0,)))
        if state is None:
            state = term
        else:
            state_ref[(b - 1) * STATE : b * STATE, :] = state.astype(BF16)
            state = spread_row(jnp.exp(ends[b]), sel) * state + term

    part_rows = INNER // parts
    held = max(1, part_rows // HEAD_DIM)
    size = min(part_rows, LANES)
    for pair in range(HEADS // 2):
        turned = state[:, pair * LANES : (pair + 1) * LANES].T.astype(BF16)
        for k in range(LANES // size):
            first = pair * LANES + k * size
            part, at = first // part_rows, first % part_rows
            send_ref[part, at : at + size, :] = turned[k * size : (k + 1) * size, :]
    pad_row = lax.broadcasted_iota(jnp.int32, (PAD, LANES), 0)
    over = sum(ends[1:], ends[0])
    for part in range(parts):
        pad = jnp.zeros((PAD, LANES), F32)
        for i in range(held):
            h = part * part_rows // HEAD_DIM + i
            decay = jnp.broadcast_to(over[:, h : h + 1], (PAD, LANES))
            high = decay.astype(BF16).astype(F32)
            pad = jnp.where(pad_row == 2 * i, high, jnp.where(pad_row == 2 * i + 1, decay - high, pad))
        send_ref[part, part_rows:, :] = pad.astype(BF16)


def mix_kernel(
    layer, u_ref, w_ref, act_ref, cum_ref, shifted_ref, state_ref, skip_ref, sel_ref, y_ref, wide_ref
):
    rows = u_ref.shape[0]
    u = u_ref[...]
    q_pos = lax.broadcasted_iota(jnp.int32, (SPAN, SPAN), 0)
    s_pos = lax.broadcasted_iota(jnp.int32, (SPAN, SPAN), 1)
    lower = q_pos >= s_pos
    lane = lax.broadcasted_iota(jnp.int32, (SPAN, LANES), 1)
    left = lane < HEAD_DIM
    zero = jnp.zeros((SPAN, LANES), BF16)
    sel = sel_ref[...]
    skip = spread_row(skip_ref[layer : layer + 1, :], sel)
    before = jnp.zeros((1, HEADS), F32)
    for b in range(rows // SPAN):
        r = slice(b * SPAN, (b + 1) * SPAN)
        cum = cum_ref[r, :]
        in_map = act_ref[r, INNER : INNER + STATE]
        out_map = act_ref[r, INNER + STATE :]
        affinity = dot(out_map, in_map, ((1,), (1,)))
        wide_ref[r, :] = spread(jnp.exp(cum + before), sel)
        before = before + cum[SPAN - 1 : SPAN, :]
        if b:
            y_ref[r, :] = dot(out_map, state_ref[(b - 1) * STATE : b * STATE, :]) * spread(jnp.exp(cum), sel)
        for pair in range(HEADS // 2):
            cols = slice(pair * LANES, (pair + 1) * LANES)
            values = act_ref[r, cols]
            mixing = []
            for h in (2 * pair, 2 * pair + 1):
                gap = cum[:, h : h + 1] - shifted_ref[h : h + 1, r]
                mixing.append(jnp.where(lower, affinity * jnp.exp(gap), 0.0).astype(BF16))
            both = jnp.concatenate(mixing, axis=1)
            stacked = jnp.concatenate(
                [jnp.where(left, values, zero), jnp.where(left, zero, values)], axis=0
            )
            y = dot(both, stacked) + skip[:, cols] * values.astype(F32)
            if b:
                y = y + y_ref[r, cols]
            gate = dot(u[r], w_ref[layer, :, cols]).astype(BF16).astype(F32)
            gate = gate * jax.nn.sigmoid(gate)
            y_ref[r, cols] = y * gate
            wide_ref[r, cols] = wide_ref[r, cols] * gate


def scan_kernel(got_ref, back_ref):
    parts, padded, _ = got_ref.shape
    part_rows = padded - PAD
    held = max(1, part_rows // HEAD_DIM)
    size = part_rows // held
    carry = [jnp.zeros((size, LANES), F32) for _ in range(held)]
    for d in range(parts):
        pad = got_ref[d, part_rows:, :].astype(F32)
        for i in range(held):
            rows = slice(i * size, (i + 1) * size)
            back_ref[d, rows, :] = carry[i].astype(BF16)
            decay = jnp.exp(pad[2 * i : 2 * i + 1, :] + pad[2 * i + 1 : 2 * i + 2, :])
            carry[i] = decay * carry[i] + got_ref[d, rows, :].astype(F32)


def finish_kernel(
    layer,
    enter_ref,
    act_ref,
    y_ref,
    wide_ref,
    resid_ref,
    w_ref,
    gain_ref,
    mods_ref,
    *rest,
):
    hidden_ref, a_ref, normed_ref = rest[-3:]
    out_map = act_ref[:, INNER + STATE :]
    chunk = 256
    row = lax.broadcasted_iota(jnp.int32, (chunk, chunk), 0) // HEAD_DIM
    col = lax.broadcasted_iota(jnp.int32, (chunk, chunk), 1) // HEAD_DIM
    same = jnp.where(row == col, 1.0 / HEAD_DIM, 0.0).astype(BF16)
    for c in range(0, INNER, chunk):
        cols = slice(c, c + chunk)
        carried = dot(out_map, enter_ref[cols, :], ((1,), (1,)))
        total = y_ref[:, cols] + carried * wide_ref[:, cols]
        square = total * total
        high = square.astype(BF16)
        low = (square - high.astype(F32)).astype(BF16)
        mean = dot(high, same) + dot(low, same)
        gain = gain_ref[layer : layer + 1, cols]
        normed_ref[:, cols] = (total * lax.rsqrt(mean + HEAD_EPS) * gain).astype(BF16)
    hidden = resid_ref[...].astype(F32) + dot(normed_ref[...], w_ref[layer])
    hidden_ref[...] = hidden
    a_ref[...] = rms_mod(hidden, mods_ref[layer, 2:3, :], mods_ref[layer, 3:4, :])


def partial_attention(q_ref, seen, kv, half, r, k_rows, done):
    left = lax.broadcasted_iota(jnp.int32, (half, LANES), 1) < HEAD_DIM
    one = jnp.ones((k_rows.stop - k_rows.start, LANES), BF16)
    zero = jnp.zeros((half, LANES), BF16)
    seen = jnp.concatenate([seen, seen], axis=0)
    together = 2
    for group in range(0, ATT_HEADS // 2, together):
        columns = [slice(p * LANES, (p + 1) * LANES) for p in range(group, group + together)]
        scores = []
        for cols in columns:
            query = q_ref[r, cols]
            sides = jnp.concatenate(
                [jnp.where(left, query, zero), jnp.where(left, zero, query)], axis=0
            )
            scores.append(dot(sides, kv[k_rows, cols], ((1,), (1,))) + seen)
        tops = [jnp.max(s, axis=-1, keepdims=True) for s in scores]
        weights = [jnp.exp(s - t).astype(BF16) for s, t in zip(scores, tops)]
        for cols, weight, top in zip(columns, weights, tops):
            values = kv[k_rows, ATTN + cols.start : ATTN + cols.stop]
            both = dot(weight, jnp.concatenate([values, one], axis=1))
            number = jnp.where(left, both[:half, :LANES], both[half:, :LANES])
            total = jnp.where(left, both[:half, LANES:], both[half:, LANES:])
            done(cols, number, total, jnp.where(left, top[:half], top[half:]))


def memory_kernel(
    layer, a_ref, wq_ref, wm_ref, seen_ref, q_ref, number_ref, total_ref, top_ref, kv_ref
):
    rows = a_ref.shape[0]
    half = rows // 2
    a = a_ref[...]
    q_ref[...] = (dot(a, wq_ref[layer]).astype(BF16).astype(F32) * HEAD_DIM**-0.5).astype(BF16)
    kv_ref[...] = dot(a, wm_ref[layer]).astype(BF16)
    for part in range(2):
        r = slice(part * half, (part + 1) * half)
        k_rows = slice(0, (part + 1) * half)

        def done(cols, number, total, top):
            number_ref[r, cols] = number
            total_ref[r, cols] = total
            top_ref[r, cols] = top

        seen = seen_ref[r, rows : rows + k_rows.stop]
        partial_attention(q_ref, seen, kv_ref, half, r, k_rows, done)


def attend_kernel(
    layer,
    last,
    q_ref,
    number_ref,
    total_ref,
    top_ref,
    seen_ref,
    prev_ref,
    wm_ref,
    merge_ref,
    hidden_ref,
    mods_ref,
    *rest,
):
    if last:
        resid_ref, kv_ref, out_ref = rest
    else:
        resid_ref, u_ref, tail_ref, kv_ref, out_ref = rest
    rows = q_ref.shape[0]
    half = rows // 2
    kv_ref[...] = dot(prev_ref[...], wm_ref[layer]).astype(BF16)
    for part in range(2):
        r = slice(part * half, (part + 1) * half)
        k_rows = slice(part * half, rows)

        def done(cols, number, total, top):
            top_own = top_ref[r, cols]
            highest = jnp.maximum(top, top_own)
            mine, own = jnp.exp(top - highest), jnp.exp(top_own - highest)
            number = number * mine + number_ref[r, cols] * own
            total = total * mine + total_ref[r, cols] * own
            out_ref[r, cols] = (number / total).astype(BF16)

        partial_attention(q_ref, seen_ref[r, k_rows], kv_ref, half, r, k_rows, done)
    resid = hidden_ref[...] + dot(out_ref[...], merge_ref[layer])
    resid_ref[...] = resid
    if not last:
        u = rms_mod(resid, mods_ref[layer + 1, 0:1, :], mods_ref[layer + 1, 1:2, :])
        u_ref[...] = u
        tail_ref[...] = u[rows - TAIL :]


WHOLE = pl.BlockSpec(memory_space=pltpu.VMEM)
SCALARS = pl.BlockSpec(memory_space=pltpu.SMEM)


def run(kernel, operands, outs, scratch=(), name=None, flops=0, scalars=()):
    moved = sum(o.size * o.dtype.itemsize for o in list(operands) + list(outs))
    return pl.pallas_call(
        kernel,
        in_specs=[SCALARS] * len(scalars) + [WHOLE] * len(operands),
        out_specs=[WHOLE] * len(outs),
        out_shape=list(outs),
        scratch_shapes=list(scratch),
        compiler_params=pltpu.CompilerParams(vmem_limit_bytes=20 * 1024 * 1024),
        cost_estimate=pl.CostEstimate(flops=flops, bytes_accessed=moved, transcendentals=0),
        name=name,
    )(*scalars, *operands)


def shape(dims, dtype):
    return jax.ShapeDtypeStruct(dims, dtype)


def from_behind(value, axis):
    count = lax.axis_size(axis)
    return lax.ppermute(value, axis, [(i, i + 1) for i in range(count - 1)])


def shards(
    latents,
    timestep,
    lookback,
    modulation,
    input_weight,
    step_weight,
    conv_weight,
    step_bias,
    decay_log,
    skip_gain,
    norm_gain,
    output_weight,
    query_weight,
    memory_weight,
    merge_weight,
):
    frames_dev, tok_frame, width = latents.shape
    rows = frames_dev * tok_frame
    spans = rows // SPAN
    parts = lax.axis_size("frames")
    part_rows = INNER // parts
    step_weight = jnp.swapaxes(step_weight, 1, 2)
    step_bias = jnp.swapaxes(step_bias, 1, 2)
    resid = latents.reshape(rows, width)
    (sel,) = run(
        select_kernel, (), [shape((2 * HEADS, INNER), BF16)], name="select", flops=OPENING
    )
    u, tail, mods, bias, seen = run(
        first_kernel,
        (sel, resid, modulation, step_bias),
        [
            shape((rows, width), BF16),
            shape((TAIL, width), BF16),
            shape((LAYERS,) + modulation.shape[2:], F32),
            shape((LAYERS, 8, HEADS), F32),
            shape((rows, 2 * rows), F32),
        ],
        name="first",
        flops=OPENING,
        scalars=(timestep, lookback),
    )
    for layer in range(LAYERS):
        tail = from_behind(tail, "frames")
        act, cum, shifted, state, send = run(
            functools.partial(local_kernel, layer, parts),
            (u, tail, input_weight, step_weight, conv_weight, bias, decay_log, sel),
            [
                shape((rows, INNER + 2 * STATE), BF16),
                shape((rows, HEADS), F32),
                shape((HEADS, rows), F32),
                shape((max(spans - 1, 1) * STATE, INNER), BF16),
                shape((parts, part_rows + PAD, LANES), BF16),
            ],
            [pltpu.VMEM((2, rows + TAIL, 256), F32)],
            name="local",
            flops=2 * rows * width * (INNER + 2 * STATE),
        )
        y, wide = run(
            functools.partial(mix_kernel, layer),
            (u, input_weight, act, cum, shifted, state, skip_gain, sel),
            [shape((rows, INNER), F32), shape((rows, INNER), F32)],
            name="mix",
            flops=2 * rows * width * INNER,
        )
        send, y, wide, act = lax.optimization_barrier((send, y, wide, act))
        got = lax.all_to_all(send, "frames", 0, 0)
        (back,) = run(
            scan_kernel,
            (got,),
            [shape((parts, part_rows, LANES), BF16)],
            name="scan",
        )
        enter = lax.all_to_all(back, "frames", 0, 0).reshape(INNER, LANES)
        hidden, a = run(
            functools.partial(finish_kernel, layer),
            (enter, act, y, wide, resid, output_weight, norm_gain, mods)
            + (() if layer else (query_weight, memory_weight, merge_weight)),
            [shape((rows, width), F32), shape((rows, width), BF16)],
            [pltpu.VMEM((rows, INNER), BF16)],
            name="finish",
        )
        prev = from_behind(a, "frames")
        q, number, total, top = run(
            functools.partial(memory_kernel, layer),
            (a, query_weight, memory_weight, seen),
            [shape((rows, ATTN), BF16)] + [shape((rows, ATTN), F32)] * 3,
            [pltpu.VMEM((rows, 2 * ATTN), BF16)],
            name="memory",
            flops=2 * rows * width * 3 * ATTN,
        )
        last = layer == LAYERS - 1
        outs = [shape((rows, width), F32)]
        if not last:
            outs += [shape((rows, width), BF16), shape((TAIL, width), BF16)]
        result = run(
            functools.partial(attend_kernel, layer, last),
            (q, number, total, top, seen, prev, memory_weight, merge_weight, hidden, mods),
            outs,
            [pltpu.VMEM((rows, 2 * ATTN), BF16), pltpu.VMEM((rows, ATTN), BF16)],
            name="attend",
        )
        resid = result[0]
        if not last:
            u, tail = result[1:]
    return resid.reshape(latents.shape)


def solution(mesh):
    sharded = P(("groups", "frames"))
    return jax.shard_map(
        shards,
        mesh=mesh,
        in_specs=(P(("groups", "frames"), None, None), sharded, sharded) + (P(),) * 12,
        out_specs=P(("groups", "frames"), None, None),
        check_vma=False,
    )
```

```python
import functools

import jax
import jax.numpy as jnp
from jax import lax
from jax.experimental import pallas as pl
from jax.experimental.pallas import tpu as pltpu
from jax.sharding import PartitionSpec as P

HEADS = 16
HEAD_DIM = 64
STATE = 128
ATT_HEADS = 8
LAYERS = 2
CONV = 4
SPAN = 128
WINDOW = 8
EPS = 1e-06
HEAD_EPS = 1e-05
INNER = HEADS * HEAD_DIM
ATTN = ATT_HEADS * HEAD_DIM
PAD = 16
LANES = 128
TAIL = 16
F32 = jnp.float32
OPENING = 4 * 10**9
BF16 = jnp.bfloat16


def dot(a, b, dims=((1,), (0,)), precision=None):
    return lax.dot_general(a, b, (dims, ((), ())), precision=precision, preferred_element_type=F32)


def rms_mod(x, shift, scale):
    normed = x * lax.rsqrt(jnp.mean(x * x, axis=-1, keepdims=True) + EPS)
    return (normed * (1.0 + scale) + shift).astype(BF16)


def spread(per_head, sel):
    high = per_head.astype(BF16)
    low = (per_head - high.astype(F32)).astype(BF16)
    return dot(jnp.concatenate([high, low], axis=1), sel)


def spread_row(per_head, sel):
    return spread(jnp.broadcast_to(per_head, (16, HEADS)), sel)[0:1, :]


def select_kernel(sel_ref):
    row = lax.broadcasted_iota(jnp.int32, sel_ref.shape, 0) % HEADS
    head = lax.broadcasted_iota(jnp.int32, sel_ref.shape, 1) // HEAD_DIM
    sel_ref[...] = jnp.where(row == head, 1.0, 0.0).astype(BF16)


def first_kernel(
    step_ref,
    reach_ref,
    sel_ref,
    x_ref,
    all_mods_ref,
    all_bias_ref,
    u_ref,
    mods_ref,
    bias_ref,
    seen_ref,
):
    rows, width = u_ref.shape
    tok_frame = rows // WINDOW
    step = step_ref[0]
    for layer in range(LAYERS):
        mods_ref[layer] = all_mods_ref[layer, step].astype(F32)
    u_ref[...] = rms_mod(x_ref[...].astype(F32), mods_ref[0, 0:1, :], mods_ref[0, 1:2, :])
    chosen = lax.broadcasted_iota(jnp.int32, (8, all_bias_ref.shape[-1]), 1) == step
    chosen = jnp.where(chosen, 1.0, 0.0).astype(F32)
    for layer in range(LAYERS):
        bias_ref[layer] = dot(
            chosen, all_bias_ref[layer], ((1,), (1,)), precision=lax.Precision.HIGHEST
        )
    key_frame = lax.broadcasted_iota(jnp.int32, (tok_frame, 2 * rows), 1) // tok_frame
    first = WINDOW - lax.axis_index("frames") * WINDOW
    for f in range(WINDOW):
        low = jnp.maximum(first, f + WINDOW - reach_ref[f])
        seen = (key_frame >= low) & (key_frame <= f + WINDOW)
        seen_ref[f * tok_frame : (f + 1) * tok_frame, :] = jnp.where(seen, 0.0, -1e30)


def local_kernel(
    layer,
    parts,
    u_ref,
    w_ref,
    sw_ref,
    conv_ref,
    bias_ref,
    decay_ref,
    sel_ref,
    act_ref,
    own_ref,
    cum_ref,
    shifted_ref,
    edge_ref,
    state_ref,
    send_ref,
    ext_ref,
    tail_ref,
    pad_ref,
):
    rows = u_ref.shape[0]
    u = u_ref[...]
    sel = sel_ref[...]
    raw = dot(u, sw_ref[layer], ((1,), (1,))) + bias_ref[layer, 0:1, :]
    step = jnp.maximum(raw, 0.0) + jnp.log1p(jnp.exp(-jnp.abs(raw)))
    log_decay = -jnp.exp(decay_ref[layer : layer + 1, :]) * step
    log_step = jnp.log(step)
    q_pos = lax.broadcasted_iota(jnp.int32, (SPAN, SPAN), 0)
    s_pos = lax.broadcasted_iota(jnp.int32, (SPAN, SPAN), 1)
    lower = jnp.where(q_pos >= s_pos, 1.0, 0.0).astype(F32)
    whole_tokens = lax.broadcasted_iota(jnp.int32, (SPAN, HEADS), 0) >= CONV - 1
    ends, edges = [], []
    for b in range(rows // SPAN):
        r = slice(b * SPAN, (b + 1) * SPAN)
        cum = dot(lower, log_decay[r], precision=lax.Precision.HIGHEST)
        end = cum[SPAN - 1 : SPAN, :]
        cum_ref[r, :] = cum
        shifted_ref[:, r] = (cum - log_step[r]).T
        edge = jnp.exp(end - cum) * step[r]
        if b == 0:
            edge_ref[...] = edge[0:TAIL, :]
            edge = jnp.where(whole_tokens, edge, 0.0)
        ends.append(end)
        edges.append(spread(edge, sel))

    chunk = 256
    for slot in range(2):
        ext_ref[slot, 0:TAIL, :] = jnp.zeros((TAIL, chunk), F32)
        ext_ref[slot, TAIL + rows :, :] = jnp.zeros((TAIL, chunk), F32)
    for c in [INNER] + list(range(0, INNER, chunk)):
        w = w_ref[layer, :, INNER + c : INNER + c + chunk]
        slot = c // chunk % 2
        ext_ref[slot, TAIL : TAIL + rows, :] = dot(u, w).astype(BF16).astype(F32)
        total, after = None, None
        for k in range(CONV):
            start = TAIL - (CONV - 1) + k
            taps = conv_ref[layer, k : k + 1, c : c + chunk]
            term = taps * ext_ref[slot, start : start + rows, :]
            next_term = taps * ext_ref[slot, start + rows : start + rows + 8, :]
            total = term if total is None else total + term
            after = next_term if after is None else after + next_term
        act_ref[:, c : c + chunk] = (total * jax.nn.sigmoid(total)).astype(BF16)
        own_ref[:, c : c + chunk] = total[0:8, :]
        tail_ref[:, c : c + chunk] = after

    state = None
    for b in range(rows // SPAN):
        r = slice(b * SPAN, (b + 1) * SPAN)
        in_map = act_ref[r, INNER : INNER + STATE]
        scaled = (act_ref[r, 0:INNER].astype(F32) * edges[b]).astype(BF16)
        term = dot(in_map, scaled, ((0,), (0,)))
        if state is None:
            state = term
        else:
            state_ref[(b - 1) * STATE : b * STATE, :] = state
            state = spread_row(jnp.exp(ends[b]), sel) * state + term

    part_rows = INNER // parts
    for pair in range(HEADS // 2):
        turned = state[:, pair * LANES : (pair + 1) * LANES].T.astype(BF16)
        for k in range(LANES // part_rows):
            part = (pair * LANES) // part_rows + k
            send_ref[part, 0:part_rows, :] = turned[k * part_rows : (k + 1) * part_rows, :]
    over = sum(ends[1:], ends[0])
    edge = jnp.exp(over - cum_ref[0:8, :]) * step[0:8, :]
    left = lax.broadcasted_iota(jnp.int32, (8, LANES), 1) < HEAD_DIM
    few = CONV - 1

    def halves(value):
        high = value.astype(BF16).astype(F32)
        return jnp.where(left, high, value - high)

    for part in range(parts):
        first = part * part_rows
        h, at = first // HEAD_DIM, first % HEAD_DIM
        cols = slice(h // 2 * LANES, (h // 2 + 1) * LANES)
        side = h % 2 * HEAD_DIM
        own = pltpu.roll(own_ref[:, cols], (2 * LANES - side - at) % LANES, 1)
        tail = pltpu.roll(tail_ref[:, cols], (2 * LANES + HEAD_DIM - side) % LANES, 1)
        if at:
            own = jnp.where(left, own, 0.0)
        decay = jnp.broadcast_to(over[:, h : h + 1], (8, LANES))
        pad_ref[part, 0:1, :] = halves(decay)[0:1, :]
        pad_ref[part, 1 : 1 + few, :] = jnp.where(left, own, tail)[0:few, :]
        pad_ref[part, 4 : 4 + few, :] = own_ref[0:few, INNER : INNER + STATE]
        pad_ref[part, 7 : 7 + few, :] = tail_ref[0:few, INNER : INNER + STATE]
        broad = jnp.broadcast_to(edge[:, h : h + 1], (8, LANES))
        pad_ref[part, 10 : 10 + few, :] = halves(broad)[0:few, :]
        pad_ref[part, 13 : 13 + few, :] = tail_ref[0:few, INNER + STATE :]
        send_ref[part, part_rows:, :] = pad_ref[part].astype(BF16)


def silu(x):
    return x * jax.nn.sigmoid(x)


def scan_kernel(got_ref, back_ref, pad_ref):
    parts, padded, _ = got_ref.shape
    part_rows = padded - PAD
    rows = slice(0, part_rows)
    offset = lax.axis_index("frames") * part_rows % HEAD_DIM
    few = lax.broadcasted_iota(jnp.int32, (8, LANES), 0) < CONV - 1
    left = lax.broadcasted_iota(jnp.int32, (8, LANES), 1) < HEAD_DIM
    pad_ref[0:PAD, :] = jnp.zeros((PAD, LANES), F32)
    pad_ref[(parts + 1) * PAD :, :] = jnp.zeros((8, LANES), F32)
    for d in range(parts):
        pad_ref[(d + 1) * PAD : (d + 2) * PAD, :] = got_ref[d, part_rows:, :].astype(F32)
    carry = jnp.zeros((part_rows, LANES), F32)
    for d in range(parts):
        back_ref[d, rows, :] = carry.astype(BF16)
        back_ref[d, part_rows:, :] = pad_ref[d * PAD : (d + 1) * PAD, :].astype(BF16)
        last, mine = d * PAD, (d + 1) * PAD
        decay = pad_ref[mine : mine + 1, :]
        decay = jnp.exp(decay + pltpu.roll(decay, HEAD_DIM, 1))
        from_tail = pltpu.roll(pad_ref[last + 1 : last + 9, :], HEAD_DIM, 1)
        if part_rows < HEAD_DIM:
            from_tail = pltpu.roll(jnp.where(left, from_tail, 0.0), (LANES - offset) % LANES, 1)
        values = silu(pad_ref[mine + 1 : mine + 9, :] + from_tail)
        in_map = silu(pad_ref[mine + 4 : mine + 12, :] + pad_ref[last + 7 : last + 15, :])
        edge = pad_ref[mine + 10 : mine + 18, :]
        edge = edge + pltpu.roll(edge, HEAD_DIM, 1)
        scaled = jnp.where(few, values.astype(BF16).astype(F32) * edge, 0.0)
        in_map = jnp.where(few, in_map, 0.0)
        added = dot(scaled, in_map, ((0,), (0,)))
        carry = decay * carry + (got_ref[d, rows, :].astype(F32) + added[rows, :])


def finish_kernel(
    layer,
    u_ref,
    w_ref,
    act_ref,
    own_ref,
    cum_ref,
    shifted_ref,
    edge_ref,
    state_ref,
    skip_ref,
    sel_ref,
    enter_ref,
    resid_ref,
    wo_ref,
    gain_ref,
    mods_ref,
    *rest,
):
    hidden_ref, a_ref, first_ref, y_ref, gate_ref, normed_ref = rest[-6:]
    rows = u_ref.shape[0]
    parts, padded, _ = enter_ref.shape
    part_rows = padded - PAD
    u = u_ref[...]
    sel = sel_ref[...]
    lane = lax.broadcasted_iota(jnp.int32, (SPAN, LANES), 1)
    left = lane < HEAD_DIM
    few = lax.broadcasted_iota(jnp.int32, (TAIL, LANES), 0) < CONV - 1
    nothing = jnp.zeros((TAIL - 8, LANES), F32)

    def fixed(cols, tail):
        total = jnp.concatenate([own_ref[:, cols] + tail[0:8, :], nothing], axis=0)
        first_ref[:, cols] = jnp.where(
            few, silu(total), act_ref[0:TAIL, cols].astype(F32)
        ).astype(BF16)

    for pair in range(HEADS // 2):
        pads = [
            enter_ref[h * HEAD_DIM // part_rows, part_rows:, :].astype(F32)
            for h in (2 * pair, 2 * pair + 1)
        ]
        tail = jnp.where(left[0:PAD], pltpu.roll(pads[0], HEAD_DIM, 1), pads[1])
        fixed(slice(pair * LANES, (pair + 1) * LANES), pltpu.roll(tail, PAD - 1, 0))
    common = enter_ref[0, part_rows:, :].astype(F32)
    fixed(slice(INNER, INNER + STATE), pltpu.roll(common, PAD - 7, 0))
    fixed(slice(INNER + STATE, INNER + 2 * STATE), pltpu.roll(common, PAD - 13, 0))

    def acts(b, cols):
        if b:
            return act_ref[b * SPAN : (b + 1) * SPAN, cols]
        return jnp.concatenate([first_ref[:, cols], act_ref[TAIL:SPAN, cols]], axis=0)

    first_tokens = lax.broadcasted_iota(jnp.int32, (TAIL, HEADS), 0) < CONV - 1
    early = spread(jnp.where(first_tokens, edge_ref[...], 0.0), sel)
    early = (first_ref[:, 0:INNER].astype(F32) * early).astype(BF16)
    late = dot(first_ref[:, INNER : INNER + STATE], early, ((0,), (0,)))

    spans = rows // SPAN
    out_maps = [acts(b, slice(INNER + STATE, INNER + 2 * STATE)) for b in range(spans)]
    out_map = jnp.concatenate(out_maps, axis=0)
    before = jnp.zeros((1, HEADS), F32)
    scales = []
    for b in range(spans):
        cum = cum_ref[b * SPAN : (b + 1) * SPAN, :]
        scales.append(jnp.exp(cum + before))
        before = before + cum[SPAN - 1 : SPAN, :]
    wide = spread(jnp.concatenate(scales, axis=0), sel)
    chunk = 256
    for c in range(0, INNER, chunk):
        cols = slice(c, c + chunk)
        gate_ref[:, cols] = silu(dot(u, w_ref[layer, :, cols]).astype(BF16).astype(F32))
        entering = jnp.concatenate(
            [enter_ref[p, 0:part_rows, :] for p in range(c // part_rows, (c + chunk) // part_rows)],
            axis=0,
        )
        y_ref[:, cols] = dot(out_map, entering, ((1,), (1,))) * wide[:, cols]
    decayed = jnp.ones((1, HEADS), F32)
    for b in range(1, spans):
        r = slice(b * SPAN, (b + 1) * SPAN)
        state = state_ref[(b - 1) * STATE : b * STATE, :] + spread_row(decayed, sel) * late
        cum = cum_ref[r, :]
        decayed = decayed * jnp.exp(cum[SPAN - 1 : SPAN, :])
        y_ref[r, :] = y_ref[r, :] + dot(out_maps[b], state.astype(BF16)) * spread(jnp.exp(cum), sel)

    q_pos = lax.broadcasted_iota(jnp.int32, (SPAN, SPAN), 0)
    s_pos = lax.broadcasted_iota(jnp.int32, (SPAN, SPAN), 1)
    lower = q_pos >= s_pos
    zero = jnp.zeros((SPAN, LANES), BF16)
    skip = spread_row(skip_ref[layer : layer + 1, :], sel)
    for b in range(spans):
        r = slice(b * SPAN, (b + 1) * SPAN)
        cum = cum_ref[r, :]
        affinity = dot(out_maps[b], acts(b, slice(INNER, INNER + STATE)), ((1,), (1,)))
        for pair in range(HEADS // 2):
            cols = slice(pair * LANES, (pair + 1) * LANES)
            values = acts(b, cols)
            mixing = []
            for h in (2 * pair, 2 * pair + 1):
                gap = cum[:, h : h + 1] - shifted_ref[h : h + 1, r]
                mixing.append(jnp.where(lower, affinity * jnp.exp(gap), 0.0).astype(BF16))
            both = jnp.concatenate(mixing, axis=1)
            stacked = jnp.concatenate(
                [jnp.where(left, values, zero), jnp.where(left, zero, values)], axis=0
            )
            y = dot(both, stacked) + skip[:, cols] * values.astype(F32) + y_ref[r, cols]
            y_ref[r, cols] = y * gate_ref[r, cols]

    row = lax.broadcasted_iota(jnp.int32, (chunk, chunk), 0) // HEAD_DIM
    col = lax.broadcasted_iota(jnp.int32, (chunk, chunk), 1) // HEAD_DIM
    same = jnp.where(row == col, 1.0 / HEAD_DIM, 0.0).astype(BF16)
    for c in range(0, INNER, chunk):
        cols = slice(c, c + chunk)
        total = y_ref[:, cols]
        square = total * total
        high = square.astype(BF16)
        low = (square - high.astype(F32)).astype(BF16)
        mean = dot(high, same) + dot(low, same)
        gain = gain_ref[layer : layer + 1, cols]
        normed_ref[:, cols] = (total * lax.rsqrt(mean + HEAD_EPS) * gain).astype(BF16)
    hidden = resid_ref[...].astype(F32) + dot(normed_ref[...], wo_ref[layer])
    hidden_ref[...] = hidden
    a_ref[...] = rms_mod(hidden, mods_ref[layer, 2:3, :], mods_ref[layer, 3:4, :])


def partial_attention(q_ref, seen, kv, half, r, k_rows, done):
    left = lax.broadcasted_iota(jnp.int32, (half, LANES), 1) < HEAD_DIM
    one = jnp.ones((k_rows.stop - k_rows.start, LANES), BF16)
    zero = jnp.zeros((half, LANES), BF16)
    seen = jnp.concatenate([seen, seen], axis=0)
    together = 2
    for group in range(0, ATT_HEADS // 2, together):
        columns = [slice(p * LANES, (p + 1) * LANES) for p in range(group, group + together)]
        scores = []
        for cols in columns:
            query = q_ref[r, cols]
            sides = jnp.concatenate(
                [jnp.where(left, query, zero), jnp.where(left, zero, query)], axis=0
            )
            scores.append(dot(sides, kv[k_rows, cols], ((1,), (1,))) + seen)
        tops = [jnp.max(s, axis=-1, keepdims=True) for s in scores]
        weights = [jnp.exp(s - t).astype(BF16) for s, t in zip(scores, tops)]
        for cols, weight, top in zip(columns, weights, tops):
            values = kv[k_rows, ATTN + cols.start : ATTN + cols.stop]
            both = dot(weight, jnp.concatenate([values, one], axis=1))
            number = jnp.where(left, both[:half, :LANES], both[half:, :LANES])
            total = jnp.where(left, both[:half, LANES:], both[half:, LANES:])
            done(cols, number, total, jnp.where(left, top[:half], top[half:]))


def memory_kernel(
    layer, a_ref, wq_ref, wm_ref, seen_ref, q_ref, number_ref, total_ref, top_ref, kv_ref
):
    rows = a_ref.shape[0]
    half = rows // 2
    a = a_ref[...]
    q_ref[...] = (dot(a, wq_ref[layer]).astype(BF16).astype(F32) * HEAD_DIM**-0.5).astype(BF16)
    kv_ref[...] = dot(a, wm_ref[layer]).astype(BF16)
    for part in range(2):
        r = slice(part * half, (part + 1) * half)
        k_rows = slice(0, (part + 1) * half)

        def done(cols, number, total, top):
            number_ref[r, cols] = number
            total_ref[r, cols] = total
            top_ref[r, cols] = top

        seen = seen_ref[r, rows : rows + k_rows.stop]
        partial_attention(q_ref, seen, kv_ref, half, r, k_rows, done)


def attend_kernel(
    layer,
    last,
    q_ref,
    number_ref,
    total_ref,
    top_ref,
    seen_ref,
    prev_ref,
    wm_ref,
    merge_ref,
    hidden_ref,
    mods_ref,
    *rest,
):
    if last:
        resid_ref, kv_ref, out_ref = rest
    else:
        resid_ref, u_ref, kv_ref, out_ref = rest
    rows = q_ref.shape[0]
    half = rows // 2
    kv_ref[...] = dot(prev_ref[...], wm_ref[layer]).astype(BF16)
    for part in range(2):
        r = slice(part * half, (part + 1) * half)
        k_rows = slice(part * half, rows)

        def done(cols, number, total, top):
            top_own = top_ref[r, cols]
            highest = jnp.maximum(top, top_own)
            mine, own = jnp.exp(top - highest), jnp.exp(top_own - highest)
            number = number * mine + number_ref[r, cols] * own
            total = total * mine + total_ref[r, cols] * own
            out_ref[r, cols] = (number / total).astype(BF16)

        partial_attention(q_ref, seen_ref[r, k_rows], kv_ref, half, r, k_rows, done)
    resid = hidden_ref[...] + dot(out_ref[...], merge_ref[layer])
    resid_ref[...] = resid
    if not last:
        u_ref[...] = rms_mod(resid, mods_ref[layer + 1, 0:1, :], mods_ref[layer + 1, 1:2, :])


WHOLE = pl.BlockSpec(memory_space=pltpu.VMEM)
SCALARS = pl.BlockSpec(memory_space=pltpu.SMEM)


def run(kernel, operands, outs, scratch=(), name=None, flops=0, scalars=()):
    moved = sum(o.size * o.dtype.itemsize for o in list(operands) + list(outs))
    return pl.pallas_call(
        kernel,
        in_specs=[SCALARS] * len(scalars) + [WHOLE] * len(operands),
        out_specs=[WHOLE] * len(outs),
        out_shape=list(outs),
        scratch_shapes=list(scratch),
        compiler_params=pltpu.CompilerParams(vmem_limit_bytes=20 * 1024 * 1024),
        cost_estimate=pl.CostEstimate(flops=flops, bytes_accessed=moved, transcendentals=0),
        name=name,
    )(*scalars, *operands)


def shape(dims, dtype):
    return jax.ShapeDtypeStruct(dims, dtype)


def from_behind(value, axis):
    count = lax.axis_size(axis)
    return lax.ppermute(value, axis, [(i, i + 1) for i in range(count - 1)])


def shards(
    latents,
    timestep,
    lookback,
    modulation,
    input_weight,
    step_weight,
    conv_weight,
    step_bias,
    decay_log,
    skip_gain,
    norm_gain,
    output_weight,
    query_weight,
    memory_weight,
    merge_weight,
):
    frames_dev, tok_frame, width = latents.shape
    rows = frames_dev * tok_frame
    spans = rows // SPAN
    parts = lax.axis_size("frames")
    part_rows = INNER // parts
    mixed = INNER + 2 * STATE
    step_weight = jnp.swapaxes(step_weight, 1, 2)
    step_bias = jnp.swapaxes(step_bias, 1, 2)
    resid = latents.reshape(rows, width)
    (sel,) = run(
        select_kernel, (), [shape((2 * HEADS, INNER), BF16)], name="select", flops=OPENING
    )
    u, mods, bias, seen = run(
        first_kernel,
        (sel, resid, modulation, step_bias),
        [
            shape((rows, width), BF16),
            shape((LAYERS,) + modulation.shape[2:], F32),
            shape((LAYERS, 8, HEADS), F32),
            shape((rows, 2 * rows), F32),
        ],
        name="first",
        flops=OPENING,
        scalars=(timestep, lookback),
    )
    for layer in range(LAYERS):
        act, own, cum, shifted, edge, state, send = run(
            functools.partial(local_kernel, layer, parts),
            (u, input_weight, step_weight, conv_weight, bias, decay_log, sel),
            [
                shape((rows, mixed), BF16),
                shape((8, mixed), F32),
                shape((rows, HEADS), F32),
                shape((HEADS, rows), F32),
                shape((TAIL, HEADS), F32),
                shape((max(spans - 1, 1) * STATE, INNER), F32),
                shape((parts, part_rows + PAD, LANES), BF16),
            ],
            [
                pltpu.VMEM((2, rows + 2 * TAIL, 256), F32),
                pltpu.VMEM((8, mixed), F32),
                pltpu.VMEM((parts, PAD, LANES), F32),
            ],
            name="local",
            flops=2 * rows * width * mixed,
        )
        got = lax.all_to_all(send, "frames", 0, 0)
        (back,) = run(
            scan_kernel,
            (got,),
            [shape(got.shape, BF16)],
            [pltpu.VMEM(((parts + 1) * PAD + 8, LANES), F32)],
            name="scan",
        )
        enter = lax.all_to_all(back, "frames", 0, 0)
        hidden, a = run(
            functools.partial(finish_kernel, layer),
            (u, input_weight, act, own, cum, shifted, edge, state, skip_gain, sel)
            + (enter, resid, output_weight, norm_gain, mods)
            + (() if layer else (query_weight, memory_weight, merge_weight)),
            [shape((rows, width), F32), shape((rows, width), BF16)],
            [
                pltpu.VMEM((TAIL, mixed), BF16),
                pltpu.VMEM((rows, INNER), F32),
                pltpu.VMEM((rows, INNER), F32),
                pltpu.VMEM((rows, INNER), BF16),
            ],
            name="finish",
        )
        prev = from_behind(a, "frames")
        q, number, total, top = run(
            functools.partial(memory_kernel, layer),
            (a, query_weight, memory_weight, seen),
            [shape((rows, ATTN), BF16)] + [shape((rows, ATTN), F32)] * 3,
            [pltpu.VMEM((rows, 2 * ATTN), BF16)],
            name="memory",
            flops=2 * rows * width * 3 * ATTN,
        )
        last = layer == LAYERS - 1
        outs = [shape((rows, width), F32)]
        if not last:
            outs += [shape((rows, width), BF16)]
        result = run(
            functools.partial(attend_kernel, layer, last),
            (q, number, total, top, seen, prev, memory_weight, merge_weight, hidden, mods),
            outs,
            [pltpu.VMEM((rows, 2 * ATTN), BF16), pltpu.VMEM((rows, ATTN), BF16)],
            name="attend",
        )
        resid = result[0]
        if not last:
            u = result[1]
    return resid.reshape(latents.shape)


def solution(mesh):
    sharded = P(("groups", "frames"))
    return jax.shard_map(
        shards,
        mesh=mesh,
        in_specs=(P(("groups", "frames"), None, None), sharded, sharded) + (P(),) * 12,
        out_specs=P(("groups", "frames"), None, None),
        check_vma=False,
    )
```

```python
import functools

import jax
import jax.numpy as jnp
from jax import lax
from jax.experimental import pallas as pl
from jax.experimental.pallas import tpu as pltpu
from jax.sharding import PartitionSpec as P

HEADS = 16
HEAD_DIM = 64
STATE = 128
ATT_HEADS = 8
LAYERS = 2
CONV = 4
SPAN = 128
WINDOW = 8
EPS = 1e-06
HEAD_EPS = 1e-05
INNER = HEADS * HEAD_DIM
ATTN = ATT_HEADS * HEAD_DIM
PAD = 16
BLOCK = HEAD_DIM + PAD
HALF = HEADS // 2
LANES = 128
TAIL = 16
F32 = jnp.float32
OPENING = 4 * 10**9
BF16 = jnp.bfloat16


def dot(a, b, dims=((1,), (0,)), precision=None):
    return lax.dot_general(a, b, (dims, ((), ())), precision=precision, preferred_element_type=F32)


def rms_mod(x, shift, scale):
    normed = x * lax.rsqrt(jnp.mean(x * x, axis=-1, keepdims=True) + EPS)
    return (normed * (1.0 + scale) + shift).astype(BF16)


def spread(per_head, sel):
    high = per_head.astype(BF16)
    low = (per_head - high.astype(F32)).astype(BF16)
    return dot(jnp.concatenate([high, low], axis=1), sel)


def spread_row(per_head, sel):
    return spread(jnp.broadcast_to(per_head, (16, HEADS)), sel)[0:1, :]


def select_kernel(sel_ref):
    row = lax.broadcasted_iota(jnp.int32, sel_ref.shape, 0) % HEADS
    head = lax.broadcasted_iota(jnp.int32, sel_ref.shape, 1) // HEAD_DIM
    sel_ref[...] = jnp.where(row == head, 1.0, 0.0).astype(BF16)


def first_kernel(
    step_ref,
    reach_ref,
    sel_ref,
    x_ref,
    all_mods_ref,
    all_bias_ref,
    u_ref,
    tail_ref,
    mods_ref,
    bias_ref,
    seen_ref,
):
    rows, width = u_ref.shape
    tok_frame = rows // WINDOW
    step = step_ref[0]
    for layer in range(LAYERS):
        mods_ref[layer] = all_mods_ref[layer, step].astype(F32)
    u = rms_mod(x_ref[...].astype(F32), mods_ref[0, 0:1, :], mods_ref[0, 1:2, :])
    u_ref[...] = u
    tail_ref[...] = u[rows - TAIL :]
    chosen = lax.broadcasted_iota(jnp.int32, (8, all_bias_ref.shape[-1]), 1) == step
    chosen = jnp.where(chosen, 1.0, 0.0).astype(F32)
    for layer in range(LAYERS):
        bias_ref[layer] = dot(
            chosen, all_bias_ref[layer], ((1,), (1,)), precision=lax.Precision.HIGHEST
        )
    key_frame = lax.broadcasted_iota(jnp.int32, (tok_frame, 2 * rows), 1) // tok_frame
    first = WINDOW - lax.axis_index("frames") * WINDOW
    for f in range(WINDOW):
        low = jnp.maximum(first, f + WINDOW - reach_ref[f])
        seen = (key_frame >= low) & (key_frame <= f + WINDOW)
        seen_ref[f * tok_frame : (f + 1) * tok_frame, :] = jnp.where(seen, 0.0, -1e30)


def core_index():
    return lax.axis_index("frames") % 2


def local_kernel(
    layer,
    u_ref,
    before_ref,
    w_ref,
    sw_ref,
    conv_ref,
    bias_ref,
    decay_ref,
    sel_ref,
    act_ref,
    own_ref,
    cum_ref,
    shifted_ref,
    edge_ref,
    state_ref,
    keep_ref,
    give_ref,
    ext_ref,
    tail_ref,
    pad_ref,
    send_ref,
):
    rows = u_ref.shape[0]
    u = u_ref[...]
    sel = sel_ref[...]
    core = core_index()
    tail_rows = before_ref[...].astype(F32) * core.astype(F32)
    tail_rows = tail_rows.astype(BF16)
    raw = dot(u, sw_ref[layer], ((1,), (1,))) + bias_ref[layer, 0:1, :]
    step = jnp.maximum(raw, 0.0) + jnp.log1p(jnp.exp(-jnp.abs(raw)))
    log_decay = -jnp.exp(decay_ref[layer : layer + 1, :]) * step
    log_step = jnp.log(step)
    q_pos = lax.broadcasted_iota(jnp.int32, (SPAN, SPAN), 0)
    s_pos = lax.broadcasted_iota(jnp.int32, (SPAN, SPAN), 1)
    lower = jnp.where(q_pos >= s_pos, 1.0, 0.0).astype(F32)
    whole_tokens = lax.broadcasted_iota(jnp.int32, (SPAN, HEADS), 0) >= (CONV - 1) * (1 - core)
    ends, edges = [], []
    for b in range(rows // SPAN):
        r = slice(b * SPAN, (b + 1) * SPAN)
        cum = dot(lower, log_decay[r], precision=lax.Precision.HIGHEST)
        end = cum[SPAN - 1 : SPAN, :]
        cum_ref[r, :] = cum
        shifted_ref[:, r] = (cum - log_step[r]).T
        edge = jnp.exp(end - cum) * step[r]
        if b == 0:
            edge_ref[...] = edge[0:TAIL, :]
            edge = jnp.where(whole_tokens, edge, 0.0)
        ends.append(end)
        edges.append(spread(edge, sel))

    chunk = 256
    for slot in range(2):
        ext_ref[slot, TAIL + rows :, :] = jnp.zeros((TAIL, chunk), F32)
    for c in [INNER] + list(range(0, INNER, chunk)):
        w = w_ref[layer, :, INNER + c : INNER + c + chunk]
        slot = c // chunk % 2
        ext_ref[slot, 0:TAIL, :] = dot(tail_rows, w).astype(BF16).astype(F32)
        ext_ref[slot, TAIL : TAIL + rows, :] = dot(u, w).astype(BF16).astype(F32)
        total, after = None, None
        for k in range(CONV):
            start = TAIL - (CONV - 1) + k
            taps = conv_ref[layer, k : k + 1, c : c + chunk]
            term = taps * ext_ref[slot, start : start + rows, :]
            next_term = taps * ext_ref[slot, start + rows : start + rows + 8, :]
            total = term if total is None else total + term
            after = next_term if after is None else after + next_term
        act_ref[:, c : c + chunk] = (total * jax.nn.sigmoid(total)).astype(BF16)
        own_ref[:, c : c + chunk] = total[0:8, :]
        tail_ref[:, c : c + chunk] = after

    state = None
    for b in range(rows // SPAN):
        r = slice(b * SPAN, (b + 1) * SPAN)
        in_map = act_ref[r, INNER : INNER + STATE]
        scaled = (act_ref[r, 0:INNER].astype(F32) * edges[b]).astype(BF16)
        term = dot(in_map, scaled, ((0,), (0,)))
        if state is None:
            state = term
        else:
            state_ref[(b - 1) * STATE : b * STATE, :] = state
            state = spread_row(jnp.exp(ends[b]), sel) * state + term

    for pair in range(HEADS // 2):
        turned = state[:, pair * LANES : (pair + 1) * LANES].T.astype(BF16)
        for side in range(2):
            send_ref[2 * pair + side, 0:HEAD_DIM, :] = turned[side * HEAD_DIM : (side + 1) * HEAD_DIM, :]
    over = sum(ends[1:], ends[0])
    edge = jnp.exp(over - cum_ref[0:8, :]) * step[0:8, :]
    left = lax.broadcasted_iota(jnp.int32, (8, LANES), 1) < HEAD_DIM
    few = CONV - 1
    for h in range(HEADS):
        cols = slice(h // 2 * LANES, (h // 2 + 1) * LANES)
        own, tail = own_ref[:, cols], tail_ref[:, cols]
        if h % 2:
            own = pltpu.roll(own, HEAD_DIM, 1)
        else:
            tail = pltpu.roll(tail, HEAD_DIM, 1)
        pad_ref[h, 0:1, :] = halves(jnp.broadcast_to(over[:, h : h + 1], (8, LANES)))[0:1, :]
        pad_ref[h, 1 : 1 + few, :] = jnp.where(left, own, tail)[0:few, :]
        pad_ref[h, 4 : 4 + few, :] = own_ref[0:few, INNER : INNER + STATE]
        pad_ref[h, 7 : 7 + few, :] = tail_ref[0:few, INNER : INNER + STATE]
        broad = jnp.broadcast_to(edge[:, h : h + 1], (8, LANES))
        pad_ref[h, 10 : 10 + few, :] = halves(broad)[0:few, :]
        pad_ref[h, 13 : 13 + few, :] = tail_ref[0:few, INNER + STATE :]
        send_ref[h, HEAD_DIM:, :] = pad_ref[h].astype(BF16)
    keep_ref[...] = send_ref[pl.ds(core * HALF, HALF)]
    give_ref[...] = send_ref[pl.ds((1 - core) * HALF, HALF)]


def halves(value):
    left = lax.broadcasted_iota(jnp.int32, value.shape, 1) < HEAD_DIM
    high = value.astype(BF16).astype(F32)
    return jnp.where(left, high, value - high)


def joined(value):
    return value + pltpu.roll(value, HEAD_DIM, 1)


def chip_kernel(keep_ref, got_ref, send_ref, pair_ref):
    parts, padded, _ = send_ref.shape
    part_rows = padded - PAD
    core = core_index()
    pair_ref[core] = keep_ref[...]
    pair_ref[1 - core] = got_ref[...]
    row = lax.broadcasted_iota(jnp.int32, (PAD, LANES), 0)
    left = lax.broadcasted_iota(jnp.int32, (PAD, LANES), 1) < HEAD_DIM
    for h in range(HALF):
        one = pair_ref[0, h, HEAD_DIM:, :].astype(F32)
        two = pair_ref[1, h, HEAD_DIM:, :].astype(F32)
        one_sum, two_sum = joined(one), joined(two)
        decay = jnp.exp(two_sum[0:1, :])
        state = decay * pair_ref[0, h, 0:HEAD_DIM, :].astype(F32) + pair_ref[
            1, h, 0:HEAD_DIM, :
        ].astype(F32)
        state = state.astype(BF16)
        exact = halves(jnp.where(row == 0, one_sum + two_sum, one_sum * decay))
        for k in range(HEAD_DIM // part_rows):
            at = k * part_rows
            own = pltpu.roll(jnp.where(left, one, 0.0), LANES - at, 1) if at else one
            pad = jnp.where(row < 4, jnp.where(left, own, two), jnp.where(row < 7, one, two))
            pad = jnp.where((row == 0) | ((row >= 10) & (row < 13)), exact, pad)
            part = h * (HEAD_DIM // part_rows) + k
            send_ref[part, 0:part_rows, :] = state[at : at + part_rows, :]
            send_ref[part, part_rows:, :] = pad.astype(BF16)


def enter_kernel(keep_ref, got_ref, back_ref, mine_ref, give_ref, pair_ref, enter_ref, pad_ref):
    parts, padded, _ = back_ref.shape
    part_rows = padded - PAD
    each = HEAD_DIM // part_rows
    core = core_index()
    pair_ref[core] = keep_ref[...]
    pair_ref[1 - core] = got_ref[...]
    few = lax.broadcasted_iota(jnp.int32, (8, LANES), 0) < CONV - 1
    for h in range(HALF):
        pad = back_ref[h * each, part_rows:, :]
        pad_ref[2 * h] = pad.astype(F32)
        pad_ref[2 * h + 1] = pair_ref[0, h, HEAD_DIM:, :].astype(F32)
    for h in range(HALF):
        last, mine = 2 * h, 2 * h + 1
        entering = jnp.concatenate(
            [back_ref[h * each + k, 0:part_rows, :] for k in range(each)], axis=0
        )
        values = silu(pad_ref[mine, 1:9, :] + pltpu.roll(pad_ref[last, 1:9, :], HEAD_DIM, 1))
        in_map = silu(pad_ref[mine, 4:12, :] + pad_ref[last, 7:15, :])
        edge = joined(pad_ref[mine, 8:16, :])
        edge = pltpu.roll(edge, 6, 0)
        scaled = jnp.where(few, values.astype(BF16).astype(F32) * edge, 0.0)
        added = dot(scaled, jnp.where(few, in_map, 0.0), ((0,), (0,)))[0:HEAD_DIM, :]
        decay = jnp.exp(joined(pad_ref[mine, 0:8, :])[0:1, :])
        after = decay * entering.astype(F32) + pair_ref[0, h, 0:HEAD_DIM, :].astype(F32) + added
        pad = back_ref[h * each, part_rows:, :]
        enter_ref[0, h, 0:HEAD_DIM, :] = entering
        enter_ref[1, h, 0:HEAD_DIM, :] = after.astype(BF16)
        enter_ref[0, h, HEAD_DIM:, :] = pad
        enter_ref[1, h, HEAD_DIM:, :] = pad
    mine_ref[...] = enter_ref[core]
    give_ref[...] = enter_ref[1 - core]


def silu(x):
    return x * jax.nn.sigmoid(x)


def scan_kernel(got_ref, back_ref, pad_ref):
    parts, padded, _ = got_ref.shape
    part_rows = padded - PAD
    rows = slice(0, part_rows)
    offset = lax.axis_index("frames") // 2 * part_rows % HEAD_DIM
    few = lax.broadcasted_iota(jnp.int32, (8, LANES), 0) < CONV - 1
    left = lax.broadcasted_iota(jnp.int32, (8, LANES), 1) < HEAD_DIM
    pad_ref[0:PAD, :] = jnp.zeros((PAD, LANES), F32)
    pad_ref[(parts + 1) * PAD :, :] = jnp.zeros((8, LANES), F32)
    for d in range(parts):
        pad_ref[(d + 1) * PAD : (d + 2) * PAD, :] = got_ref[d, part_rows:, :].astype(F32)
    carry = jnp.zeros((part_rows, LANES), F32)
    for d in range(parts):
        back_ref[d, rows, :] = carry.astype(BF16)
        back_ref[d, part_rows:, :] = pad_ref[d * PAD : (d + 1) * PAD, :].astype(BF16)
        last, mine = d * PAD, (d + 1) * PAD
        decay = pad_ref[mine : mine + 1, :]
        decay = jnp.exp(decay + pltpu.roll(decay, HEAD_DIM, 1))
        from_tail = pltpu.roll(pad_ref[last + 1 : last + 9, :], HEAD_DIM, 1)
        if part_rows < HEAD_DIM:
            from_tail = pltpu.roll(jnp.where(left, from_tail, 0.0), (LANES - offset) % LANES, 1)
        values = silu(pad_ref[mine + 1 : mine + 9, :] + from_tail)
        in_map = silu(pad_ref[mine + 4 : mine + 12, :] + pad_ref[last + 7 : last + 15, :])
        edge = pad_ref[mine + 10 : mine + 18, :]
        edge = edge + pltpu.roll(edge, HEAD_DIM, 1)
        scaled = jnp.where(few, values.astype(BF16).astype(F32) * edge, 0.0)
        in_map = jnp.where(few, in_map, 0.0)
        added = dot(scaled, in_map, ((0,), (0,)))
        carry = decay * carry + (got_ref[d, rows, :].astype(F32) + added[rows, :])


def finish_kernel(
    layer,
    u_ref,
    w_ref,
    act_ref,
    own_ref,
    cum_ref,
    shifted_ref,
    edge_ref,
    state_ref,
    skip_ref,
    sel_ref,
    mine_ref,
    other_ref,
    resid_ref,
    wo_ref,
    gain_ref,
    mods_ref,
    *rest,
):
    hidden_ref, a_ref, first_ref, y_ref, gate_ref, normed_ref, enter_ref = rest[-7:]
    rows = u_ref.shape[0]
    core = core_index()
    enter_ref[pl.ds(core * HALF, HALF)] = mine_ref[...]
    enter_ref[pl.ds((1 - core) * HALF, HALF)] = other_ref[...]
    start = (1 - core).astype(F32)
    u = u_ref[...]
    sel = sel_ref[...]
    lane = lax.broadcasted_iota(jnp.int32, (SPAN, LANES), 1)
    left = lane < HEAD_DIM
    few = lax.broadcasted_iota(jnp.int32, (TAIL, LANES), 0) < CONV - 1
    nothing = jnp.zeros((TAIL - 8, LANES), F32)

    def fixed(cols, tail):
        total = jnp.concatenate([own_ref[:, cols] + start * tail[0:8, :], nothing], axis=0)
        first_ref[:, cols] = jnp.where(
            few, silu(total), act_ref[0:TAIL, cols].astype(F32)
        ).astype(BF16)

    for pair in range(HEADS // 2):
        pads = [
            enter_ref[h, HEAD_DIM:, :].astype(F32)
            for h in (2 * pair, 2 * pair + 1)
        ]
        tail = jnp.where(left[0:PAD], pltpu.roll(pads[0], HEAD_DIM, 1), pads[1])
        fixed(slice(pair * LANES, (pair + 1) * LANES), pltpu.roll(tail, PAD - 1, 0))
    common = enter_ref[0, HEAD_DIM:, :].astype(F32)
    fixed(slice(INNER, INNER + STATE), pltpu.roll(common, PAD - 7, 0))
    fixed(slice(INNER + STATE, INNER + 2 * STATE), pltpu.roll(common, PAD - 13, 0))

    def acts(b, cols):
        if b:
            return act_ref[b * SPAN : (b + 1) * SPAN, cols]
        return jnp.concatenate([first_ref[:, cols], act_ref[TAIL:SPAN, cols]], axis=0)

    first_tokens = lax.broadcasted_iota(jnp.int32, (TAIL, HEADS), 0) < CONV - 1
    early = spread(jnp.where(first_tokens, edge_ref[...], 0.0) * start, sel)
    early = (first_ref[:, 0:INNER].astype(F32) * early).astype(BF16)
    late = dot(first_ref[:, INNER : INNER + STATE], early, ((0,), (0,)))

    spans = rows // SPAN
    out_maps = [acts(b, slice(INNER + STATE, INNER + 2 * STATE)) for b in range(spans)]
    out_map = jnp.concatenate(out_maps, axis=0)
    before = jnp.zeros((1, HEADS), F32)
    scales = []
    for b in range(spans):
        cum = cum_ref[b * SPAN : (b + 1) * SPAN, :]
        scales.append(jnp.exp(cum + before))
        before = before + cum[SPAN - 1 : SPAN, :]
    wide = spread(jnp.concatenate(scales, axis=0), sel)
    chunk = 256
    for c in range(0, INNER, chunk):
        cols = slice(c, c + chunk)
        gate_ref[:, cols] = silu(dot(u, w_ref[layer, :, cols]).astype(BF16).astype(F32))
        entering = jnp.concatenate(
            [enter_ref[h, 0:HEAD_DIM, :] for h in range(c // HEAD_DIM, (c + chunk) // HEAD_DIM)],
            axis=0,
        )
        y_ref[:, cols] = dot(out_map, entering, ((1,), (1,))) * wide[:, cols]
    decayed = jnp.ones((1, HEADS), F32)
    for b in range(1, spans):
        r = slice(b * SPAN, (b + 1) * SPAN)
        state = state_ref[(b - 1) * STATE : b * STATE, :] + spread_row(decayed, sel) * late
        cum = cum_ref[r, :]
        decayed = decayed * jnp.exp(cum[SPAN - 1 : SPAN, :])
        y_ref[r, :] = y_ref[r, :] + dot(out_maps[b], state.astype(BF16)) * spread(jnp.exp(cum), sel)

    q_pos = lax.broadcasted_iota(jnp.int32, (SPAN, SPAN), 0)
    s_pos = lax.broadcasted_iota(jnp.int32, (SPAN, SPAN), 1)
    lower = q_pos >= s_pos
    zero = jnp.zeros((SPAN, LANES), BF16)
    skip = spread_row(skip_ref[layer : layer + 1, :], sel)
    for b in range(spans):
        r = slice(b * SPAN, (b + 1) * SPAN)
        cum = cum_ref[r, :]
        affinity = dot(out_maps[b], acts(b, slice(INNER, INNER + STATE)), ((1,), (1,)))
        for pair in range(HEADS // 2):
            cols = slice(pair * LANES, (pair + 1) * LANES)
            values = acts(b, cols)
            mixing = []
            for h in (2 * pair, 2 * pair + 1):
                gap = cum[:, h : h + 1] - shifted_ref[h : h + 1, r]
                mixing.append(jnp.where(lower, affinity * jnp.exp(gap), 0.0).astype(BF16))
            both = jnp.concatenate(mixing, axis=1)
            stacked = jnp.concatenate(
                [jnp.where(left, values, zero), jnp.where(left, zero, values)], axis=0
            )
            y = dot(both, stacked) + skip[:, cols] * values.astype(F32) + y_ref[r, cols]
            y_ref[r, cols] = y * gate_ref[r, cols]

    row = lax.broadcasted_iota(jnp.int32, (chunk, chunk), 0) // HEAD_DIM
    col = lax.broadcasted_iota(jnp.int32, (chunk, chunk), 1) // HEAD_DIM
    same = jnp.where(row == col, 1.0 / HEAD_DIM, 0.0).astype(BF16)
    for c in range(0, INNER, chunk):
        cols = slice(c, c + chunk)
        total = y_ref[:, cols]
        square = total * total
        high = square.astype(BF16)
        low = (square - high.astype(F32)).astype(BF16)
        mean = dot(high, same) + dot(low, same)
        gain = gain_ref[layer : layer + 1, cols]
        normed_ref[:, cols] = (total * lax.rsqrt(mean + HEAD_EPS) * gain).astype(BF16)
    hidden = resid_ref[...].astype(F32) + dot(normed_ref[...], wo_ref[layer])
    hidden_ref[...] = hidden
    a_ref[...] = rms_mod(hidden, mods_ref[layer, 2:3, :], mods_ref[layer, 3:4, :])


def partial_attention(q_ref, seen, kv, half, r, k_rows, done):
    left = lax.broadcasted_iota(jnp.int32, (half, LANES), 1) < HEAD_DIM
    one = jnp.ones((k_rows.stop - k_rows.start, LANES), BF16)
    zero = jnp.zeros((half, LANES), BF16)
    seen = jnp.concatenate([seen, seen], axis=0)
    together = 2
    for group in range(0, ATT_HEADS // 2, together):
        columns = [slice(p * LANES, (p + 1) * LANES) for p in range(group, group + together)]
        scores = []
        for cols in columns:
            query = q_ref[r, cols]
            sides = jnp.concatenate(
                [jnp.where(left, query, zero), jnp.where(left, zero, query)], axis=0
            )
            scores.append(dot(sides, kv[k_rows, cols], ((1,), (1,))) + seen)
        tops = [jnp.max(s, axis=-1, keepdims=True) for s in scores]
        weights = [jnp.exp(s - t).astype(BF16) for s, t in zip(scores, tops)]
        for cols, weight, top in zip(columns, weights, tops):
            values = kv[k_rows, ATTN + cols.start : ATTN + cols.stop]
            both = dot(weight, jnp.concatenate([values, one], axis=1))
            number = jnp.where(left, both[:half, :LANES], both[half:, :LANES])
            total = jnp.where(left, both[:half, LANES:], both[half:, LANES:])
            done(cols, number, total, jnp.where(left, top[:half], top[half:]))


def memory_kernel(
    layer, a_ref, wq_ref, wm_ref, seen_ref, q_ref, number_ref, total_ref, top_ref, kv_ref
):
    rows = a_ref.shape[0]
    half = rows // 2
    a = a_ref[...]
    q_ref[...] = (dot(a, wq_ref[layer]).astype(BF16).astype(F32) * HEAD_DIM**-0.5).astype(BF16)
    kv_ref[...] = dot(a, wm_ref[layer]).astype(BF16)
    for part in range(2):
        r = slice(part * half, (part + 1) * half)
        k_rows = slice(0, (part + 1) * half)

        def done(cols, number, total, top):
            number_ref[r, cols] = number
            total_ref[r, cols] = total
            top_ref[r, cols] = top

        seen = seen_ref[r, rows : rows + k_rows.stop]
        partial_attention(q_ref, seen, kv_ref, half, r, k_rows, done)


def attend_kernel(
    layer,
    last,
    q_ref,
    number_ref,
    total_ref,
    top_ref,
    seen_ref,
    prev_ref,
    wm_ref,
    merge_ref,
    hidden_ref,
    mods_ref,
    *rest,
):
    if last:
        resid_ref, kv_ref, out_ref = rest
    else:
        resid_ref, u_ref, tail_ref, kv_ref, out_ref = rest
    rows = q_ref.shape[0]
    half = rows // 2
    kv_ref[...] = dot(prev_ref[...], wm_ref[layer]).astype(BF16)
    for part in range(2):
        r = slice(part * half, (part + 1) * half)
        k_rows = slice(part * half, rows)

        def done(cols, number, total, top):
            top_own = top_ref[r, cols]
            highest = jnp.maximum(top, top_own)
            mine, own = jnp.exp(top - highest), jnp.exp(top_own - highest)
            number = number * mine + number_ref[r, cols] * own
            total = total * mine + total_ref[r, cols] * own
            out_ref[r, cols] = (number / total).astype(BF16)

        partial_attention(q_ref, seen_ref[r, k_rows], kv_ref, half, r, k_rows, done)
    resid = hidden_ref[...] + dot(out_ref[...], merge_ref[layer])
    resid_ref[...] = resid
    if not last:
        u = rms_mod(resid, mods_ref[layer + 1, 0:1, :], mods_ref[layer + 1, 1:2, :])
        u_ref[...] = u
        tail_ref[...] = u[rows - TAIL :]


WHOLE = pl.BlockSpec(memory_space=pltpu.VMEM)
SCALARS = pl.BlockSpec(memory_space=pltpu.SMEM)


def run(kernel, operands, outs, scratch=(), name=None, flops=0, scalars=()):
    moved = sum(o.size * o.dtype.itemsize for o in list(operands) + list(outs))
    return pl.pallas_call(
        kernel,
        in_specs=[SCALARS] * len(scalars) + [WHOLE] * len(operands),
        out_specs=[WHOLE] * len(outs),
        out_shape=list(outs),
        scratch_shapes=list(scratch),
        compiler_params=pltpu.CompilerParams(vmem_limit_bytes=20 * 1024 * 1024),
        cost_estimate=pl.CostEstimate(flops=flops, bytes_accessed=moved, transcendentals=0),
        name=name,
    )(*scalars, *operands)


def shape(dims, dtype):
    return jax.ShapeDtypeStruct(dims, dtype)


def swapped(value, axis):
    count = lax.axis_size(axis)
    return lax.ppermute(value, axis, [(i, i ^ 1) for i in range(count)])


def over_chips(value, axis):
    count = lax.axis_size(axis)
    groups = [list(range(core, count, 2)) for core in range(2)]
    return lax.all_to_all(value, axis, 0, 0, axis_index_groups=groups)


def from_behind(value, axis):
    count = lax.axis_size(axis)
    return lax.ppermute(value, axis, [(i, i + 1) for i in range(count - 1)])


def shards(
    latents,
    timestep,
    lookback,
    modulation,
    input_weight,
    step_weight,
    conv_weight,
    step_bias,
    decay_log,
    skip_gain,
    norm_gain,
    output_weight,
    query_weight,
    memory_weight,
    merge_weight,
):
    frames_dev, tok_frame, width = latents.shape
    rows = frames_dev * tok_frame
    spans = rows // SPAN
    parts = lax.axis_size("frames") // 2
    part_rows = HALF * HEAD_DIM // parts
    mixed = INNER + 2 * STATE
    step_weight = jnp.swapaxes(step_weight, 1, 2)
    step_bias = jnp.swapaxes(step_bias, 1, 2)
    resid = latents.reshape(rows, width)
    (sel,) = run(
        select_kernel, (), [shape((2 * HEADS, INNER), BF16)], name="select", flops=OPENING
    )
    u, tail, mods, bias, seen = run(
        first_kernel,
        (sel, resid, modulation, step_bias),
        [
            shape((rows, width), BF16),
            shape((TAIL, width), BF16),
            shape((LAYERS,) + modulation.shape[2:], F32),
            shape((LAYERS, 8, HEADS), F32),
            shape((rows, 2 * rows), F32),
        ],
        name="first",
        flops=OPENING,
        scalars=(timestep, lookback),
    )
    for layer in range(LAYERS):
        before = swapped(tail, "frames")
        act, own, cum, shifted, edge, state, keep, give = run(
            functools.partial(local_kernel, layer),
            (u, before, input_weight, step_weight, conv_weight, bias, decay_log, sel),
            [
                shape((rows, mixed), BF16),
                shape((8, mixed), F32),
                shape((rows, HEADS), F32),
                shape((HEADS, rows), F32),
                shape((TAIL, HEADS), F32),
                shape((max(spans - 1, 1) * STATE, INNER), F32),
                shape((HALF, BLOCK, LANES), BF16),
                shape((HALF, BLOCK, LANES), BF16),
            ],
            [
                pltpu.VMEM((2, rows + 2 * TAIL, 256), F32),
                pltpu.VMEM((8, mixed), F32),
                pltpu.VMEM((HEADS, PAD, LANES), F32),
                pltpu.VMEM((HEADS, BLOCK, LANES), BF16),
            ],
            name="local",
            flops=2 * rows * width * mixed,
        )
        got = swapped(give, "frames")
        (send,) = run(
            chip_kernel,
            (keep, got),
            [shape((parts, part_rows + PAD, LANES), BF16)],
            [pltpu.VMEM((2, HALF, BLOCK, LANES), BF16)],
            name="chip",
        )
        (back,) = run(
            scan_kernel,
            (over_chips(send, "frames"),),
            [shape(send.shape, BF16)],
            [pltpu.VMEM(((parts + 1) * PAD + 8, LANES), F32)],
            name="scan",
        )
        mine, give = run(
            enter_kernel,
            (keep, got, over_chips(back, "frames")),
            [shape(keep.shape, BF16)] * 2,
            [
                pltpu.VMEM((2, HALF, BLOCK, LANES), BF16),
                pltpu.VMEM((2, HALF, BLOCK, LANES), BF16),
                pltpu.VMEM((HEADS, PAD, LANES), F32),
            ],
            name="enter",
        )
        other = swapped(give, "frames")
        hidden, a = run(
            functools.partial(finish_kernel, layer),
            (u, input_weight, act, own, cum, shifted, edge, state, skip_gain, sel)
            + (mine, other, resid, output_weight, norm_gain, mods)
            + (() if layer else (query_weight, memory_weight, merge_weight)),
            [shape((rows, width), F32), shape((rows, width), BF16)],
            [
                pltpu.VMEM((TAIL, mixed), BF16),
                pltpu.VMEM((rows, INNER), F32),
                pltpu.VMEM((rows, INNER), F32),
                pltpu.VMEM((rows, INNER), BF16),
                pltpu.VMEM((HEADS, BLOCK, LANES), BF16),
            ],
            name="finish",
        )
        prev = from_behind(a, "frames")
        q, number, total, top = run(
            functools.partial(memory_kernel, layer),
            (a, query_weight, memory_weight, seen),
            [shape((rows, ATTN), BF16)] + [shape((rows, ATTN), F32)] * 3,
            [pltpu.VMEM((rows, 2 * ATTN), BF16)],
            name="memory",
            flops=2 * rows * width * 3 * ATTN,
        )
        last = layer == LAYERS - 1
        outs = [shape((rows, width), F32)]
        if not last:
            outs += [shape((rows, width), BF16), shape((TAIL, width), BF16)]
        result = run(
            functools.partial(attend_kernel, layer, last),
            (q, number, total, top, seen, prev, memory_weight, merge_weight, hidden, mods),
            outs,
            [pltpu.VMEM((rows, 2 * ATTN), BF16), pltpu.VMEM((rows, ATTN), BF16)],
            name="attend",
        )
        resid = result[0]
        if not last:
            u, tail = result[1:]
    return resid.reshape(latents.shape)


def solution(mesh):
    sharded = P(("groups", "frames"))
    return jax.shard_map(
        shards,
        mesh=mesh,
        in_specs=(P(("groups", "frames"), None, None), sharded, sharded) + (P(),) * 12,
        out_specs=P(("groups", "frames"), None, None),
        check_vma=False,
    )
```

```python
import functools

import jax
import jax.numpy as jnp
from jax import lax
from jax.experimental import pallas as pl
from jax.experimental.pallas import tpu as pltpu
from jax.sharding import PartitionSpec as P

HEADS = 16
HEAD_DIM = 64
STATE = 128
ATT_HEADS = 8
LAYERS = 2
CONV = 4
SPAN = 128
WINDOW = 8
EPS = 1e-06
HEAD_EPS = 1e-05
INNER = HEADS * HEAD_DIM
ATTN = ATT_HEADS * HEAD_DIM
PAD = 16
BLOCK = HEAD_DIM + PAD
HALF = HEADS // 2
LANES = 128
TAIL = 16
F32 = jnp.float32
OPENING = 4 * 10**9
BF16 = jnp.bfloat16


def dot(a, b, dims=((1,), (0,)), precision=None):
    return lax.dot_general(a, b, (dims, ((), ())), precision=precision, preferred_element_type=F32)


def rms_mod(x, shift, scale):
    normed = x * lax.rsqrt(jnp.mean(x * x, axis=-1, keepdims=True) + EPS)
    return (normed * (1.0 + scale) + shift).astype(BF16)


def spread(per_head, sel):
    high = per_head.astype(BF16)
    low = (per_head - high.astype(F32)).astype(BF16)
    return dot(jnp.concatenate([high, low], axis=1), sel)


def spread_row(per_head, sel):
    return spread(jnp.broadcast_to(per_head, (16, HEADS)), sel)[0:1, :]


def select_kernel(sel_ref):
    row = lax.broadcasted_iota(jnp.int32, sel_ref.shape, 0) % HEADS
    head = lax.broadcasted_iota(jnp.int32, sel_ref.shape, 1) // HEAD_DIM
    sel_ref[...] = jnp.where(row == head, 1.0, 0.0).astype(BF16)


def first_kernel(
    step_ref,
    sel_ref,
    x_ref,
    all_mods_ref,
    all_bias_ref,
    u_ref,
    tail_ref,
    mods_ref,
    bias_ref,
):
    rows, width = u_ref.shape
    step = step_ref[0]
    for layer in range(LAYERS):
        mods_ref[layer] = all_mods_ref[layer, step].astype(F32)
    u = rms_mod(x_ref[...].astype(F32), mods_ref[0, 0:1, :], mods_ref[0, 1:2, :])
    u_ref[...] = u
    tail_ref[...] = u[rows - TAIL :]
    chosen = lax.broadcasted_iota(jnp.int32, (8, all_bias_ref.shape[-1]), 1) == step
    chosen = jnp.where(chosen, 1.0, 0.0).astype(F32)
    for layer in range(LAYERS):
        bias_ref[layer] = dot(
            chosen, all_bias_ref[layer], ((1,), (1,)), precision=lax.Precision.HIGHEST
        )


def core_index():
    return lax.axis_index("frames") % 2


def local_kernel(
    layer,
    u_ref,
    before_ref,
    w_ref,
    sw_ref,
    conv_ref,
    bias_ref,
    decay_ref,
    sel_ref,
    act_ref,
    own_ref,
    cum_ref,
    shifted_ref,
    edge_ref,
    state_ref,
    keep_ref,
    give_ref,
    ext_ref,
    tail_ref,
    pad_ref,
    send_ref,
):
    rows = u_ref.shape[0]
    u = u_ref[...]
    sel = sel_ref[...]
    core = core_index()
    tail_rows = before_ref[...].astype(F32) * core.astype(F32)
    tail_rows = tail_rows.astype(BF16)
    raw = dot(u, sw_ref[layer], ((1,), (1,))) + bias_ref[layer, 0:1, :]
    step = jnp.maximum(raw, 0.0) + jnp.log1p(jnp.exp(-jnp.abs(raw)))
    log_decay = -jnp.exp(decay_ref[layer : layer + 1, :]) * step
    log_step = jnp.log(step)
    q_pos = lax.broadcasted_iota(jnp.int32, (SPAN, SPAN), 0)
    s_pos = lax.broadcasted_iota(jnp.int32, (SPAN, SPAN), 1)
    lower = jnp.where(q_pos >= s_pos, 1.0, 0.0).astype(F32)
    whole_tokens = lax.broadcasted_iota(jnp.int32, (SPAN, HEADS), 0) >= (CONV - 1) * (1 - core)
    ends, edges = [], []
    for b in range(rows // SPAN):
        r = slice(b * SPAN, (b + 1) * SPAN)
        cum = dot(lower, log_decay[r], precision=lax.Precision.HIGHEST)
        end = cum[SPAN - 1 : SPAN, :]
        cum_ref[r, :] = cum
        shifted_ref[:, r] = (cum - log_step[r]).T
        edge = jnp.exp(end - cum) * step[r]
        if b == 0:
            edge_ref[...] = edge[0:TAIL, :]
            edge = jnp.where(whole_tokens, edge, 0.0)
        ends.append(end)
        edges.append(spread(edge, sel))

    chunk = 256
    for slot in range(2):
        ext_ref[slot, TAIL + rows :, :] = jnp.zeros((TAIL, chunk), F32)
    for c in [INNER] + list(range(0, INNER, chunk)):
        w = w_ref[layer, :, INNER + c : INNER + c + chunk]
        slot = c // chunk % 2
        ext_ref[slot, 0:TAIL, :] = dot(tail_rows, w).astype(BF16).astype(F32)
        ext_ref[slot, TAIL : TAIL + rows, :] = dot(u, w).astype(BF16).astype(F32)
        total, after = None, None
        for k in range(CONV):
            start = TAIL - (CONV - 1) + k
            taps = conv_ref[layer, k : k + 1, c : c + chunk]
            term = taps * ext_ref[slot, start : start + rows, :]
            next_term = taps * ext_ref[slot, start + rows : start + rows + 8, :]
            total = term if total is None else total + term
            after = next_term if after is None else after + next_term
        act_ref[:, c : c + chunk] = (total * jax.nn.sigmoid(total)).astype(BF16)
        own_ref[:, c : c + chunk] = total[0:8, :]
        tail_ref[:, c : c + chunk] = after

    state = None
    for b in range(rows // SPAN):
        r = slice(b * SPAN, (b + 1) * SPAN)
        in_map = act_ref[r, INNER : INNER + STATE]
        scaled = (act_ref[r, 0:INNER].astype(F32) * edges[b]).astype(BF16)
        term = dot(in_map, scaled, ((0,), (0,)))
        if state is None:
            state = term
        else:
            state_ref[(b - 1) * STATE : b * STATE, :] = state
            state = spread_row(jnp.exp(ends[b]), sel) * state + term

    for pair in range(HEADS // 2):
        turned = state[:, pair * LANES : (pair + 1) * LANES].T.astype(BF16)
        for side in range(2):
            send_ref[2 * pair + side, 0:HEAD_DIM, :] = turned[side * HEAD_DIM : (side + 1) * HEAD_DIM, :]
    over = sum(ends[1:], ends[0])
    edge = jnp.exp(over - cum_ref[0:8, :]) * step[0:8, :]
    left = lax.broadcasted_iota(jnp.int32, (8, LANES), 1) < HEAD_DIM
    few = CONV - 1
    for h in range(HEADS):
        cols = slice(h // 2 * LANES, (h // 2 + 1) * LANES)
        own, tail = own_ref[:, cols], tail_ref[:, cols]
        if h % 2:
            own = pltpu.roll(own, HEAD_DIM, 1)
        else:
            tail = pltpu.roll(tail, HEAD_DIM, 1)
        pad_ref[h, 0:1, :] = halves(jnp.broadcast_to(over[:, h : h + 1], (8, LANES)))[0:1, :]
        pad_ref[h, 1 : 1 + few, :] = jnp.where(left, own, tail)[0:few, :]
        pad_ref[h, 4 : 4 + few, :] = own_ref[0:few, INNER : INNER + STATE]
        pad_ref[h, 7 : 7 + few, :] = tail_ref[0:few, INNER : INNER + STATE]
        broad = jnp.broadcast_to(edge[:, h : h + 1], (8, LANES))
        pad_ref[h, 10 : 10 + few, :] = halves(broad)[0:few, :]
        pad_ref[h, 13 : 13 + few, :] = tail_ref[0:few, INNER + STATE :]
        send_ref[h, HEAD_DIM:, :] = pad_ref[h].astype(BF16)
    keep_ref[...] = send_ref[pl.ds(core * HALF, HALF)]
    give_ref[...] = send_ref[pl.ds((1 - core) * HALF, HALF)]


def halves(value):
    left = lax.broadcasted_iota(jnp.int32, value.shape, 1) < HEAD_DIM
    high = value.astype(BF16).astype(F32)
    return jnp.where(left, high, value - high)


def joined(value):
    return value + pltpu.roll(value, HEAD_DIM, 1)


def chip_kernel(keep_ref, got_ref, send_ref, pair_ref):
    parts, padded, _ = send_ref.shape
    part_rows = padded - PAD
    core = core_index()
    pair_ref[core] = keep_ref[...]
    pair_ref[1 - core] = got_ref[...]
    row = lax.broadcasted_iota(jnp.int32, (PAD, LANES), 0)
    left = lax.broadcasted_iota(jnp.int32, (PAD, LANES), 1) < HEAD_DIM
    for h in range(HALF):
        one = pair_ref[0, h, HEAD_DIM:, :].astype(F32)
        two = pair_ref[1, h, HEAD_DIM:, :].astype(F32)
        one_sum, two_sum = joined(one), joined(two)
        decay = jnp.exp(two_sum[0:1, :])
        state = decay * pair_ref[0, h, 0:HEAD_DIM, :].astype(F32) + pair_ref[
            1, h, 0:HEAD_DIM, :
        ].astype(F32)
        state = state.astype(BF16)
        exact = halves(jnp.where(row == 0, one_sum + two_sum, one_sum * decay))
        for k in range(HEAD_DIM // part_rows):
            at = k * part_rows
            own = pltpu.roll(jnp.where(left, one, 0.0), LANES - at, 1) if at else one
            pad = jnp.where(row < 4, jnp.where(left, own, two), jnp.where(row < 7, one, two))
            pad = jnp.where((row == 0) | ((row >= 10) & (row < 13)), exact, pad)
            part = h * (HEAD_DIM // part_rows) + k
            send_ref[part, 0:part_rows, :] = state[at : at + part_rows, :]
            send_ref[part, part_rows:, :] = pad.astype(BF16)


def enter_kernel(keep_ref, got_ref, back_ref, mine_ref, give_ref, pair_ref, enter_ref, pad_ref):
    parts, padded, _ = back_ref.shape
    part_rows = padded - PAD
    each = HEAD_DIM // part_rows
    core = core_index()
    pair_ref[core] = keep_ref[...]
    pair_ref[1 - core] = got_ref[...]
    few = lax.broadcasted_iota(jnp.int32, (8, LANES), 0) < CONV - 1
    for h in range(HALF):
        pad = back_ref[h * each, part_rows:, :]
        pad_ref[2 * h] = pad.astype(F32)
        pad_ref[2 * h + 1] = pair_ref[0, h, HEAD_DIM:, :].astype(F32)
    for h in range(HALF):
        last, mine = 2 * h, 2 * h + 1
        entering = jnp.concatenate(
            [back_ref[h * each + k, 0:part_rows, :] for k in range(each)], axis=0
        )
        values = silu(pad_ref[mine, 1:9, :] + pltpu.roll(pad_ref[last, 1:9, :], HEAD_DIM, 1))
        in_map = silu(pad_ref[mine, 4:12, :] + pad_ref[last, 7:15, :])
        edge = joined(pad_ref[mine, 8:16, :])
        edge = pltpu.roll(edge, 6, 0)
        scaled = jnp.where(few, values.astype(BF16).astype(F32) * edge, 0.0)
        added = dot(scaled, jnp.where(few, in_map, 0.0), ((0,), (0,)))[0:HEAD_DIM, :]
        decay = jnp.exp(joined(pad_ref[mine, 0:8, :])[0:1, :])
        after = decay * entering.astype(F32) + pair_ref[0, h, 0:HEAD_DIM, :].astype(F32) + added
        pad = back_ref[h * each, part_rows:, :]
        enter_ref[0, h, 0:HEAD_DIM, :] = entering
        enter_ref[1, h, 0:HEAD_DIM, :] = after.astype(BF16)
        enter_ref[0, h, HEAD_DIM:, :] = pad
        enter_ref[1, h, HEAD_DIM:, :] = pad
    mine_ref[...] = enter_ref[core]
    give_ref[...] = enter_ref[1 - core]


def silu(x):
    return x * jax.nn.sigmoid(x)


def scan_kernel(got_ref, *rest):
    back_ref, pad_ref = rest[-2:]
    parts, padded, _ = got_ref.shape
    part_rows = padded - PAD
    rows = slice(0, part_rows)
    offset = lax.axis_index("frames") // 2 * part_rows % HEAD_DIM
    few = lax.broadcasted_iota(jnp.int32, (8, LANES), 0) < CONV - 1
    left = lax.broadcasted_iota(jnp.int32, (8, LANES), 1) < HEAD_DIM
    pad_ref[0:PAD, :] = jnp.zeros((PAD, LANES), F32)
    pad_ref[(parts + 1) * PAD :, :] = jnp.zeros((8, LANES), F32)
    for d in range(parts):
        pad_ref[(d + 1) * PAD : (d + 2) * PAD, :] = got_ref[d, part_rows:, :].astype(F32)
    carry = jnp.zeros((part_rows, LANES), F32)
    for d in range(parts):
        back_ref[d, rows, :] = carry.astype(BF16)
        back_ref[d, part_rows:, :] = pad_ref[d * PAD : (d + 1) * PAD, :].astype(BF16)
        last, mine = d * PAD, (d + 1) * PAD
        decay = pad_ref[mine : mine + 1, :]
        decay = jnp.exp(decay + pltpu.roll(decay, HEAD_DIM, 1))
        from_tail = pltpu.roll(pad_ref[last + 1 : last + 9, :], HEAD_DIM, 1)
        if part_rows < HEAD_DIM:
            from_tail = pltpu.roll(jnp.where(left, from_tail, 0.0), (LANES - offset) % LANES, 1)
        values = silu(pad_ref[mine + 1 : mine + 9, :] + from_tail)
        in_map = silu(pad_ref[mine + 4 : mine + 12, :] + pad_ref[last + 7 : last + 15, :])
        edge = pad_ref[mine + 10 : mine + 18, :]
        edge = edge + pltpu.roll(edge, HEAD_DIM, 1)
        scaled = jnp.where(few, values.astype(BF16).astype(F32) * edge, 0.0)
        in_map = jnp.where(few, in_map, 0.0)
        added = dot(scaled, in_map, ((0,), (0,)))
        carry = decay * carry + (got_ref[d, rows, :].astype(F32) + added[rows, :])


def mixed_values(affinity, cum, shifted, values, skip, pair):
    q_pos = lax.broadcasted_iota(jnp.int32, (SPAN, SPAN), 0)
    s_pos = lax.broadcasted_iota(jnp.int32, (SPAN, SPAN), 1)
    lower = q_pos >= s_pos
    left = lax.broadcasted_iota(jnp.int32, (SPAN, LANES), 1) < HEAD_DIM
    zero = jnp.zeros((SPAN, LANES), BF16)
    mixing = []
    for h in (2 * pair, 2 * pair + 1):
        gap = cum[:, h : h + 1] - shifted[h : h + 1, :]
        mixing.append(jnp.where(lower, affinity * jnp.exp(gap), 0.0).astype(BF16))
    both = jnp.concatenate(mixing, axis=1)
    stacked = jnp.concatenate([jnp.where(left, values, zero), jnp.where(left, zero, values)], axis=0)
    return dot(both, stacked) + skip * values.astype(F32)


def later_kernel(layer, act_ref, cum_ref, shifted_ref, skip_ref, sel_ref, y_ref):
    skip = spread_row(skip_ref[layer : layer + 1, :], sel_ref[...])
    for b in range(1, act_ref.shape[0] // SPAN):
        r = slice(b * SPAN, (b + 1) * SPAN)
        maps = act_ref[r, INNER:]
        affinity = dot(maps[:, STATE:], maps[:, :STATE], ((1,), (1,)))
        cum, shifted = cum_ref[r, :], shifted_ref[:, r]
        for pair in range(HEADS // 2):
            cols = slice(pair * LANES, (pair + 1) * LANES)
            y_ref[(b - 1) * SPAN : b * SPAN, cols] = mixed_values(
                affinity, cum, shifted, act_ref[r, cols], skip[:, cols], pair
            )


def gate_kernel(layer, u_ref, w_ref, gate_ref):
    chunk = 256
    for c in range(0, INNER, chunk):
        cols = slice(c, c + chunk)
        gate_ref[:, cols] = silu(dot(u_ref[...], w_ref[layer, :, cols]).astype(BF16).astype(F32))


def finish_kernel(
    layer,
    gate_ref,
    later_ref,
    act_ref,
    own_ref,
    cum_ref,
    shifted_ref,
    edge_ref,
    state_ref,
    skip_ref,
    sel_ref,
    mine_ref,
    other_ref,
    resid_ref,
    wo_ref,
    gain_ref,
    mods_ref,
    *rest,
):
    hidden_ref, a_ref, first_ref, y_ref, normed_ref, enter_ref = rest[-6:]
    rows = gate_ref.shape[0]
    core = core_index()
    enter_ref[pl.ds(core * HALF, HALF)] = mine_ref[...]
    enter_ref[pl.ds((1 - core) * HALF, HALF)] = other_ref[...]
    start = (1 - core).astype(F32)
    sel = sel_ref[...]
    lane = lax.broadcasted_iota(jnp.int32, (SPAN, LANES), 1)
    left = lane < HEAD_DIM
    few = lax.broadcasted_iota(jnp.int32, (TAIL, LANES), 0) < CONV - 1
    nothing = jnp.zeros((TAIL - 8, LANES), F32)

    def fixed(cols, tail):
        total = jnp.concatenate([own_ref[:, cols] + start * tail[0:8, :], nothing], axis=0)
        first_ref[:, cols] = jnp.where(
            few, silu(total), act_ref[0:TAIL, cols].astype(F32)
        ).astype(BF16)

    for pair in range(HEADS // 2):
        pads = [
            enter_ref[h, HEAD_DIM:, :].astype(F32)
            for h in (2 * pair, 2 * pair + 1)
        ]
        tail = jnp.where(left[0:PAD], pltpu.roll(pads[0], HEAD_DIM, 1), pads[1])
        fixed(slice(pair * LANES, (pair + 1) * LANES), pltpu.roll(tail, PAD - 1, 0))
    common = enter_ref[0, HEAD_DIM:, :].astype(F32)
    fixed(slice(INNER, INNER + STATE), pltpu.roll(common, PAD - 7, 0))
    fixed(slice(INNER + STATE, INNER + 2 * STATE), pltpu.roll(common, PAD - 13, 0))

    def acts(b, cols):
        if b:
            return act_ref[b * SPAN : (b + 1) * SPAN, cols]
        return jnp.concatenate([first_ref[:, cols], act_ref[TAIL:SPAN, cols]], axis=0)

    first_tokens = lax.broadcasted_iota(jnp.int32, (TAIL, HEADS), 0) < CONV - 1
    early = spread(jnp.where(first_tokens, edge_ref[...], 0.0) * start, sel)
    early = (first_ref[:, 0:INNER].astype(F32) * early).astype(BF16)
    late = dot(first_ref[:, INNER : INNER + STATE], early, ((0,), (0,)))

    spans = rows // SPAN
    out_maps = [acts(b, slice(INNER + STATE, INNER + 2 * STATE)) for b in range(spans)]
    out_map = jnp.concatenate(out_maps, axis=0)
    before = jnp.zeros((1, HEADS), F32)
    scales = []
    for b in range(spans):
        cum = cum_ref[b * SPAN : (b + 1) * SPAN, :]
        scales.append(jnp.exp(cum + before))
        before = before + cum[SPAN - 1 : SPAN, :]
    wide = spread(jnp.concatenate(scales, axis=0), sel)
    chunk = 256
    for c in range(0, INNER, chunk):
        cols = slice(c, c + chunk)
        entering = jnp.concatenate(
            [enter_ref[h, 0:HEAD_DIM, :] for h in range(c // HEAD_DIM, (c + chunk) // HEAD_DIM)],
            axis=0,
        )
        y_ref[:, cols] = dot(out_map, entering, ((1,), (1,))) * wide[:, cols]
    decayed = jnp.ones((1, HEADS), F32)
    for b in range(1, spans):
        r = slice(b * SPAN, (b + 1) * SPAN)
        state = state_ref[(b - 1) * STATE : b * STATE, :] + spread_row(decayed, sel) * late
        cum = cum_ref[r, :]
        decayed = decayed * jnp.exp(cum[SPAN - 1 : SPAN, :])
        own = later_ref[(b - 1) * SPAN : b * SPAN, :]
        own = own + dot(out_maps[b], state.astype(BF16)) * spread(jnp.exp(cum), sel)
        y_ref[r, :] = (y_ref[r, :] + own) * gate_ref[r, :]

    skip = spread_row(skip_ref[layer : layer + 1, :], sel)
    r = slice(0, SPAN)
    affinity = dot(out_maps[0], acts(0, slice(INNER, INNER + STATE)), ((1,), (1,)))
    cum, shifted = cum_ref[r, :], shifted_ref[:, r]
    for pair in range(HEADS // 2):
        cols = slice(pair * LANES, (pair + 1) * LANES)
        y = mixed_values(affinity, cum, shifted, acts(0, cols), skip[:, cols], pair)
        y_ref[r, cols] = (y + y_ref[r, cols]) * gate_ref[r, cols]

    row = lax.broadcasted_iota(jnp.int32, (chunk, chunk), 0) // HEAD_DIM
    col = lax.broadcasted_iota(jnp.int32, (chunk, chunk), 1) // HEAD_DIM
    same = jnp.where(row == col, 1.0 / HEAD_DIM, 0.0).astype(BF16)
    for c in range(0, INNER, chunk):
        cols = slice(c, c + chunk)
        total = y_ref[:, cols]
        square = total * total
        high = square.astype(BF16)
        low = (square - high.astype(F32)).astype(BF16)
        mean = dot(high, same) + dot(low, same)
        gain = gain_ref[layer : layer + 1, cols]
        normed_ref[:, cols] = (total * lax.rsqrt(mean + HEAD_EPS) * gain).astype(BF16)
    hidden = resid_ref[...].astype(F32) + dot(normed_ref[...], wo_ref[layer])
    hidden_ref[...] = hidden
    a_ref[...] = rms_mod(hidden, mods_ref[layer, 2:3, :], mods_ref[layer, 3:4, :])


def partial_attention(q_ref, seen, kv, half, r, k_rows, done):
    left = lax.broadcasted_iota(jnp.int32, (half, LANES), 1) < HEAD_DIM
    one = jnp.ones((k_rows.stop - k_rows.start, LANES), BF16)
    zero = jnp.zeros((half, LANES), BF16)
    seen = jnp.concatenate([seen, seen], axis=0)
    together = 2
    for group in range(0, ATT_HEADS // 2, together):
        columns = [slice(p * LANES, (p + 1) * LANES) for p in range(group, group + together)]
        scores = []
        for cols in columns:
            query = q_ref[r, cols]
            sides = jnp.concatenate(
                [jnp.where(left, query, zero), jnp.where(left, zero, query)], axis=0
            )
            scores.append(dot(sides, kv[k_rows, cols], ((1,), (1,))) + seen)
        tops = [jnp.max(s, axis=-1, keepdims=True) for s in scores]
        weights = [jnp.exp(s - t).astype(BF16) for s, t in zip(scores, tops)]
        for cols, weight, top in zip(columns, weights, tops):
            values = kv[k_rows, ATTN + cols.start : ATTN + cols.stop]
            both = dot(weight, jnp.concatenate([values, one], axis=1))
            number = jnp.where(left, both[:half, :LANES], both[half:, :LANES])
            total = jnp.where(left, both[:half, LANES:], both[half:, LANES:])
            done(cols, number, total, jnp.where(left, top[:half], top[half:]))


def memory_kernel(
    layer, reach_ref, a_ref, wq_ref, wm_ref, q_ref, number_ref, total_ref, top_ref, seen_ref, kv_ref
):
    rows = a_ref.shape[0]
    half = rows // 2
    a = a_ref[...]
    tok_frame = rows // WINDOW
    key_frame = lax.broadcasted_iota(jnp.int32, (tok_frame, 2 * rows), 1) // tok_frame
    first = WINDOW - lax.axis_index("frames") * WINDOW
    for f in range(WINDOW):
        low = jnp.maximum(first, f + WINDOW - reach_ref[f])
        seen = (key_frame >= low) & (key_frame <= f + WINDOW)
        seen_ref[f * tok_frame : (f + 1) * tok_frame, :] = jnp.where(seen, 0.0, -1e30)
    q_ref[...] = (dot(a, wq_ref[layer]).astype(BF16).astype(F32) * HEAD_DIM**-0.5).astype(BF16)
    kv_ref[...] = dot(a, wm_ref[layer]).astype(BF16)
    for part in range(2):
        r = slice(part * half, (part + 1) * half)
        k_rows = slice(0, (part + 1) * half)

        def done(cols, number, total, top):
            number_ref[r, cols] = number
            total_ref[r, cols] = total
            top_ref[r, cols] = top

        seen = seen_ref[r, rows : rows + k_rows.stop]
        partial_attention(q_ref, seen, kv_ref, half, r, k_rows, done)


def attend_kernel(
    layer,
    last,
    q_ref,
    number_ref,
    total_ref,
    top_ref,
    seen_ref,
    prev_ref,
    wm_ref,
    merge_ref,
    hidden_ref,
    mods_ref,
    *rest,
):
    if last:
        resid_ref, kv_ref, out_ref = rest
    else:
        resid_ref, u_ref, tail_ref, kv_ref, out_ref = rest
    rows = q_ref.shape[0]
    half = rows // 2
    kv_ref[...] = dot(prev_ref[...], wm_ref[layer]).astype(BF16)
    for part in range(2):
        r = slice(part * half, (part + 1) * half)
        k_rows = slice(part * half, rows)

        def done(cols, number, total, top):
            top_own = top_ref[r, cols]
            highest = jnp.maximum(top, top_own)
            mine, own = jnp.exp(top - highest), jnp.exp(top_own - highest)
            number = number * mine + number_ref[r, cols] * own
            total = total * mine + total_ref[r, cols] * own
            out_ref[r, cols] = (number / total).astype(BF16)

        partial_attention(q_ref, seen_ref[r, k_rows], kv_ref, half, r, k_rows, done)
    resid = hidden_ref[...] + dot(out_ref[...], merge_ref[layer])
    resid_ref[...] = resid
    if not last:
        u = rms_mod(resid, mods_ref[layer + 1, 0:1, :], mods_ref[layer + 1, 1:2, :])
        u_ref[...] = u
        tail_ref[...] = u[rows - TAIL :]


WHOLE = pl.BlockSpec(memory_space=pltpu.VMEM)
SCALARS = pl.BlockSpec(memory_space=pltpu.SMEM)


def run(kernel, operands, outs, scratch=(), name=None, flops=0, scalars=()):
    moved = sum(o.size * o.dtype.itemsize for o in list(operands) + list(outs))
    return pl.pallas_call(
        kernel,
        in_specs=[SCALARS] * len(scalars) + [WHOLE] * len(operands),
        out_specs=[WHOLE] * len(outs),
        out_shape=list(outs),
        scratch_shapes=list(scratch),
        compiler_params=pltpu.CompilerParams(vmem_limit_bytes=20 * 1024 * 1024),
        cost_estimate=pl.CostEstimate(flops=flops, bytes_accessed=moved, transcendentals=0),
        name=name,
    )(*scalars, *operands)


def shape(dims, dtype):
    return jax.ShapeDtypeStruct(dims, dtype)


def swapped(value, axis):
    count = lax.axis_size(axis)
    return lax.ppermute(value, axis, [(i, i ^ 1) for i in range(count)])


def over_chips(value, axis):
    count = lax.axis_size(axis)
    groups = [list(range(core, count, 2)) for core in range(2)]
    return lax.all_to_all(value, axis, 0, 0, axis_index_groups=groups)


def from_behind(value, axis):
    count = lax.axis_size(axis)
    return lax.ppermute(value, axis, [(i, i + 1) for i in range(count - 1)])


def shards(
    latents,
    timestep,
    lookback,
    modulation,
    input_weight,
    step_weight,
    conv_weight,
    step_bias,
    decay_log,
    skip_gain,
    norm_gain,
    output_weight,
    query_weight,
    memory_weight,
    merge_weight,
):
    frames_dev, tok_frame, width = latents.shape
    rows = frames_dev * tok_frame
    spans = rows // SPAN
    parts = lax.axis_size("frames") // 2
    part_rows = HALF * HEAD_DIM // parts
    mixed = INNER + 2 * STATE
    step_weight = jnp.swapaxes(step_weight, 1, 2)
    step_bias = jnp.swapaxes(step_bias, 1, 2)
    resid = latents.reshape(rows, width)
    (sel,) = run(
        select_kernel, (), [shape((2 * HEADS, INNER), BF16)], name="select", flops=OPENING
    )
    u, tail, mods, bias = run(
        first_kernel,
        (sel, resid, modulation, step_bias),
        [
            shape((rows, width), BF16),
            shape((TAIL, width), BF16),
            shape((LAYERS,) + modulation.shape[2:], F32),
            shape((LAYERS, 8, HEADS), F32),
        ],
        name="first",
        flops=OPENING,
        scalars=(timestep,),
    )
    for layer in range(LAYERS):
        before = swapped(tail, "frames")
        act, own, cum, shifted, edge, state, keep, give = run(
            functools.partial(local_kernel, layer),
            (u, before, input_weight, step_weight, conv_weight, bias, decay_log, sel),
            [
                shape((rows, mixed), BF16),
                shape((8, mixed), F32),
                shape((rows, HEADS), F32),
                shape((HEADS, rows), F32),
                shape((TAIL, HEADS), F32),
                shape((max(spans - 1, 1) * STATE, INNER), F32),
                shape((HALF, BLOCK, LANES), BF16),
                shape((HALF, BLOCK, LANES), BF16),
            ],
            [
                pltpu.VMEM((2, rows + 2 * TAIL, 256), F32),
                pltpu.VMEM((8, mixed), F32),
                pltpu.VMEM((HEADS, PAD, LANES), F32),
                pltpu.VMEM((HEADS, BLOCK, LANES), BF16),
            ],
            name="local",
            flops=2 * rows * width * mixed,
        )
        got = swapped(give, "frames")
        (later,) = run(
            functools.partial(later_kernel, layer),
            (act, cum, shifted, skip_gain, sel),
            [shape((max(spans - 1, 1) * SPAN, INNER), F32)],
            name="later",
            flops=2 * rows * SPAN * INNER,
        )
        got, later = lax.optimization_barrier((got, later))
        (send,) = run(
            chip_kernel,
            (keep, got),
            [shape((parts, part_rows + PAD, LANES), BF16)],
            [pltpu.VMEM((2, HALF, BLOCK, LANES), BF16)],
            name="chip",
        )
        (back,) = run(
            scan_kernel,
            (over_chips(send, "frames"),)
            + (() if layer else (output_weight, norm_gain, query_weight, memory_weight, merge_weight)),
            [shape(send.shape, BF16)],
            [pltpu.VMEM(((parts + 1) * PAD + 8, LANES), F32)],
            name="scan",
        )
        mine, give = run(
            enter_kernel,
            (keep, got, over_chips(back, "frames")),
            [shape(keep.shape, BF16)] * 2,
            [
                pltpu.VMEM((2, HALF, BLOCK, LANES), BF16),
                pltpu.VMEM((2, HALF, BLOCK, LANES), BF16),
                pltpu.VMEM((HEADS, PAD, LANES), F32),
            ],
            name="enter",
        )
        give, u = lax.optimization_barrier((give, u))
        other = swapped(give, "frames")
        (gate,) = run(
            functools.partial(gate_kernel, layer),
            (u, input_weight),
            [shape((rows, INNER), F32)],
            name="gate",
            flops=2 * rows * width * INNER,
        )
        hidden, a = run(
            functools.partial(finish_kernel, layer),
            (gate, later, act, own, cum, shifted, edge, state, skip_gain, sel)
            + (mine, other, resid, output_weight, norm_gain, mods),
            [shape((rows, width), F32), shape((rows, width), BF16)],
            [
                pltpu.VMEM((TAIL, mixed), BF16),
                pltpu.VMEM((rows, INNER), F32),
                pltpu.VMEM((rows, INNER), BF16),
                pltpu.VMEM((HEADS, BLOCK, LANES), BF16),
            ],
            name="finish",
        )
        prev = from_behind(a, "frames")
        q, number, total, top, seen = run(
            functools.partial(memory_kernel, layer),
            (a, query_weight, memory_weight),
            [shape((rows, ATTN), BF16)]
            + [shape((rows, ATTN), F32)] * 3
            + [shape((rows, 2 * rows), F32)],
            [pltpu.VMEM((rows, 2 * ATTN), BF16)],
            name="memory",
            scalars=(lookback,),
            flops=2 * rows * width * 3 * ATTN,
        )
        last = layer == LAYERS - 1
        outs = [shape((rows, width), F32)]
        if not last:
            outs += [shape((rows, width), BF16), shape((TAIL, width), BF16)]
        result = run(
            functools.partial(attend_kernel, layer, last),
            (q, number, total, top, seen, prev, memory_weight, merge_weight, hidden, mods),
            outs,
            [pltpu.VMEM((rows, 2 * ATTN), BF16), pltpu.VMEM((rows, ATTN), BF16)],
            name="attend",
        )
        resid = result[0]
        if not last:
            u, tail = result[1:]
    return resid.reshape(latents.shape)


def solution(mesh):
    sharded = P(("groups", "frames"))
    return jax.shard_map(
        shards,
        mesh=mesh,
        in_specs=(P(("groups", "frames"), None, None), sharded, sharded) + (P(),) * 12,
        out_specs=P(("groups", "frames"), None, None),
        check_vma=False,
    )
```

```python
import functools

import jax
import jax.numpy as jnp
from jax import lax
from jax.experimental import pallas as pl
from jax.experimental.pallas import tpu as pltpu
from jax.sharding import PartitionSpec as P

HEADS = 16
HEAD_DIM = 64
STATE = 128
ATT_HEADS = 8
LAYERS = 2
CONV = 4
SPAN = 128
WINDOW = 8
EPS = 1e-06
HEAD_EPS = 1e-05
INNER = HEADS * HEAD_DIM
ATTN = ATT_HEADS * HEAD_DIM
PAD = 16
BLOCK = HEAD_DIM + PAD
HALF = HEADS // 2
LANES = 128
TAIL = 16
F32 = jnp.float32
OPENING = 4 * 10**9
BF16 = jnp.bfloat16


def dot(a, b, dims=((1,), (0,)), precision=None):
    return lax.dot_general(a, b, (dims, ((), ())), precision=precision, preferred_element_type=F32)


def rms_mod(x, shift, scale):
    normed = x * lax.rsqrt(jnp.mean(x * x, axis=-1, keepdims=True) + EPS)
    return (normed * (1.0 + scale) + shift).astype(BF16)


def split(per_head):
    high = per_head.astype(BF16)
    low = (per_head - high.astype(F32)).astype(BF16)
    return jnp.concatenate([high, low], axis=1)


def spread(per_head, sel):
    return dot(split(per_head), sel)


def spread_row(per_head, sel):
    return spread(jnp.broadcast_to(per_head, (16, HEADS)), sel)[0:1, :]


def select_kernel(sel_ref):
    row = lax.broadcasted_iota(jnp.int32, sel_ref.shape, 0) % HEADS
    head = lax.broadcasted_iota(jnp.int32, sel_ref.shape, 1) // HEAD_DIM
    sel_ref[...] = jnp.where(row == head, 1.0, 0.0).astype(BF16)


def first_kernel(
    step_ref,
    sel_ref,
    x_ref,
    all_mods_ref,
    all_bias_ref,
    u_ref,
    tail_ref,
    mods_ref,
    bias_ref,
):
    rows, width = u_ref.shape
    step = step_ref[0]
    for layer in range(LAYERS):
        mods_ref[layer] = all_mods_ref[layer, step].astype(F32)
    u = rms_mod(x_ref[...].astype(F32), mods_ref[0, 0:1, :], mods_ref[0, 1:2, :])
    u_ref[...] = u
    tail_ref[...] = u[rows - TAIL :]
    chosen = lax.broadcasted_iota(jnp.int32, (8, all_bias_ref.shape[-1]), 1) == step
    chosen = jnp.where(chosen, 1.0, 0.0).astype(F32)
    for layer in range(LAYERS):
        bias_ref[layer] = dot(
            chosen, all_bias_ref[layer], ((1,), (1,)), precision=lax.Precision.HIGHEST
        )


def core_index():
    return lax.axis_index("frames") % 2


def local_kernel(
    layer,
    u_ref,
    before_ref,
    w_ref,
    sw_ref,
    conv_ref,
    bias_ref,
    decay_ref,
    sel_ref,
    act_ref,
    own_ref,
    cum_ref,
    shifted_ref,
    edge_ref,
    state_ref,
    keep_ref,
    give_ref,
    ext_ref,
    tail_ref,
    pad_ref,
    send_ref,
    scaled_ref,
):
    rows = u_ref.shape[0]
    u = u_ref[...]
    sel = sel_ref[...]
    core = core_index()
    tail_rows = before_ref[...].astype(F32) * core.astype(F32)
    tail_rows = tail_rows.astype(BF16)
    raw = dot(u, sw_ref[layer], ((1,), (1,))) + bias_ref[layer, 0:1, :]
    step = jnp.maximum(raw, 0.0) + jnp.log1p(jnp.exp(-jnp.abs(raw)))
    log_decay = -jnp.exp(decay_ref[layer : layer + 1, :]) * step
    log_step = jnp.log(step)
    q_pos = lax.broadcasted_iota(jnp.int32, (SPAN, SPAN), 0)
    s_pos = lax.broadcasted_iota(jnp.int32, (SPAN, SPAN), 1)
    lower = jnp.where(q_pos >= s_pos, 1.0, 0.0).astype(F32)
    whole_tokens = lax.broadcasted_iota(jnp.int32, (SPAN, HEADS), 0) >= (CONV - 1) * (1 - core)
    ends, edges = [], []
    for b in range(rows // SPAN):
        r = slice(b * SPAN, (b + 1) * SPAN)
        cum = dot(lower, log_decay[r], precision=lax.Precision.HIGHEST)
        end = cum[SPAN - 1 : SPAN, :]
        cum_ref[r, :] = cum
        shifted_ref[:, r] = (cum - log_step[r]).T
        edge = jnp.exp(end - cum) * step[r]
        if b == 0:
            edge_ref[...] = edge[0:TAIL, :]
            edge = jnp.where(whole_tokens, edge, 0.0)
        ends.append(end)
        edges.append(edge)

    edges = split(jnp.concatenate(edges, axis=0))
    chunk = 256
    for slot in range(2):
        ext_ref[slot, TAIL + rows :, :] = jnp.zeros((TAIL, chunk), F32)
    for c in [INNER] + list(range(0, INNER, chunk)):
        w = w_ref[layer, :, INNER + c : INNER + c + chunk]
        slot = c // chunk % 2
        ext_ref[slot, 0:TAIL, :] = dot(tail_rows, w).astype(BF16).astype(F32)
        ext_ref[slot, TAIL : TAIL + rows, :] = dot(u, w).astype(BF16).astype(F32)
        total, after = None, None
        for k in range(CONV):
            start = TAIL - (CONV - 1) + k
            taps = conv_ref[layer, k : k + 1, c : c + chunk]
            term = taps * ext_ref[slot, start : start + rows, :]
            next_term = taps * ext_ref[slot, start + rows : start + rows + 8, :]
            total = term if total is None else total + term
            after = next_term if after is None else after + next_term
        act = (total * jax.nn.sigmoid(total)).astype(BF16)
        act_ref[:, c : c + chunk] = act
        if c < INNER:
            scale = dot(edges, sel_ref[:, c : c + chunk])
            scaled_ref[:, c : c + chunk] = (act.astype(F32) * scale).astype(BF16)
        own_ref[:, c : c + chunk] = total[0:8, :]
        tail_ref[:, c : c + chunk] = after

    state = None
    for b in range(rows // SPAN):
        r = slice(b * SPAN, (b + 1) * SPAN)
        in_map = act_ref[r, INNER : INNER + STATE]
        term = dot(in_map, scaled_ref[r, :], ((0,), (0,)))
        if state is None:
            state = term
        else:
            state_ref[(b - 1) * STATE : b * STATE, :] = state
            state = spread_row(jnp.exp(ends[b]), sel) * state + term

    for pair in range(HEADS // 2):
        turned = state[:, pair * LANES : (pair + 1) * LANES].T.astype(BF16)
        for side in range(2):
            send_ref[2 * pair + side, 0:HEAD_DIM, :] = turned[side * HEAD_DIM : (side + 1) * HEAD_DIM, :]
    over = sum(ends[1:], ends[0])
    edge = jnp.exp(over - cum_ref[0:8, :]) * step[0:8, :]
    left = lax.broadcasted_iota(jnp.int32, (8, LANES), 1) < HEAD_DIM
    few = CONV - 1
    for h in range(HEADS):
        cols = slice(h // 2 * LANES, (h // 2 + 1) * LANES)
        own, tail = own_ref[:, cols], tail_ref[:, cols]
        if h % 2:
            own = pltpu.roll(own, HEAD_DIM, 1)
        else:
            tail = pltpu.roll(tail, HEAD_DIM, 1)
        pad_ref[h, 0:1, :] = halves(jnp.broadcast_to(over[:, h : h + 1], (8, LANES)))[0:1, :]
        pad_ref[h, 1 : 1 + few, :] = jnp.where(left, own, tail)[0:few, :]
        pad_ref[h, 4 : 4 + few, :] = own_ref[0:few, INNER : INNER + STATE]
        pad_ref[h, 7 : 7 + few, :] = tail_ref[0:few, INNER : INNER + STATE]
        broad = jnp.broadcast_to(edge[:, h : h + 1], (8, LANES))
        pad_ref[h, 10 : 10 + few, :] = halves(broad)[0:few, :]
        pad_ref[h, 13 : 13 + few, :] = tail_ref[0:few, INNER + STATE :]
        send_ref[h, HEAD_DIM:, :] = pad_ref[h].astype(BF16)
    keep_ref[...] = send_ref[pl.ds(core * HALF, HALF)]
    give_ref[...] = send_ref[pl.ds((1 - core) * HALF, HALF)]


def halves(value):
    left = lax.broadcasted_iota(jnp.int32, value.shape, 1) < HEAD_DIM
    high = value.astype(BF16).astype(F32)
    return jnp.where(left, high, value - high)


def joined(value):
    return value + pltpu.roll(value, HEAD_DIM, 1)


def chip_kernel(keep_ref, got_ref, send_ref, pair_ref):
    parts, padded, _ = send_ref.shape
    part_rows = padded - PAD
    core = core_index()
    pair_ref[core] = keep_ref[...]
    pair_ref[1 - core] = got_ref[...]
    row = lax.broadcasted_iota(jnp.int32, (PAD, LANES), 0)
    left = lax.broadcasted_iota(jnp.int32, (PAD, LANES), 1) < HEAD_DIM
    for h in range(HALF):
        one = pair_ref[0, h, HEAD_DIM:, :].astype(F32)
        two = pair_ref[1, h, HEAD_DIM:, :].astype(F32)
        one_sum, two_sum = joined(one), joined(two)
        decay = jnp.exp(two_sum[0:1, :])
        state = decay * pair_ref[0, h, 0:HEAD_DIM, :].astype(F32) + pair_ref[
            1, h, 0:HEAD_DIM, :
        ].astype(F32)
        state = state.astype(BF16)
        exact = halves(jnp.where(row == 0, one_sum + two_sum, one_sum * decay))
        for k in range(HEAD_DIM // part_rows):
            at = k * part_rows
            own = pltpu.roll(jnp.where(left, one, 0.0), LANES - at, 1) if at else one
            pad = jnp.where(row < 4, jnp.where(left, own, two), jnp.where(row < 7, one, two))
            pad = jnp.where((row == 0) | ((row >= 10) & (row < 13)), exact, pad)
            part = h * (HEAD_DIM // part_rows) + k
            send_ref[part, 0:part_rows, :] = state[at : at + part_rows, :]
            send_ref[part, part_rows:, :] = pad.astype(BF16)


def enter_kernel(keep_ref, got_ref, back_ref, mine_ref, give_ref, pair_ref, enter_ref, pad_ref):
    parts, padded, _ = back_ref.shape
    part_rows = padded - PAD
    each = HEAD_DIM // part_rows
    core = core_index()
    pair_ref[core] = keep_ref[...]
    pair_ref[1 - core] = got_ref[...]
    few = lax.broadcasted_iota(jnp.int32, (8, LANES), 0) < CONV - 1
    for h in range(HALF):
        pad = back_ref[h * each, part_rows:, :]
        pad_ref[2 * h] = pad.astype(F32)
        pad_ref[2 * h + 1] = pair_ref[0, h, HEAD_DIM:, :].astype(F32)
    for h in range(HALF):
        last, mine = 2 * h, 2 * h + 1
        entering = jnp.concatenate(
            [back_ref[h * each + k, 0:part_rows, :] for k in range(each)], axis=0
        )
        values = silu(pad_ref[mine, 1:9, :] + pltpu.roll(pad_ref[last, 1:9, :], HEAD_DIM, 1))
        in_map = silu(pad_ref[mine, 4:12, :] + pad_ref[last, 7:15, :])
        edge = joined(pad_ref[mine, 8:16, :])
        edge = pltpu.roll(edge, 6, 0)
        scaled = jnp.where(few, values.astype(BF16).astype(F32) * edge, 0.0)
        added = dot(scaled, jnp.where(few, in_map, 0.0), ((0,), (0,)))[0:HEAD_DIM, :]
        decay = jnp.exp(joined(pad_ref[mine, 0:8, :])[0:1, :])
        after = decay * entering.astype(F32) + pair_ref[0, h, 0:HEAD_DIM, :].astype(F32) + added
        pad = back_ref[h * each, part_rows:, :]
        enter_ref[0, h, 0:HEAD_DIM, :] = entering
        enter_ref[1, h, 0:HEAD_DIM, :] = after.astype(BF16)
        enter_ref[0, h, HEAD_DIM:, :] = pad
        enter_ref[1, h, HEAD_DIM:, :] = pad
    mine_ref[...] = enter_ref[core]
    give_ref[...] = enter_ref[1 - core]


def silu(x):
    return x * jax.nn.sigmoid(x)


def scan_kernel(got_ref, *rest):
    back_ref, pad_ref = rest[-2:]
    parts, padded, _ = got_ref.shape
    part_rows = padded - PAD
    rows = slice(0, part_rows)
    offset = lax.axis_index("frames") // 2 * part_rows % HEAD_DIM
    few = lax.broadcasted_iota(jnp.int32, (8, LANES), 0) < CONV - 1
    left = lax.broadcasted_iota(jnp.int32, (8, LANES), 1) < HEAD_DIM
    pad_ref[0:PAD, :] = jnp.zeros((PAD, LANES), F32)
    pad_ref[(parts + 1) * PAD :, :] = jnp.zeros((8, LANES), F32)
    for d in range(parts):
        pad_ref[(d + 1) * PAD : (d + 2) * PAD, :] = got_ref[d, part_rows:, :].astype(F32)
    carry = jnp.zeros((part_rows, LANES), F32)
    for d in range(parts):
        back_ref[d, rows, :] = carry.astype(BF16)
        back_ref[d, part_rows:, :] = pad_ref[d * PAD : (d + 1) * PAD, :].astype(BF16)
        last, mine = d * PAD, (d + 1) * PAD
        decay = pad_ref[mine : mine + 1, :]
        decay = jnp.exp(decay + pltpu.roll(decay, HEAD_DIM, 1))
        from_tail = pltpu.roll(pad_ref[last + 1 : last + 9, :], HEAD_DIM, 1)
        if part_rows < HEAD_DIM:
            from_tail = pltpu.roll(jnp.where(left, from_tail, 0.0), (LANES - offset) % LANES, 1)
        values = silu(pad_ref[mine + 1 : mine + 9, :] + from_tail)
        in_map = silu(pad_ref[mine + 4 : mine + 12, :] + pad_ref[last + 7 : last + 15, :])
        edge = pad_ref[mine + 10 : mine + 18, :]
        edge = edge + pltpu.roll(edge, HEAD_DIM, 1)
        scaled = jnp.where(few, values.astype(BF16).astype(F32) * edge, 0.0)
        in_map = jnp.where(few, in_map, 0.0)
        added = dot(scaled, in_map, ((0,), (0,)))
        carry = decay * carry + (got_ref[d, rows, :].astype(F32) + added[rows, :])


def mixed_values(affinity, cum, shifted, values, skip, pair):
    q_pos = lax.broadcasted_iota(jnp.int32, (SPAN, SPAN), 0)
    s_pos = lax.broadcasted_iota(jnp.int32, (SPAN, SPAN), 1)
    lower = q_pos >= s_pos
    left = lax.broadcasted_iota(jnp.int32, (SPAN, LANES), 1) < HEAD_DIM
    zero = jnp.zeros((SPAN, LANES), BF16)
    mixing = []
    for h in (2 * pair, 2 * pair + 1):
        gap = cum[:, h : h + 1] - shifted[h : h + 1, :]
        mixing.append(jnp.where(lower, affinity * jnp.exp(gap), 0.0).astype(BF16))
    both = jnp.concatenate(mixing, axis=1)
    stacked = jnp.concatenate([jnp.where(left, values, zero), jnp.where(left, zero, values)], axis=0)
    return dot(both, stacked) + skip * values.astype(F32)


def later_kernel(layer, act_ref, cum_ref, shifted_ref, skip_ref, sel_ref, y_ref, decay_ref):
    skip = spread_row(skip_ref[layer : layer + 1, :], sel_ref[...])
    for b in range(1, act_ref.shape[0] // SPAN):
        r = slice(b * SPAN, (b + 1) * SPAN)
        maps = act_ref[r, INNER:]
        affinity = dot(maps[:, STATE:], maps[:, :STATE], ((1,), (1,)))
        cum, shifted = cum_ref[r, :], shifted_ref[:, r]
        decays = split(jnp.exp(cum))
        for c in range(0, INNER, 256):
            decay_ref[(b - 1) * SPAN : b * SPAN, c : c + 256] = dot(decays, sel_ref[:, c : c + 256])
        for pair in range(HEADS // 2):
            cols = slice(pair * LANES, (pair + 1) * LANES)
            y_ref[(b - 1) * SPAN : b * SPAN, cols] = mixed_values(
                affinity, cum, shifted, act_ref[r, cols], skip[:, cols], pair
            )


def gate_kernel(layer, u_ref, w_ref, cum_ref, sel_ref, gate_ref, wide_ref):
    chunk = 256
    before = jnp.zeros((1, HEADS), F32)
    scales = []
    for b in range(u_ref.shape[0] // SPAN):
        cum = cum_ref[b * SPAN : (b + 1) * SPAN, :]
        scales.append(jnp.exp(cum + before))
        before = before + cum[SPAN - 1 : SPAN, :]
    scales = split(jnp.concatenate(scales, axis=0))
    for c in range(0, INNER, chunk):
        cols = slice(c, c + chunk)
        wide_ref[:, cols] = dot(scales, sel_ref[:, cols])
        gate_ref[:, cols] = silu(dot(u_ref[...], w_ref[layer, :, cols]).astype(BF16).astype(F32))


def finish_kernel(
    layer,
    gate_ref,
    wide_ref,
    later_ref,
    decay_ref,
    act_ref,
    own_ref,
    cum_ref,
    shifted_ref,
    edge_ref,
    state_ref,
    skip_ref,
    sel_ref,
    mine_ref,
    other_ref,
    resid_ref,
    wo_ref,
    gain_ref,
    mods_ref,
    *rest,
):
    hidden_ref, a_ref, first_ref, y_ref, normed_ref, enter_ref = rest[-6:]
    rows = gate_ref.shape[0]
    core = core_index()
    enter_ref[pl.ds(core * HALF, HALF)] = mine_ref[...]
    enter_ref[pl.ds((1 - core) * HALF, HALF)] = other_ref[...]
    start = (1 - core).astype(F32)
    sel = sel_ref[...]
    lane = lax.broadcasted_iota(jnp.int32, (SPAN, LANES), 1)
    left = lane < HEAD_DIM
    few = lax.broadcasted_iota(jnp.int32, (TAIL, LANES), 0) < CONV - 1
    nothing = jnp.zeros((TAIL - 8, LANES), F32)

    def fixed(cols, tail):
        total = jnp.concatenate([own_ref[:, cols] + start * tail[0:8, :], nothing], axis=0)
        first_ref[:, cols] = jnp.where(
            few, silu(total), act_ref[0:TAIL, cols].astype(F32)
        ).astype(BF16)

    for pair in range(HEADS // 2):
        pads = [
            enter_ref[h, HEAD_DIM:, :].astype(F32)
            for h in (2 * pair, 2 * pair + 1)
        ]
        tail = jnp.where(left[0:PAD], pltpu.roll(pads[0], HEAD_DIM, 1), pads[1])
        fixed(slice(pair * LANES, (pair + 1) * LANES), pltpu.roll(tail, PAD - 1, 0))
    common = enter_ref[0, HEAD_DIM:, :].astype(F32)
    fixed(slice(INNER, INNER + STATE), pltpu.roll(common, PAD - 7, 0))
    fixed(slice(INNER + STATE, INNER + 2 * STATE), pltpu.roll(common, PAD - 13, 0))

    def acts(b, cols):
        if b:
            return act_ref[b * SPAN : (b + 1) * SPAN, cols]
        return jnp.concatenate([first_ref[:, cols], act_ref[TAIL:SPAN, cols]], axis=0)

    first_tokens = lax.broadcasted_iota(jnp.int32, (TAIL, HEADS), 0) < CONV - 1
    early_scale = split(jnp.where(first_tokens, edge_ref[...], 0.0) * start)
    early_map = first_ref[:, INNER : INNER + STATE]
    spans = rows // SPAN
    out_maps = [acts(b, slice(INNER + STATE, INNER + 2 * STATE)) for b in range(spans)]
    out_map = jnp.concatenate(out_maps, axis=0)
    decayed = [jnp.ones((1, INNER), F32)]
    for b in range(1, spans - 1):
        end = (b + 1) * SPAN - 1
        decayed.append(decayed[-1] * spread_row(jnp.exp(cum_ref[end : end + 1, :]), sel))
    chunk = 256
    for c in range(0, INNER, chunk):
        cols = slice(c, c + chunk)
        entering = jnp.concatenate(
            [enter_ref[h, 0:HEAD_DIM, :] for h in range(c // HEAD_DIM, (c + chunk) // HEAD_DIM)],
            axis=0,
        )
        y_ref[:, cols] = dot(out_map, entering, ((1,), (1,))) * wide_ref[:, cols]
    early = (first_ref[:, 0:INNER].astype(F32) * dot(early_scale, sel)).astype(BF16)
    late = dot(early_map, early, ((0,), (0,)))
    for b in range(1, spans):
        r, own = slice(b * SPAN, (b + 1) * SPAN), slice((b - 1) * SPAN, b * SPAN)
        state = late if b == 1 else decayed[b - 1] * late
        state = state_ref[(b - 1) * STATE : b * STATE, :] + state
        within = later_ref[own, :] + dot(out_maps[b], state.astype(BF16)) * decay_ref[own, :]
        y_ref[r, :] = (y_ref[r, :] + within) * gate_ref[r, :]

    skip = spread_row(skip_ref[layer : layer + 1, :], sel)
    r = slice(0, SPAN)
    affinity = dot(out_maps[0], acts(0, slice(INNER, INNER + STATE)), ((1,), (1,)))
    cum, shifted = cum_ref[r, :], shifted_ref[:, r]
    for pair in range(HEADS // 2):
        cols = slice(pair * LANES, (pair + 1) * LANES)
        y = mixed_values(affinity, cum, shifted, acts(0, cols), skip[:, cols], pair)
        y_ref[r, cols] = (y + y_ref[r, cols]) * gate_ref[r, cols]

    row = lax.broadcasted_iota(jnp.int32, (chunk, chunk), 0) // HEAD_DIM
    col = lax.broadcasted_iota(jnp.int32, (chunk, chunk), 1) // HEAD_DIM
    same = jnp.where(row == col, 1.0 / HEAD_DIM, 0.0).astype(BF16)
    for c in range(0, INNER, chunk):
        cols = slice(c, c + chunk)
        total = y_ref[:, cols]
        square = total * total
        high = square.astype(BF16)
        low = (square - high.astype(F32)).astype(BF16)
        mean = dot(high, same) + dot(low, same)
        gain = gain_ref[layer : layer + 1, cols]
        normed_ref[:, cols] = (total * lax.rsqrt(mean + HEAD_EPS) * gain).astype(BF16)
    hidden = resid_ref[...].astype(F32) + dot(normed_ref[...], wo_ref[layer])
    hidden_ref[...] = hidden
    a_ref[...] = rms_mod(hidden, mods_ref[layer, 2:3, :], mods_ref[layer, 3:4, :])


def partial_attention(q_ref, seen, kv, half, r, k_rows, done):
    left = lax.broadcasted_iota(jnp.int32, (half, LANES), 1) < HEAD_DIM
    one = jnp.ones((k_rows.stop - k_rows.start, LANES), BF16)
    zero = jnp.zeros((half, LANES), BF16)
    seen = jnp.concatenate([seen, seen], axis=0)
    together = 4
    for group in range(0, ATT_HEADS // 2, together):
        columns = [slice(p * LANES, (p + 1) * LANES) for p in range(group, group + together)]
        scores = []
        for cols in columns:
            query = q_ref[r, cols]
            sides = jnp.concatenate(
                [jnp.where(left, query, zero), jnp.where(left, zero, query)], axis=0
            )
            scores.append(dot(sides, kv[k_rows, cols], ((1,), (1,))) + seen)
        tops = [jnp.max(s, axis=-1, keepdims=True) for s in scores]
        weights = [jnp.exp(s - t).astype(BF16) for s, t in zip(scores, tops)]
        for cols, weight, top in zip(columns, weights, tops):
            values = kv[k_rows, ATTN + cols.start : ATTN + cols.stop]
            both = dot(weight, jnp.concatenate([values, one], axis=1))
            number = jnp.where(left, both[:half, :LANES], both[half:, :LANES])
            total = jnp.where(left, both[:half, LANES:], both[half:, LANES:])
            done(cols, number, total, jnp.where(left, top[:half], top[half:]))


def memory_kernel(
    layer, reach_ref, a_ref, wq_ref, wm_ref, q_ref, number_ref, total_ref, top_ref, seen_ref, kv_ref
):
    rows = a_ref.shape[0]
    half = rows // 2
    a = a_ref[...]
    tok_frame = rows // WINDOW
    key_frame = lax.broadcasted_iota(jnp.int32, (tok_frame, 2 * rows), 1) // tok_frame
    first = WINDOW - lax.axis_index("frames") * WINDOW
    for f in range(WINDOW):
        low = jnp.maximum(first, f + WINDOW - reach_ref[f])
        seen = (key_frame >= low) & (key_frame <= f + WINDOW)
        seen_ref[f * tok_frame : (f + 1) * tok_frame, :] = jnp.where(seen, 0.0, -1e30)
    q_ref[...] = (dot(a, wq_ref[layer]).astype(BF16).astype(F32) * HEAD_DIM**-0.5).astype(BF16)
    kv_ref[...] = dot(a, wm_ref[layer]).astype(BF16)
    for part in range(2):
        r = slice(part * half, (part + 1) * half)
        k_rows = slice(0, (part + 1) * half)

        def done(cols, number, total, top):
            number_ref[r, cols] = number
            total_ref[r, cols] = total
            top_ref[r, cols] = top

        seen = seen_ref[r, rows : rows + k_rows.stop]
        partial_attention(q_ref, seen, kv_ref, half, r, k_rows, done)


def attend_kernel(
    layer,
    last,
    q_ref,
    number_ref,
    total_ref,
    top_ref,
    seen_ref,
    prev_ref,
    wm_ref,
    merge_ref,
    hidden_ref,
    mods_ref,
    *rest,
):
    if last:
        resid_ref, kv_ref, out_ref = rest
    else:
        resid_ref, u_ref, tail_ref, kv_ref, out_ref = rest
    rows = q_ref.shape[0]
    half = rows // 2
    kv_ref[...] = dot(prev_ref[...], wm_ref[layer]).astype(BF16)
    for part in range(2):
        r = slice(part * half, (part + 1) * half)
        k_rows = slice(part * half, rows)

        def done(cols, number, total, top):
            top_own = top_ref[r, cols]
            highest = jnp.maximum(top, top_own)
            mine, own = jnp.exp(top - highest), jnp.exp(top_own - highest)
            number = number * mine + number_ref[r, cols] * own
            total = total * mine + total_ref[r, cols] * own
            out_ref[r, cols] = (number / total).astype(BF16)

        partial_attention(q_ref, seen_ref[r, k_rows], kv_ref, half, r, k_rows, done)
    resid = hidden_ref[...] + dot(out_ref[...], merge_ref[layer])
    resid_ref[...] = resid
    if not last:
        u = rms_mod(resid, mods_ref[layer + 1, 0:1, :], mods_ref[layer + 1, 1:2, :])
        u_ref[...] = u
        tail_ref[...] = u[rows - TAIL :]


WHOLE = pl.BlockSpec(memory_space=pltpu.VMEM)
SCALARS = pl.BlockSpec(memory_space=pltpu.SMEM)


def run(kernel, operands, outs, scratch=(), name=None, flops=0, scalars=()):
    moved = sum(o.size * o.dtype.itemsize for o in list(operands) + list(outs))
    return pl.pallas_call(
        kernel,
        in_specs=[SCALARS] * len(scalars) + [WHOLE] * len(operands),
        out_specs=[WHOLE] * len(outs),
        out_shape=list(outs),
        scratch_shapes=list(scratch),
        compiler_params=pltpu.CompilerParams(vmem_limit_bytes=20 * 1024 * 1024),
        cost_estimate=pl.CostEstimate(flops=flops, bytes_accessed=moved, transcendentals=0),
        name=name,
    )(*scalars, *operands)


def shape(dims, dtype):
    return jax.ShapeDtypeStruct(dims, dtype)


def swapped(value, axis):
    count = lax.axis_size(axis)
    return lax.ppermute(value, axis, [(i, i ^ 1) for i in range(count)])


def over_chips(value, axis):
    count = lax.axis_size(axis)
    groups = [list(range(core, count, 2)) for core in range(2)]
    return lax.all_to_all(value, axis, 0, 0, axis_index_groups=groups)


def from_behind(value, axis):
    count = lax.axis_size(axis)
    return lax.ppermute(value, axis, [(i, i + 1) for i in range(count - 1)])


def shards(
    latents,
    timestep,
    lookback,
    modulation,
    input_weight,
    step_weight,
    conv_weight,
    step_bias,
    decay_log,
    skip_gain,
    norm_gain,
    output_weight,
    query_weight,
    memory_weight,
    merge_weight,
):
    frames_dev, tok_frame, width = latents.shape
    rows = frames_dev * tok_frame
    spans = rows // SPAN
    parts = lax.axis_size("frames") // 2
    part_rows = HALF * HEAD_DIM // parts
    mixed = INNER + 2 * STATE
    step_weight = jnp.swapaxes(step_weight, 1, 2)
    step_bias = jnp.swapaxes(step_bias, 1, 2)
    resid = latents.reshape(rows, width)
    (sel,) = run(
        select_kernel, (), [shape((2 * HEADS, INNER), BF16)], name="select", flops=OPENING
    )
    u, tail, mods, bias = run(
        first_kernel,
        (sel, resid, modulation, step_bias),
        [
            shape((rows, width), BF16),
            shape((TAIL, width), BF16),
            shape((LAYERS,) + modulation.shape[2:], F32),
            shape((LAYERS, 8, HEADS), F32),
        ],
        name="first",
        flops=OPENING,
        scalars=(timestep,),
    )
    for layer in range(LAYERS):
        before = swapped(tail, "frames")
        act, own, cum, shifted, edge, state, keep, give = run(
            functools.partial(local_kernel, layer),
            (u, before, input_weight, step_weight, conv_weight, bias, decay_log, sel),
            [
                shape((rows, mixed), BF16),
                shape((8, mixed), F32),
                shape((rows, HEADS), F32),
                shape((HEADS, rows), F32),
                shape((TAIL, HEADS), F32),
                shape((max(spans - 1, 1) * STATE, INNER), F32),
                shape((HALF, BLOCK, LANES), BF16),
                shape((HALF, BLOCK, LANES), BF16),
            ],
            [
                pltpu.VMEM((2, rows + 2 * TAIL, 256), F32),
                pltpu.VMEM((8, mixed), F32),
                pltpu.VMEM((HEADS, PAD, LANES), F32),
                pltpu.VMEM((HEADS, BLOCK, LANES), BF16),
                pltpu.VMEM((rows, INNER), BF16),
            ],
            name="local",
            flops=2 * rows * width * mixed,
        )
        got = swapped(give, "frames")
        later, decays = run(
            functools.partial(later_kernel, layer),
            (act, cum, shifted, skip_gain, sel),
            [shape((max(spans - 1, 1) * SPAN, INNER), F32)] * 2,
            name="later",
            flops=2 * rows * SPAN * INNER,
        )
        got, later, decays = lax.optimization_barrier((got, later, decays))
        (send,) = run(
            chip_kernel,
            (keep, got),
            [shape((parts, part_rows + PAD, LANES), BF16)],
            [pltpu.VMEM((2, HALF, BLOCK, LANES), BF16)],
            name="chip",
        )
        (back,) = run(
            scan_kernel,
            (over_chips(send, "frames"),)
            + (() if layer else (output_weight, norm_gain, query_weight, memory_weight, merge_weight)),
            [shape(send.shape, BF16)],
            [pltpu.VMEM(((parts + 1) * PAD + 8, LANES), F32)],
            name="scan",
        )
        mine, give = run(
            enter_kernel,
            (keep, got, over_chips(back, "frames")),
            [shape(keep.shape, BF16)] * 2,
            [
                pltpu.VMEM((2, HALF, BLOCK, LANES), BF16),
                pltpu.VMEM((2, HALF, BLOCK, LANES), BF16),
                pltpu.VMEM((HEADS, PAD, LANES), F32),
            ],
            name="enter",
        )
        give, u = lax.optimization_barrier((give, u))
        other = swapped(give, "frames")
        gate, wide = run(
            functools.partial(gate_kernel, layer),
            (u, input_weight, cum, sel),
            [shape((rows, INNER), F32)] * 2,
            name="gate",
            flops=2 * rows * width * INNER,
        )
        hidden, a = run(
            functools.partial(finish_kernel, layer),
            (gate, wide, later, decays, act, own, cum, shifted, edge, state, skip_gain, sel)
            + (mine, other, resid, output_weight, norm_gain, mods),
            [shape((rows, width), F32), shape((rows, width), BF16)],
            [
                pltpu.VMEM((TAIL, mixed), BF16),
                pltpu.VMEM((rows, INNER), F32),
                pltpu.VMEM((rows, INNER), BF16),
                pltpu.VMEM((HEADS, BLOCK, LANES), BF16),
            ],
            name="finish",
        )
        prev = from_behind(a, "frames")
        q, number, total, top, seen = run(
            functools.partial(memory_kernel, layer),
            (a, query_weight, memory_weight),
            [shape((rows, ATTN), BF16)]
            + [shape((rows, ATTN), F32)] * 3
            + [shape((rows, 2 * rows), F32)],
            [pltpu.VMEM((rows, 2 * ATTN), BF16)],
            name="memory",
            scalars=(lookback,),
            flops=2 * rows * width * 3 * ATTN,
        )
        last = layer == LAYERS - 1
        outs = [shape((rows, width), F32)]
        if not last:
            outs += [shape((rows, width), BF16), shape((TAIL, width), BF16)]
        result = run(
            functools.partial(attend_kernel, layer, last),
            (q, number, total, top, seen, prev, memory_weight, merge_weight, hidden, mods),
            outs,
            [pltpu.VMEM((rows, 2 * ATTN), BF16), pltpu.VMEM((rows, ATTN), BF16)],
            name="attend",
        )
        resid = result[0]
        if not last:
            u, tail = result[1:]
    return resid.reshape(latents.shape)


def solution(mesh):
    sharded = P(("groups", "frames"))
    return jax.shard_map(
        shards,
        mesh=mesh,
        in_specs=(P(("groups", "frames"), None, None), sharded, sharded) + (P(),) * 12,
        out_specs=P(("groups", "frames"), None, None),
        check_vma=False,
    )
```

```python
import functools

import jax
import jax.numpy as jnp
from jax import lax
from jax.experimental import pallas as pl
from jax.experimental.pallas import tpu as pltpu
from jax.sharding import PartitionSpec as P

HEADS = 16
HEAD_DIM = 64
STATE = 128
ATT_HEADS = 8
LAYERS = 2
CONV = 4
SPAN = 128
WINDOW = 8
EPS = 1e-06
HEAD_EPS = 1e-05
INNER = HEADS * HEAD_DIM
ATTN = ATT_HEADS * HEAD_DIM
PAD = 16
BLOCK = HEAD_DIM + PAD
HALF = HEADS // 2
LANES = 128
TAIL = 16
F32 = jnp.float32
OPENING = 4 * 10**9
BF16 = jnp.bfloat16


def dot(a, b, dims=((1,), (0,)), precision=None):
    return lax.dot_general(a, b, (dims, ((), ())), precision=precision, preferred_element_type=F32)


def rms_mod(x, shift, scale):
    normed = x * lax.rsqrt(jnp.mean(x * x, axis=-1, keepdims=True) + EPS)
    return (normed * (1.0 + scale) + shift).astype(BF16)


def split(per_head):
    high = per_head.astype(BF16)
    low = (per_head - high.astype(F32)).astype(BF16)
    return jnp.concatenate([high, low], axis=1)


def spread(per_head, sel):
    return dot(split(per_head), sel)


def spread_row(per_head, sel):
    return spread(jnp.broadcast_to(per_head, (16, HEADS)), sel)[0:1, :]


def select_kernel(sel_ref):
    row = lax.broadcasted_iota(jnp.int32, sel_ref.shape, 0) % HEADS
    head = lax.broadcasted_iota(jnp.int32, sel_ref.shape, 1) // HEAD_DIM
    sel_ref[...] = jnp.where(row == head, 1.0, 0.0).astype(BF16)


def first_kernel(
    step_ref,
    sel_ref,
    x_ref,
    all_mods_ref,
    all_bias_ref,
    u_ref,
    tail_ref,
    mods_ref,
    bias_ref,
):
    rows, width = u_ref.shape
    step = step_ref[0]
    for layer in range(LAYERS):
        mods_ref[layer] = all_mods_ref[layer, step].astype(F32)
    u = rms_mod(x_ref[...].astype(F32), mods_ref[0, 0:1, :], mods_ref[0, 1:2, :])
    u_ref[...] = u
    tail_ref[...] = u[rows - TAIL :]
    chosen = lax.broadcasted_iota(jnp.int32, (8, all_bias_ref.shape[-1]), 1) == step
    chosen = jnp.where(chosen, 1.0, 0.0).astype(F32)
    for layer in range(LAYERS):
        bias_ref[layer] = dot(
            chosen, all_bias_ref[layer], ((1,), (1,)), precision=lax.Precision.HIGHEST
        )


def core_index():
    return lax.axis_index("frames") % 2


def local_kernel(
    layer,
    u_ref,
    before_ref,
    w_ref,
    sw_ref,
    conv_ref,
    bias_ref,
    decay_ref,
    sel_ref,
    act_ref,
    own_ref,
    cum_ref,
    shifted_ref,
    edge_ref,
    state_ref,
    keep_ref,
    give_ref,
    ext_ref,
    tail_ref,
    pad_ref,
    send_ref,
    scaled_ref,
):
    rows = u_ref.shape[0]
    u = u_ref[...]
    sel = sel_ref[...]
    core = core_index()
    tail_rows = before_ref[...].astype(F32) * core.astype(F32)
    with_tail = jnp.concatenate([tail_rows.astype(BF16), u], axis=0)
    raw = dot(u, sw_ref[layer], ((1,), (1,))) + bias_ref[layer, 0:1, :]
    step = jnp.maximum(raw, 0.0) + jnp.log1p(jnp.exp(-jnp.abs(raw)))
    log_decay = -jnp.exp(decay_ref[layer : layer + 1, :]) * step
    log_step = jnp.log(step)
    q_pos = lax.broadcasted_iota(jnp.int32, (SPAN, SPAN), 0)
    s_pos = lax.broadcasted_iota(jnp.int32, (SPAN, SPAN), 1)
    lower = jnp.where(q_pos >= s_pos, 1.0, 0.0).astype(F32)
    whole_tokens = lax.broadcasted_iota(jnp.int32, (SPAN, HEADS), 0) >= (CONV - 1) * (1 - core)
    ends, edges = [], []
    for b in range(rows // SPAN):
        r = slice(b * SPAN, (b + 1) * SPAN)
        cum = dot(lower, log_decay[r], precision=lax.Precision.HIGHEST)
        end = cum[SPAN - 1 : SPAN, :]
        cum_ref[r, :] = cum
        shifted_ref[:, r] = (cum - log_step[r]).T
        edge = jnp.exp(end - cum) * step[r]
        if b == 0:
            edge_ref[...] = edge[0:TAIL, :]
            edge = jnp.where(whole_tokens, edge, 0.0)
        ends.append(end)
        edges.append(edge)

    edges = split(jnp.concatenate(edges, axis=0))
    chunk = 256
    for slot in range(2):
        ext_ref[slot, TAIL + rows :, :] = jnp.zeros((TAIL, chunk), F32)
    for c in [INNER] + list(range(0, INNER, chunk)):
        w = w_ref[layer, :, INNER + c : INNER + c + chunk]
        slot = c // chunk % 2
        ext_ref[slot, 0 : TAIL + rows, :] = dot(with_tail, w).astype(BF16).astype(F32)
        total, after = None, None
        for k in range(CONV):
            start = TAIL - (CONV - 1) + k
            taps = conv_ref[layer, k : k + 1, c : c + chunk]
            term = taps * ext_ref[slot, start : start + rows, :]
            next_term = taps * ext_ref[slot, start + rows : start + rows + 8, :]
            total = term if total is None else total + term
            after = next_term if after is None else after + next_term
        act = (total * jax.nn.sigmoid(total)).astype(BF16)
        act_ref[:, c : c + chunk] = act
        if c < INNER:
            scale = dot(edges, sel_ref[:, c : c + chunk])
            scaled_ref[:, c : c + chunk] = (act.astype(F32) * scale).astype(BF16)
        own_ref[:, c : c + chunk] = total[0:8, :]
        tail_ref[:, c : c + chunk] = after

    state = None
    for b in range(rows // SPAN):
        r = slice(b * SPAN, (b + 1) * SPAN)
        in_map = act_ref[r, INNER : INNER + STATE]
        term = dot(in_map, scaled_ref[r, :], ((0,), (0,)))
        if state is None:
            state = term
        else:
            state_ref[(b - 1) * STATE : b * STATE, :] = state
            state = spread_row(jnp.exp(ends[b]), sel) * state + term

    for pair in range(HEADS // 2):
        turned = state[:, pair * LANES : (pair + 1) * LANES].T.astype(BF16)
        for side in range(2):
            send_ref[2 * pair + side, 0:HEAD_DIM, :] = turned[side * HEAD_DIM : (side + 1) * HEAD_DIM, :]
    over = sum(ends[1:], ends[0])
    edge = jnp.exp(over - cum_ref[0:8, :]) * step[0:8, :]
    left = lax.broadcasted_iota(jnp.int32, (8, LANES), 1) < HEAD_DIM
    few = CONV - 1
    for h in range(HEADS):
        cols = slice(h // 2 * LANES, (h // 2 + 1) * LANES)
        own, tail = own_ref[:, cols], tail_ref[:, cols]
        if h % 2:
            own = pltpu.roll(own, HEAD_DIM, 1)
        else:
            tail = pltpu.roll(tail, HEAD_DIM, 1)
        pad_ref[h, 0:1, :] = halves(jnp.broadcast_to(over[:, h : h + 1], (8, LANES)))[0:1, :]
        pad_ref[h, 1 : 1 + few, :] = jnp.where(left, own, tail)[0:few, :]
        pad_ref[h, 4 : 4 + few, :] = own_ref[0:few, INNER : INNER + STATE]
        pad_ref[h, 7 : 7 + few, :] = tail_ref[0:few, INNER : INNER + STATE]
        broad = jnp.broadcast_to(edge[:, h : h + 1], (8, LANES))
        pad_ref[h, 10 : 10 + few, :] = halves(broad)[0:few, :]
        pad_ref[h, 13 : 13 + few, :] = tail_ref[0:few, INNER + STATE :]
        send_ref[h, HEAD_DIM:, :] = pad_ref[h].astype(BF16)
    keep_ref[...] = send_ref[pl.ds(core * HALF, HALF)]
    give_ref[...] = send_ref[pl.ds((1 - core) * HALF, HALF)]


def halves(value):
    left = lax.broadcasted_iota(jnp.int32, value.shape, 1) < HEAD_DIM
    high = value.astype(BF16).astype(F32)
    return jnp.where(left, high, value - high)


def joined(value):
    return value + pltpu.roll(value, HEAD_DIM, 1)


def chip_kernel(keep_ref, got_ref, send_ref, pair_ref):
    parts, padded, _ = send_ref.shape
    part_rows = padded - PAD
    core = core_index()
    pair_ref[core] = keep_ref[...]
    pair_ref[1 - core] = got_ref[...]
    row = lax.broadcasted_iota(jnp.int32, (PAD, LANES), 0)
    left = lax.broadcasted_iota(jnp.int32, (PAD, LANES), 1) < HEAD_DIM
    for h in range(HALF):
        one = pair_ref[0, h, HEAD_DIM:, :].astype(F32)
        two = pair_ref[1, h, HEAD_DIM:, :].astype(F32)
        one_sum, two_sum = joined(one), joined(two)
        decay = jnp.exp(two_sum[0:1, :])
        state = decay * pair_ref[0, h, 0:HEAD_DIM, :].astype(F32) + pair_ref[
            1, h, 0:HEAD_DIM, :
        ].astype(F32)
        state = state.astype(BF16)
        exact = halves(jnp.where(row == 0, one_sum + two_sum, one_sum * decay))
        for k in range(HEAD_DIM // part_rows):
            at = k * part_rows
            own = pltpu.roll(jnp.where(left, one, 0.0), LANES - at, 1) if at else one
            pad = jnp.where(row < 4, jnp.where(left, own, two), jnp.where(row < 7, one, two))
            pad = jnp.where((row == 0) | ((row >= 10) & (row < 13)), exact, pad)
            part = h * (HEAD_DIM // part_rows) + k
            send_ref[part, 0:part_rows, :] = state[at : at + part_rows, :]
            send_ref[part, part_rows:, :] = pad.astype(BF16)


def enter_kernel(keep_ref, got_ref, back_ref, mine_ref, give_ref, pair_ref, enter_ref, pad_ref):
    parts, padded, _ = back_ref.shape
    part_rows = padded - PAD
    each = HEAD_DIM // part_rows
    core = core_index()
    pair_ref[core] = keep_ref[...]
    pair_ref[1 - core] = got_ref[...]
    few = lax.broadcasted_iota(jnp.int32, (8, LANES), 0) < CONV - 1
    for h in range(HALF):
        pad = back_ref[h * each, part_rows:, :]
        pad_ref[2 * h] = pad.astype(F32)
        pad_ref[2 * h + 1] = pair_ref[0, h, HEAD_DIM:, :].astype(F32)
    for h in range(HALF):
        last, mine = 2 * h, 2 * h + 1
        entering = jnp.concatenate(
            [back_ref[h * each + k, 0:part_rows, :] for k in range(each)], axis=0
        )
        values = silu(pad_ref[mine, 1:9, :] + pltpu.roll(pad_ref[last, 1:9, :], HEAD_DIM, 1))
        in_map = silu(pad_ref[mine, 4:12, :] + pad_ref[last, 7:15, :])
        edge = joined(pad_ref[mine, 8:16, :])
        edge = pltpu.roll(edge, 6, 0)
        scaled = jnp.where(few, values.astype(BF16).astype(F32) * edge, 0.0)
        added = dot(scaled, jnp.where(few, in_map, 0.0), ((0,), (0,)))[0:HEAD_DIM, :]
        decay = jnp.exp(joined(pad_ref[mine, 0:8, :])[0:1, :])
        after = decay * entering.astype(F32) + pair_ref[0, h, 0:HEAD_DIM, :].astype(F32) + added
        pad = back_ref[h * each, part_rows:, :]
        enter_ref[0, h, 0:HEAD_DIM, :] = entering
        enter_ref[1, h, 0:HEAD_DIM, :] = after.astype(BF16)
        enter_ref[0, h, HEAD_DIM:, :] = pad
        enter_ref[1, h, HEAD_DIM:, :] = pad
    mine_ref[...] = enter_ref[core]
    give_ref[...] = enter_ref[1 - core]


def silu(x):
    return x * jax.nn.sigmoid(x)


def scan_kernel(got_ref, *rest):
    back_ref, pad_ref = rest[-2:]
    parts, padded, _ = got_ref.shape
    part_rows = padded - PAD
    rows = slice(0, part_rows)
    offset = lax.axis_index("frames") // 2 * part_rows % HEAD_DIM
    few = lax.broadcasted_iota(jnp.int32, (8, LANES), 0) < CONV - 1
    left = lax.broadcasted_iota(jnp.int32, (8, LANES), 1) < HEAD_DIM
    pad_ref[0:PAD, :] = jnp.zeros((PAD, LANES), F32)
    pad_ref[(parts + 1) * PAD :, :] = jnp.zeros((8, LANES), F32)
    for d in range(parts):
        pad_ref[(d + 1) * PAD : (d + 2) * PAD, :] = got_ref[d, part_rows:, :].astype(F32)
    carry = jnp.zeros((part_rows, LANES), F32)
    for d in range(parts):
        back_ref[d, rows, :] = carry.astype(BF16)
        back_ref[d, part_rows:, :] = pad_ref[d * PAD : (d + 1) * PAD, :].astype(BF16)
        last, mine = d * PAD, (d + 1) * PAD
        decay = pad_ref[mine : mine + 1, :]
        decay = jnp.exp(decay + pltpu.roll(decay, HEAD_DIM, 1))
        from_tail = pltpu.roll(pad_ref[last + 1 : last + 9, :], HEAD_DIM, 1)
        if part_rows < HEAD_DIM:
            from_tail = pltpu.roll(jnp.where(left, from_tail, 0.0), (LANES - offset) % LANES, 1)
        values = silu(pad_ref[mine + 1 : mine + 9, :] + from_tail)
        in_map = silu(pad_ref[mine + 4 : mine + 12, :] + pad_ref[last + 7 : last + 15, :])
        edge = pad_ref[mine + 10 : mine + 18, :]
        edge = edge + pltpu.roll(edge, HEAD_DIM, 1)
        scaled = jnp.where(few, values.astype(BF16).astype(F32) * edge, 0.0)
        in_map = jnp.where(few, in_map, 0.0)
        added = dot(scaled, in_map, ((0,), (0,)))
        carry = decay * carry + (got_ref[d, rows, :].astype(F32) + added[rows, :])


def mixed_values(affinity, cum, shifted, values, skip, pair):
    q_pos = lax.broadcasted_iota(jnp.int32, (SPAN, SPAN), 0)
    s_pos = lax.broadcasted_iota(jnp.int32, (SPAN, SPAN), 1)
    lower = q_pos >= s_pos
    left = lax.broadcasted_iota(jnp.int32, (SPAN, LANES), 1) < HEAD_DIM
    zero = jnp.zeros((SPAN, LANES), BF16)
    mixing = []
    for h in (2 * pair, 2 * pair + 1):
        gap = cum[:, h : h + 1] - shifted[h : h + 1, :]
        mixing.append(jnp.where(lower, affinity * jnp.exp(gap), 0.0).astype(BF16))
    both = jnp.concatenate(mixing, axis=1)
    stacked = jnp.concatenate([jnp.where(left, values, zero), jnp.where(left, zero, values)], axis=0)
    return dot(both, stacked) + skip * values.astype(F32)


def later_kernel(layer, act_ref, cum_ref, shifted_ref, skip_ref, sel_ref, y_ref, decay_ref):
    skip = spread_row(skip_ref[layer : layer + 1, :], sel_ref[...])
    for b in range(1, act_ref.shape[0] // SPAN):
        r = slice(b * SPAN, (b + 1) * SPAN)
        maps = act_ref[r, INNER:]
        affinity = dot(maps[:, STATE:], maps[:, :STATE], ((1,), (1,)))
        cum, shifted = cum_ref[r, :], shifted_ref[:, r]
        decays = split(jnp.exp(cum))
        for c in range(0, INNER, 256):
            decay_ref[(b - 1) * SPAN : b * SPAN, c : c + 256] = dot(decays, sel_ref[:, c : c + 256])
        for pair in range(HEADS // 2):
            cols = slice(pair * LANES, (pair + 1) * LANES)
            y_ref[(b - 1) * SPAN : b * SPAN, cols] = mixed_values(
                affinity, cum, shifted, act_ref[r, cols], skip[:, cols], pair
            )


def gate_kernel(layer, u_ref, w_ref, cum_ref, sel_ref, gate_ref, wide_ref):
    chunk = 256
    before = jnp.zeros((1, HEADS), F32)
    scales = []
    for b in range(u_ref.shape[0] // SPAN):
        cum = cum_ref[b * SPAN : (b + 1) * SPAN, :]
        scales.append(jnp.exp(cum + before))
        before = before + cum[SPAN - 1 : SPAN, :]
    scales = split(jnp.concatenate(scales, axis=0))
    for c in range(0, INNER, chunk):
        cols = slice(c, c + chunk)
        wide_ref[:, cols] = dot(scales, sel_ref[:, cols])
        gate_ref[:, cols] = silu(dot(u_ref[...], w_ref[layer, :, cols]).astype(BF16).astype(F32))


def finish_kernel(
    layer,
    gate_ref,
    wide_ref,
    later_ref,
    decay_ref,
    act_ref,
    own_ref,
    cum_ref,
    shifted_ref,
    edge_ref,
    state_ref,
    skip_ref,
    sel_ref,
    mine_ref,
    other_ref,
    resid_ref,
    wo_ref,
    gain_ref,
    mods_ref,
    *rest,
):
    hidden_ref, a_ref, first_ref, y_ref, normed_ref, enter_ref = rest[-6:]
    rows = gate_ref.shape[0]
    core = core_index()
    enter_ref[pl.ds(core * HALF, HALF)] = mine_ref[...]
    enter_ref[pl.ds((1 - core) * HALF, HALF)] = other_ref[...]
    start = (1 - core).astype(F32)
    sel = sel_ref[...]
    lane = lax.broadcasted_iota(jnp.int32, (SPAN, LANES), 1)
    left = lane < HEAD_DIM
    few = lax.broadcasted_iota(jnp.int32, (TAIL, LANES), 0) < CONV - 1
    nothing = jnp.zeros((TAIL - 8, LANES), F32)

    def fixed(cols, tail):
        total = jnp.concatenate([own_ref[:, cols] + start * tail[0:8, :], nothing], axis=0)
        first_ref[:, cols] = jnp.where(
            few, silu(total), act_ref[0:TAIL, cols].astype(F32)
        ).astype(BF16)

    for pair in range(HEADS // 2):
        pads = [
            enter_ref[h, HEAD_DIM:, :].astype(F32)
            for h in (2 * pair, 2 * pair + 1)
        ]
        tail = jnp.where(left[0:PAD], pltpu.roll(pads[0], HEAD_DIM, 1), pads[1])
        fixed(slice(pair * LANES, (pair + 1) * LANES), pltpu.roll(tail, PAD - 1, 0))
    common = enter_ref[0, HEAD_DIM:, :].astype(F32)
    fixed(slice(INNER, INNER + STATE), pltpu.roll(common, PAD - 7, 0))
    fixed(slice(INNER + STATE, INNER + 2 * STATE), pltpu.roll(common, PAD - 13, 0))

    def acts(b, cols):
        if b:
            return act_ref[b * SPAN : (b + 1) * SPAN, cols]
        return jnp.concatenate([first_ref[:, cols], act_ref[TAIL:SPAN, cols]], axis=0)

    first_tokens = lax.broadcasted_iota(jnp.int32, (TAIL, HEADS), 0) < CONV - 1
    early_scale = split(jnp.where(first_tokens, edge_ref[...], 0.0) * start)
    early_map = first_ref[:, INNER : INNER + STATE]
    spans = rows // SPAN
    out_maps = [acts(b, slice(INNER + STATE, INNER + 2 * STATE)) for b in range(spans)]
    out_map = jnp.concatenate(out_maps, axis=0)
    decayed = [jnp.ones((1, INNER), F32)]
    for b in range(1, spans - 1):
        end = (b + 1) * SPAN - 1
        decayed.append(decayed[-1] * spread_row(jnp.exp(cum_ref[end : end + 1, :]), sel))
    chunk = 256
    for c in range(0, INNER, chunk):
        cols = slice(c, c + chunk)
        entering = jnp.concatenate(
            [enter_ref[h, 0:HEAD_DIM, :] for h in range(c // HEAD_DIM, (c + chunk) // HEAD_DIM)],
            axis=0,
        )
        y_ref[:, cols] = dot(out_map, entering, ((1,), (1,))) * wide_ref[:, cols]
    early = (first_ref[:, 0:INNER].astype(F32) * dot(early_scale, sel)).astype(BF16)
    late = dot(early_map, early, ((0,), (0,)))
    for b in range(1, spans):
        r, own = slice(b * SPAN, (b + 1) * SPAN), slice((b - 1) * SPAN, b * SPAN)
        state = late if b == 1 else decayed[b - 1] * late
        state = state_ref[(b - 1) * STATE : b * STATE, :] + state
        within = later_ref[own, :] + dot(out_maps[b], state.astype(BF16)) * decay_ref[own, :]
        y_ref[r, :] = (y_ref[r, :] + within) * gate_ref[r, :]

    skip = spread_row(skip_ref[layer : layer + 1, :], sel)
    r = slice(0, SPAN)
    affinity = dot(out_maps[0], acts(0, slice(INNER, INNER + STATE)), ((1,), (1,)))
    cum, shifted = cum_ref[r, :], shifted_ref[:, r]
    for pair in range(HEADS // 2):
        cols = slice(pair * LANES, (pair + 1) * LANES)
        y = mixed_values(affinity, cum, shifted, acts(0, cols), skip[:, cols], pair)
        y_ref[r, cols] = (y + y_ref[r, cols]) * gate_ref[r, cols]

    row = lax.broadcasted_iota(jnp.int32, (chunk, chunk), 0) // HEAD_DIM
    col = lax.broadcasted_iota(jnp.int32, (chunk, chunk), 1) // HEAD_DIM
    same = jnp.where(row == col, 1.0 / HEAD_DIM, 0.0).astype(BF16)
    for c in range(0, INNER, chunk):
        cols = slice(c, c + chunk)
        total = y_ref[:, cols]
        square = total * total
        high = square.astype(BF16)
        low = (square - high.astype(F32)).astype(BF16)
        mean = dot(high, same) + dot(low, same)
        gain = gain_ref[layer : layer + 1, cols]
        normed_ref[:, cols] = (total * lax.rsqrt(mean + HEAD_EPS) * gain).astype(BF16)
    hidden = resid_ref[...].astype(F32) + dot(normed_ref[...], wo_ref[layer])
    hidden_ref[...] = hidden
    a_ref[...] = rms_mod(hidden, mods_ref[layer, 2:3, :], mods_ref[layer, 3:4, :])


def partial_attention(q_ref, seen, kv, half, r, k_rows, done):
    left = lax.broadcasted_iota(jnp.int32, (half, LANES), 1) < HEAD_DIM
    one = jnp.ones((k_rows.stop - k_rows.start, LANES), BF16)
    zero = jnp.zeros((half, LANES), BF16)
    seen = jnp.concatenate([seen, seen], axis=0)
    together = 4
    for group in range(0, ATT_HEADS // 2, together):
        columns = [slice(p * LANES, (p + 1) * LANES) for p in range(group, group + together)]
        scores = []
        for cols in columns:
            query = q_ref[r, cols]
            sides = jnp.concatenate(
                [jnp.where(left, query, zero), jnp.where(left, zero, query)], axis=0
            )
            scores.append(dot(sides, kv[k_rows, cols], ((1,), (1,))) + seen)
        tops = [jnp.max(s, axis=-1, keepdims=True) for s in scores]
        weights = [jnp.exp(s - t).astype(BF16) for s, t in zip(scores, tops)]
        for cols, weight, top in zip(columns, weights, tops):
            values = kv[k_rows, ATTN + cols.start : ATTN + cols.stop]
            both = dot(weight, jnp.concatenate([values, one], axis=1))
            number = jnp.where(left, both[:half, :LANES], both[half:, :LANES])
            total = jnp.where(left, both[:half, LANES:], both[half:, LANES:])
            done(cols, number, total, jnp.where(left, top[:half], top[half:]))


def memory_kernel(
    layer, reach_ref, a_ref, wq_ref, wm_ref, q_ref, number_ref, total_ref, top_ref, seen_ref, kv_ref
):
    rows = a_ref.shape[0]
    half = rows // 2
    a = a_ref[...]
    tok_frame = rows // WINDOW
    key_frame = lax.broadcasted_iota(jnp.int32, (tok_frame, 2 * rows), 1) // tok_frame
    first = WINDOW - lax.axis_index("frames") * WINDOW
    for f in range(WINDOW):
        low = jnp.maximum(first, f + WINDOW - reach_ref[f])
        seen = (key_frame >= low) & (key_frame <= f + WINDOW)
        seen_ref[f * tok_frame : (f + 1) * tok_frame, :] = jnp.where(seen, 0.0, -1e30)
    q_ref[...] = (dot(a, wq_ref[layer]).astype(BF16).astype(F32) * HEAD_DIM**-0.5).astype(BF16)
    kv_ref[...] = dot(a, wm_ref[layer]).astype(BF16)
    for part in range(2):
        r = slice(part * half, (part + 1) * half)
        k_rows = slice(0, (part + 1) * half)

        def done(cols, number, total, top):
            number_ref[r, cols] = number
            total_ref[r, cols] = total
            top_ref[r, cols] = top

        seen = seen_ref[r, rows : rows + k_rows.stop]
        partial_attention(q_ref, seen, kv_ref, half, r, k_rows, done)


def attend_half(part, q_ref, own_refs, seen_ref, kv_ref, first_key, out_ref):
    number_ref, total_ref, top_ref = own_refs
    rows = q_ref.shape[0]
    half = rows // 2
    r = slice(part * half, (part + 1) * half)
    keys = slice(part * half, rows)

    def done(cols, number, total, top):
        top_own = top_ref[r, cols]
        highest = jnp.maximum(top, top_own)
        mine, own = jnp.exp(top - highest), jnp.exp(top_own - highest)
        number = number * mine + number_ref[r, cols] * own
        total = total * mine + total_ref[r, cols] * own
        out_ref[r, cols] = (number / total).astype(BF16)

    k_rows = slice(keys.start - first_key, keys.stop - first_key)
    partial_attention(q_ref, seen_ref[r, keys], kv_ref, half, r, k_rows, done)
    return r


def last_rows_kernel(
    layer,
    q_ref,
    number_ref,
    total_ref,
    top_ref,
    seen_ref,
    prev_ref,
    wm_ref,
    merge_ref,
    hidden_ref,
    mods_ref,
    resid_ref,
    u_ref,
    tail_ref,
    kv_ref,
    out_ref,
):
    half = q_ref.shape[0] // 2
    kv_ref[...] = dot(prev_ref[half:, :], wm_ref[layer]).astype(BF16)
    r = attend_half(1, q_ref, (number_ref, total_ref, top_ref), seen_ref, kv_ref, half, out_ref)
    resid = hidden_ref[r, :] + dot(out_ref[r, :], merge_ref[layer])
    resid_ref[...] = resid
    u = rms_mod(resid, mods_ref[layer + 1, 0:1, :], mods_ref[layer + 1, 1:2, :])
    u_ref[...] = u
    tail_ref[...] = u[half - TAIL :]


def first_rows_kernel(
    layer,
    q_ref,
    number_ref,
    total_ref,
    top_ref,
    seen_ref,
    prev_ref,
    wm_ref,
    merge_ref,
    hidden_ref,
    mods_ref,
    late_resid_ref,
    late_u_ref,
    late_kv_ref,
    resid_ref,
    u_ref,
    kv_ref,
    out_ref,
):
    half = q_ref.shape[0] // 2
    kv_ref[0:half, :] = dot(prev_ref[0:half, :], wm_ref[layer]).astype(BF16)
    kv_ref[half:, :] = late_kv_ref[...]
    r = attend_half(0, q_ref, (number_ref, total_ref, top_ref), seen_ref, kv_ref, 0, out_ref)
    resid = hidden_ref[r, :] + dot(out_ref[r, :], merge_ref[layer])
    resid_ref[r, :] = resid
    resid_ref[half:, :] = late_resid_ref[...]
    u_ref[r, :] = rms_mod(resid, mods_ref[layer + 1, 0:1, :], mods_ref[layer + 1, 1:2, :])
    u_ref[half:, :] = late_u_ref[...]


def closing_kernel(
    layer,
    q_ref,
    number_ref,
    total_ref,
    top_ref,
    seen_ref,
    prev_ref,
    wm_ref,
    merge_ref,
    hidden_ref,
    out_hbm,
    kv_ref,
    out_ref,
    resid_ref,
    sems,
):
    kv_ref[...] = dot(prev_ref[...], wm_ref[layer]).astype(BF16)
    copies = []
    for part in range(2):
        own_refs = (number_ref, total_ref, top_ref)
        r = attend_half(part, q_ref, own_refs, seen_ref, kv_ref, 0, out_ref)
        resid_ref[part] = hidden_ref[r, :] + dot(out_ref[r, :], merge_ref[layer])
        copies.append(pltpu.make_async_copy(resid_ref.at[part], out_hbm.at[part], sems.at[part]))
        copies[-1].start()
    for copy in copies:
        copy.wait()


WHOLE = pl.BlockSpec(memory_space=pltpu.VMEM)
SCALARS = pl.BlockSpec(memory_space=pltpu.SMEM)


def run(kernel, operands, outs, scratch=(), name=None, flops=0, scalars=(), out_spec=WHOLE):
    moved = sum(o.size * o.dtype.itemsize for o in list(operands) + list(outs))
    return pl.pallas_call(
        kernel,
        in_specs=[SCALARS] * len(scalars) + [WHOLE] * len(operands),
        out_specs=[out_spec] * len(outs),
        out_shape=list(outs),
        scratch_shapes=list(scratch),
        compiler_params=pltpu.CompilerParams(vmem_limit_bytes=20 * 1024 * 1024),
        cost_estimate=pl.CostEstimate(flops=flops, bytes_accessed=moved, transcendentals=0),
        name=name,
    )(*scalars, *operands)


def shape(dims, dtype):
    return jax.ShapeDtypeStruct(dims, dtype)


def swapped(value, axis):
    count = lax.axis_size(axis)
    return lax.ppermute(value, axis, [(i, i ^ 1) for i in range(count)])


def over_chips(value, axis):
    count = lax.axis_size(axis)
    groups = [list(range(core, count, 2)) for core in range(2)]
    return lax.all_to_all(value, axis, 0, 0, axis_index_groups=groups)


def from_behind(value, axis):
    count = lax.axis_size(axis)
    return lax.ppermute(value, axis, [(i, i + 1) for i in range(count - 1)])


def shards(
    latents,
    timestep,
    lookback,
    modulation,
    input_weight,
    step_weight,
    conv_weight,
    step_bias,
    decay_log,
    skip_gain,
    norm_gain,
    output_weight,
    query_weight,
    memory_weight,
    merge_weight,
):
    frames_dev, tok_frame, width = latents.shape
    rows = frames_dev * tok_frame
    spans = rows // SPAN
    parts = lax.axis_size("frames") // 2
    part_rows = HALF * HEAD_DIM // parts
    mixed = INNER + 2 * STATE
    step_weight = jnp.swapaxes(step_weight, 1, 2)
    step_bias = jnp.swapaxes(step_bias, 1, 2)
    resid = latents.reshape(rows, width)
    (sel,) = run(
        select_kernel, (), [shape((2 * HEADS, INNER), BF16)], name="select", flops=OPENING
    )
    u, tail, mods, bias = run(
        first_kernel,
        (sel, resid, modulation, step_bias),
        [
            shape((rows, width), BF16),
            shape((TAIL, width), BF16),
            shape((LAYERS,) + modulation.shape[2:], F32),
            shape((LAYERS, 8, HEADS), F32),
        ],
        name="first",
        flops=OPENING,
        scalars=(timestep,),
    )
    for layer in range(LAYERS):
        before = swapped(tail, "frames")
        act, own, cum, shifted, edge, state, keep, give = run(
            functools.partial(local_kernel, layer),
            (u, before, input_weight, step_weight, conv_weight, bias, decay_log, sel),
            [
                shape((rows, mixed), BF16),
                shape((8, mixed), F32),
                shape((rows, HEADS), F32),
                shape((HEADS, rows), F32),
                shape((TAIL, HEADS), F32),
                shape((max(spans - 1, 1) * STATE, INNER), F32),
                shape((HALF, BLOCK, LANES), BF16),
                shape((HALF, BLOCK, LANES), BF16),
            ],
            [
                pltpu.VMEM((2, rows + 2 * TAIL, 256), F32),
                pltpu.VMEM((8, mixed), F32),
                pltpu.VMEM((HEADS, PAD, LANES), F32),
                pltpu.VMEM((HEADS, BLOCK, LANES), BF16),
                pltpu.VMEM((rows, INNER), BF16),
            ],
            name="local",
            flops=2 * rows * width * mixed,
        )
        got = swapped(give, "frames")
        later, decays = run(
            functools.partial(later_kernel, layer),
            (act, cum, shifted, skip_gain, sel),
            [shape((max(spans - 1, 1) * SPAN, INNER), F32)] * 2,
            name="later",
            flops=2 * rows * SPAN * INNER,
        )
        got, later, decays = lax.optimization_barrier((got, later, decays))
        (send,) = run(
            chip_kernel,
            (keep, got),
            [shape((parts, part_rows + PAD, LANES), BF16)],
            [pltpu.VMEM((2, HALF, BLOCK, LANES), BF16)],
            name="chip",
        )
        (back,) = run(
            scan_kernel,
            (over_chips(send, "frames"),)
            + (() if layer else (output_weight, norm_gain, query_weight, memory_weight, merge_weight)),
            [shape(send.shape, BF16)],
            [pltpu.VMEM(((parts + 1) * PAD + 8, LANES), F32)],
            name="scan",
        )
        mine, give = run(
            enter_kernel,
            (keep, got, over_chips(back, "frames")),
            [shape(keep.shape, BF16)] * 2,
            [
                pltpu.VMEM((2, HALF, BLOCK, LANES), BF16),
                pltpu.VMEM((2, HALF, BLOCK, LANES), BF16),
                pltpu.VMEM((HEADS, PAD, LANES), F32),
            ],
            name="enter",
        )
        give, u = lax.optimization_barrier((give, u))
        other = swapped(give, "frames")
        gate, wide = run(
            functools.partial(gate_kernel, layer),
            (u, input_weight, cum, sel),
            [shape((rows, INNER), F32)] * 2,
            name="gate",
            flops=2 * rows * width * INNER,
        )
        hidden, a = run(
            functools.partial(finish_kernel, layer),
            (gate, wide, later, decays, act, own, cum, shifted, edge, state, skip_gain, sel)
            + (mine, other, resid, output_weight, norm_gain, mods),
            [shape((rows, width), F32), shape((rows, width), BF16)],
            [
                pltpu.VMEM((TAIL, mixed), BF16),
                pltpu.VMEM((rows, INNER), F32),
                pltpu.VMEM((rows, INNER), BF16),
                pltpu.VMEM((HEADS, BLOCK, LANES), BF16),
            ],
            name="finish",
        )
        prev = from_behind(a, "frames")
        q, number, total, top, seen = run(
            functools.partial(memory_kernel, layer),
            (a, query_weight, memory_weight),
            [shape((rows, ATTN), BF16)]
            + [shape((rows, ATTN), F32)] * 3
            + [shape((rows, 2 * rows), F32)],
            [pltpu.VMEM((rows, 2 * ATTN), BF16)],
            name="memory",
            scalars=(lookback,),
            flops=2 * rows * width * 3 * ATTN,
        )
        half = rows // 2
        attention = (q, number, total, top, seen, prev, memory_weight, merge_weight, hidden)
        if layer == LAYERS - 1:
            (resid,) = run(
                functools.partial(closing_kernel, layer),
                attention,
                [shape((2, half, width), F32)],
                [
                    pltpu.VMEM((rows, 2 * ATTN), BF16),
                    pltpu.VMEM((rows, ATTN), BF16),
                    pltpu.VMEM((2, half, width), F32),
                    pltpu.SemaphoreType.DMA((2,)),
                ],
                name="closing",
                out_spec=pl.BlockSpec(memory_space=pl.ANY),
            )
        else:
            late_resid, late_u, tail, late_kv = run(
                functools.partial(last_rows_kernel, layer),
                attention + (mods,),
                [
                    shape((half, width), F32),
                    shape((half, width), BF16),
                    shape((TAIL, width), BF16),
                    shape((half, 2 * ATTN), BF16),
                ],
                [pltpu.VMEM((rows, ATTN), BF16)],
                name="last_rows",
            )
            resid, u = run(
                functools.partial(first_rows_kernel, layer),
                attention + (mods, late_resid, late_u, late_kv),
                [shape((rows, width), F32), shape((rows, width), BF16)],
                [pltpu.VMEM((rows, 2 * ATTN), BF16), pltpu.VMEM((rows, ATTN), BF16)],
                name="first_rows",
                flops=2 * half * width * 4 * ATTN,
            )
    return resid.reshape(latents.shape)


def solution(mesh):
    sharded = P(("groups", "frames"))
    return jax.shard_map(
        shards,
        mesh=mesh,
        in_specs=(P(("groups", "frames"), None, None), sharded, sharded) + (P(),) * 12,
        out_specs=P(("groups", "frames"), None, None),
        check_vma=False,
    )
```

```python
import functools

import jax
import jax.numpy as jnp
from jax import lax
from jax.experimental import pallas as pl
from jax.experimental.pallas import tpu as pltpu
from jax.sharding import PartitionSpec as P

HEADS = 16
HEAD_DIM = 64
STATE = 128
ATT_HEADS = 8
LAYERS = 2
CONV = 4
SPAN = 128
WINDOW = 8
EPS = 1e-06
HEAD_EPS = 1e-05
INNER = HEADS * HEAD_DIM
ATTN = ATT_HEADS * HEAD_DIM
PAD = 16
BLOCK = HEAD_DIM + PAD
HALF = HEADS // 2
LANES = 128
TAIL = 16
F32 = jnp.float32
OPENING = 4 * 10**9
BF16 = jnp.bfloat16


def dot(a, b, dims=((1,), (0,)), precision=None):
    return lax.dot_general(a, b, (dims, ((), ())), precision=precision, preferred_element_type=F32)


def rms_mod(x, shift, scale):
    normed = x * lax.rsqrt(jnp.mean(x * x, axis=-1, keepdims=True) + EPS)
    return (normed * (1.0 + scale) + shift).astype(BF16)


def split(per_head):
    high = per_head.astype(BF16)
    low = (per_head - high.astype(F32)).astype(BF16)
    return jnp.concatenate([high, low], axis=1)


def spread(per_head, sel):
    return dot(split(per_head), sel)


def spread_row(per_head, sel):
    return spread(jnp.broadcast_to(per_head, (16, HEADS)), sel)[0:1, :]


def select_kernel(sel_ref):
    row = lax.broadcasted_iota(jnp.int32, sel_ref.shape, 0) % HEADS
    head = lax.broadcasted_iota(jnp.int32, sel_ref.shape, 1) // HEAD_DIM
    sel_ref[...] = jnp.where(row == head, 1.0, 0.0).astype(BF16)


def first_kernel(
    step_ref,
    sel_ref,
    x_ref,
    all_mods_ref,
    all_bias_ref,
    u_ref,
    tail_ref,
    mods_ref,
    bias_ref,
):
    rows, width = u_ref.shape
    step = step_ref[0]
    for layer in range(LAYERS):
        mods_ref[layer] = all_mods_ref[layer, step].astype(F32)
    u = rms_mod(x_ref[...].astype(F32), mods_ref[0, 0:1, :], mods_ref[0, 1:2, :])
    u_ref[...] = u
    tail_ref[...] = u[rows - TAIL :]
    chosen = lax.broadcasted_iota(jnp.int32, (8, all_bias_ref.shape[-1]), 1) == step
    chosen = jnp.where(chosen, 1.0, 0.0).astype(F32)
    for layer in range(LAYERS):
        bias_ref[layer] = dot(
            chosen, all_bias_ref[layer], ((1,), (1,)), precision=lax.Precision.HIGHEST
        )


def core_index():
    return lax.axis_index("frames") % 2


def local_kernel(
    layer,
    u_ref,
    before_ref,
    w_ref,
    sw_ref,
    conv_ref,
    bias_ref,
    decay_ref,
    sel_ref,
    act_ref,
    own_ref,
    cum_ref,
    shifted_ref,
    edge_ref,
    state_ref,
    keep_ref,
    give_ref,
    ext_ref,
    tail_ref,
    pad_ref,
    send_ref,
    scaled_ref,
):
    rows = u_ref.shape[0]
    u = u_ref[...]
    sel = sel_ref[...]
    core = core_index()
    tail_rows = before_ref[...].astype(F32) * core.astype(F32)
    with_tail = jnp.concatenate([tail_rows.astype(BF16), u], axis=0)
    raw = dot(u, sw_ref[layer], ((1,), (1,))) + bias_ref[layer, 0:1, :]
    step = jnp.maximum(raw, 0.0) + jnp.log1p(jnp.exp(-jnp.abs(raw)))
    log_decay = -jnp.exp(decay_ref[layer : layer + 1, :]) * step
    log_step = jnp.log(step)
    q_pos = lax.broadcasted_iota(jnp.int32, (SPAN, SPAN), 0)
    s_pos = lax.broadcasted_iota(jnp.int32, (SPAN, SPAN), 1)
    lower = jnp.where(q_pos >= s_pos, 1.0, 0.0).astype(F32)
    whole_tokens = lax.broadcasted_iota(jnp.int32, (SPAN, HEADS), 0) >= (CONV - 1) * (1 - core)
    ends, edges = [], []
    for b in range(rows // SPAN):
        r = slice(b * SPAN, (b + 1) * SPAN)
        cum = dot(lower, log_decay[r], precision=lax.Precision.HIGHEST)
        end = cum[SPAN - 1 : SPAN, :]
        cum_ref[r, :] = cum
        shifted_ref[:, r] = (cum - log_step[r]).T
        edge = jnp.exp(end - cum) * step[r]
        if b == 0:
            edge_ref[...] = edge[0:TAIL, :]
            edge = jnp.where(whole_tokens, edge, 0.0)
        ends.append(end)
        edges.append(edge)

    edges = split(jnp.concatenate(edges, axis=0))
    chunk = 256
    for slot in range(2):
        ext_ref[slot, TAIL + rows :, :] = jnp.zeros((TAIL, chunk), F32)
    for c in [INNER] + list(range(0, INNER, chunk)):
        w = w_ref[layer, :, INNER + c : INNER + c + chunk]
        slot = c // chunk % 2
        ext_ref[slot, 0 : TAIL + rows, :] = dot(with_tail, w).astype(BF16).astype(F32)
        total, after = None, None
        for k in range(CONV):
            start = TAIL - (CONV - 1) + k
            taps = conv_ref[layer, k : k + 1, c : c + chunk]
            term = taps * ext_ref[slot, start : start + rows, :]
            next_term = taps * ext_ref[slot, start + rows : start + rows + 8, :]
            total = term if total is None else total + term
            after = next_term if after is None else after + next_term
        act = (total * jax.nn.sigmoid(total)).astype(BF16)
        act_ref[:, c : c + chunk] = act
        if c < INNER:
            scale = dot(edges, sel_ref[:, c : c + chunk])
            scaled_ref[:, c : c + chunk] = (act.astype(F32) * scale).astype(BF16)
        own_ref[:, c : c + chunk] = total[0:8, :]
        tail_ref[:, c : c + chunk] = after

    state = None
    for b in range(rows // SPAN):
        r = slice(b * SPAN, (b + 1) * SPAN)
        in_map = act_ref[r, INNER : INNER + STATE]
        term = dot(in_map, scaled_ref[r, :], ((0,), (0,)))
        if state is None:
            state = term
        else:
            state_ref[(b - 1) * STATE : b * STATE, :] = state
            state = spread_row(jnp.exp(ends[b]), sel) * state + term

    for pair in range(HEADS // 2):
        turned = state[:, pair * LANES : (pair + 1) * LANES].T.astype(BF16)
        for side in range(2):
            send_ref[2 * pair + side, 0:HEAD_DIM, :] = turned[side * HEAD_DIM : (side + 1) * HEAD_DIM, :]
    over = sum(ends[1:], ends[0])
    edge = jnp.exp(over - cum_ref[0:8, :]) * step[0:8, :]
    left = lax.broadcasted_iota(jnp.int32, (8, LANES), 1) < HEAD_DIM
    few = CONV - 1
    for h in range(HEADS):
        cols = slice(h // 2 * LANES, (h // 2 + 1) * LANES)
        own, tail = own_ref[:, cols], tail_ref[:, cols]
        if h % 2:
            own = pltpu.roll(own, HEAD_DIM, 1)
        else:
            tail = pltpu.roll(tail, HEAD_DIM, 1)
        pad_ref[h, 0:1, :] = halves(jnp.broadcast_to(over[:, h : h + 1], (8, LANES)))[0:1, :]
        pad_ref[h, 1 : 1 + few, :] = jnp.where(left, own, tail)[0:few, :]
        pad_ref[h, 4 : 4 + few, :] = own_ref[0:few, INNER : INNER + STATE]
        pad_ref[h, 7 : 7 + few, :] = tail_ref[0:few, INNER : INNER + STATE]
        broad = jnp.broadcast_to(edge[:, h : h + 1], (8, LANES))
        pad_ref[h, 10 : 10 + few, :] = halves(broad)[0:few, :]
        pad_ref[h, 13 : 13 + few, :] = tail_ref[0:few, INNER + STATE :]
        send_ref[h, HEAD_DIM:, :] = pad_ref[h].astype(BF16)
    keep_ref[...] = send_ref[pl.ds(core * HALF, HALF)]
    give_ref[...] = send_ref[pl.ds((1 - core) * HALF, HALF)]


def halves(value):
    left = lax.broadcasted_iota(jnp.int32, value.shape, 1) < HEAD_DIM
    high = value.astype(BF16).astype(F32)
    return jnp.where(left, high, value - high)


def joined(value):
    return value + pltpu.roll(value, HEAD_DIM, 1)


def chip_kernel(keep_ref, got_ref, send_ref, pair_ref):
    parts, padded, _ = send_ref.shape
    part_rows = padded - PAD
    core = core_index()
    pair_ref[core] = keep_ref[...]
    pair_ref[1 - core] = got_ref[...]
    row = lax.broadcasted_iota(jnp.int32, (PAD, LANES), 0)
    left = lax.broadcasted_iota(jnp.int32, (PAD, LANES), 1) < HEAD_DIM
    for h in range(HALF):
        one = pair_ref[0, h, HEAD_DIM:, :].astype(F32)
        two = pair_ref[1, h, HEAD_DIM:, :].astype(F32)
        one_sum, two_sum = joined(one), joined(two)
        decay = jnp.exp(two_sum[0:1, :])
        state = decay * pair_ref[0, h, 0:HEAD_DIM, :].astype(F32) + pair_ref[
            1, h, 0:HEAD_DIM, :
        ].astype(F32)
        state = state.astype(BF16)
        exact = halves(jnp.where(row == 0, one_sum + two_sum, one_sum * decay))
        for k in range(HEAD_DIM // part_rows):
            at = k * part_rows
            own = pltpu.roll(jnp.where(left, one, 0.0), LANES - at, 1) if at else one
            pad = jnp.where(row < 4, jnp.where(left, own, two), jnp.where(row < 7, one, two))
            pad = jnp.where((row == 0) | ((row >= 10) & (row < 13)), exact, pad)
            part = h * (HEAD_DIM // part_rows) + k
            send_ref[part, 0:part_rows, :] = state[at : at + part_rows, :]
            send_ref[part, part_rows:, :] = pad.astype(BF16)


def enter_kernel(keep_ref, got_ref, back_ref, mine_ref, give_ref, pair_ref, enter_ref, pad_ref):
    parts, padded, _ = back_ref.shape
    part_rows = padded - PAD
    each = HEAD_DIM // part_rows
    core = core_index()
    pair_ref[core] = keep_ref[...]
    pair_ref[1 - core] = got_ref[...]
    few = lax.broadcasted_iota(jnp.int32, (8, LANES), 0) < CONV - 1
    for h in range(HALF):
        pad = back_ref[h * each, part_rows:, :]
        pad_ref[2 * h] = pad.astype(F32)
        pad_ref[2 * h + 1] = pair_ref[0, h, HEAD_DIM:, :].astype(F32)
    for h in range(HALF):
        last, mine = 2 * h, 2 * h + 1
        entering = jnp.concatenate(
            [back_ref[h * each + k, 0:part_rows, :] for k in range(each)], axis=0
        )
        values = silu(pad_ref[mine, 1:9, :] + pltpu.roll(pad_ref[last, 1:9, :], HEAD_DIM, 1))
        in_map = silu(pad_ref[mine, 4:12, :] + pad_ref[last, 7:15, :])
        edge = joined(pad_ref[mine, 8:16, :])
        edge = pltpu.roll(edge, 6, 0)
        scaled = jnp.where(few, values.astype(BF16).astype(F32) * edge, 0.0)
        added = dot(scaled, jnp.where(few, in_map, 0.0), ((0,), (0,)))[0:HEAD_DIM, :]
        decay = jnp.exp(joined(pad_ref[mine, 0:8, :])[0:1, :])
        after = decay * entering.astype(F32) + pair_ref[0, h, 0:HEAD_DIM, :].astype(F32) + added
        pad = back_ref[h * each, part_rows:, :]
        enter_ref[0, h, 0:HEAD_DIM, :] = entering
        enter_ref[1, h, 0:HEAD_DIM, :] = after.astype(BF16)
        enter_ref[0, h, HEAD_DIM:, :] = pad
        enter_ref[1, h, HEAD_DIM:, :] = pad
    mine_ref[...] = enter_ref[core]
    give_ref[...] = enter_ref[1 - core]


def silu(x):
    return x * jax.nn.sigmoid(x)


def scan_kernel(got_ref, *rest):
    back_ref, pad_ref = rest[-2:]
    parts, padded, _ = got_ref.shape
    part_rows = padded - PAD
    rows = slice(0, part_rows)
    offset = lax.axis_index("frames") // 2 * part_rows % HEAD_DIM
    few = lax.broadcasted_iota(jnp.int32, (8, LANES), 0) < CONV - 1
    left = lax.broadcasted_iota(jnp.int32, (8, LANES), 1) < HEAD_DIM
    pad_ref[0:PAD, :] = jnp.zeros((PAD, LANES), F32)
    pad_ref[(parts + 1) * PAD :, :] = jnp.zeros((8, LANES), F32)
    for d in range(parts):
        pad_ref[(d + 1) * PAD : (d + 2) * PAD, :] = got_ref[d, part_rows:, :].astype(F32)
    carry = jnp.zeros((part_rows, LANES), F32)
    for d in range(parts):
        back_ref[d, rows, :] = carry.astype(BF16)
        back_ref[d, part_rows:, :] = pad_ref[d * PAD : (d + 1) * PAD, :].astype(BF16)
        last, mine = d * PAD, (d + 1) * PAD
        decay = pad_ref[mine : mine + 1, :]
        decay = jnp.exp(decay + pltpu.roll(decay, HEAD_DIM, 1))
        from_tail = pltpu.roll(pad_ref[last + 1 : last + 9, :], HEAD_DIM, 1)
        if part_rows < HEAD_DIM:
            from_tail = pltpu.roll(jnp.where(left, from_tail, 0.0), (LANES - offset) % LANES, 1)
        values = silu(pad_ref[mine + 1 : mine + 9, :] + from_tail)
        in_map = silu(pad_ref[mine + 4 : mine + 12, :] + pad_ref[last + 7 : last + 15, :])
        edge = pad_ref[mine + 10 : mine + 18, :]
        edge = edge + pltpu.roll(edge, HEAD_DIM, 1)
        scaled = jnp.where(few, values.astype(BF16).astype(F32) * edge, 0.0)
        in_map = jnp.where(few, in_map, 0.0)
        added = dot(scaled, in_map, ((0,), (0,)))
        carry = decay * carry + (got_ref[d, rows, :].astype(F32) + added[rows, :])


def mixed_values(affinity, cum, shifted, values, skip, pair):
    q_pos = lax.broadcasted_iota(jnp.int32, (SPAN, SPAN), 0)
    s_pos = lax.broadcasted_iota(jnp.int32, (SPAN, SPAN), 1)
    lower = q_pos >= s_pos
    left = lax.broadcasted_iota(jnp.int32, (SPAN, LANES), 1) < HEAD_DIM
    zero = jnp.zeros((SPAN, LANES), BF16)
    mixing = []
    for h in (2 * pair, 2 * pair + 1):
        gap = cum[:, h : h + 1] - shifted[h : h + 1, :]
        mixing.append(jnp.where(lower, affinity * jnp.exp(gap), 0.0).astype(BF16))
    both = jnp.concatenate(mixing, axis=1)
    stacked = jnp.concatenate([jnp.where(left, values, zero), jnp.where(left, zero, values)], axis=0)
    return dot(both, stacked) + skip * values.astype(F32)


def later_kernel(layer, act_ref, cum_ref, shifted_ref, skip_ref, sel_ref, y_ref, decay_ref):
    skip = spread_row(skip_ref[layer : layer + 1, :], sel_ref[...])
    for b in range(1, act_ref.shape[0] // SPAN):
        r = slice(b * SPAN, (b + 1) * SPAN)
        maps = act_ref[r, INNER:]
        affinity = dot(maps[:, STATE:], maps[:, :STATE], ((1,), (1,)))
        cum, shifted = cum_ref[r, :], shifted_ref[:, r]
        decays = split(jnp.exp(cum))
        for c in range(0, INNER, 256):
            decay_ref[(b - 1) * SPAN : b * SPAN, c : c + 256] = dot(decays, sel_ref[:, c : c + 256])
        for pair in range(HEADS // 2):
            cols = slice(pair * LANES, (pair + 1) * LANES)
            y_ref[(b - 1) * SPAN : b * SPAN, cols] = mixed_values(
                affinity, cum, shifted, act_ref[r, cols], skip[:, cols], pair
            )


def gate_kernel(layer, u_ref, w_ref, cum_ref, sel_ref, gate_ref, wide_ref):
    chunk = 256
    before = jnp.zeros((1, HEADS), F32)
    scales = []
    for b in range(u_ref.shape[0] // SPAN):
        cum = cum_ref[b * SPAN : (b + 1) * SPAN, :]
        scales.append(jnp.exp(cum + before))
        before = before + cum[SPAN - 1 : SPAN, :]
    scales = split(jnp.concatenate(scales, axis=0))
    for c in range(0, INNER, chunk):
        cols = slice(c, c + chunk)
        wide_ref[:, cols] = dot(scales, sel_ref[:, cols])
        gate_ref[:, cols] = silu(dot(u_ref[...], w_ref[layer, :, cols]).astype(BF16).astype(F32))


def finish_kernel(
    layer,
    gate_ref,
    wide_ref,
    later_ref,
    decay_ref,
    act_ref,
    own_ref,
    cum_ref,
    shifted_ref,
    edge_ref,
    state_ref,
    skip_ref,
    sel_ref,
    mine_ref,
    other_ref,
    resid_ref,
    wo_ref,
    gain_ref,
    mods_ref,
    *rest,
):
    hidden_ref, a_ref, first_ref, y_ref, normed_ref, enter_ref = rest[-6:]
    rows = gate_ref.shape[0]
    core = core_index()
    enter_ref[pl.ds(core * HALF, HALF)] = mine_ref[...]
    enter_ref[pl.ds((1 - core) * HALF, HALF)] = other_ref[...]
    start = (1 - core).astype(F32)
    sel = sel_ref[...]
    lane = lax.broadcasted_iota(jnp.int32, (SPAN, LANES), 1)
    left = lane < HEAD_DIM
    few = lax.broadcasted_iota(jnp.int32, (TAIL, LANES), 0) < CONV - 1
    nothing = jnp.zeros((TAIL - 8, LANES), F32)

    def fixed(cols, tail):
        total = jnp.concatenate([own_ref[:, cols] + start * tail[0:8, :], nothing], axis=0)
        first_ref[:, cols] = jnp.where(
            few, silu(total), act_ref[0:TAIL, cols].astype(F32)
        ).astype(BF16)

    for pair in range(HEADS // 2):
        pads = [
            enter_ref[h, HEAD_DIM:, :].astype(F32)
            for h in (2 * pair, 2 * pair + 1)
        ]
        tail = jnp.where(left[0:PAD], pltpu.roll(pads[0], HEAD_DIM, 1), pads[1])
        fixed(slice(pair * LANES, (pair + 1) * LANES), pltpu.roll(tail, PAD - 1, 0))
    common = enter_ref[0, HEAD_DIM:, :].astype(F32)
    fixed(slice(INNER, INNER + STATE), pltpu.roll(common, PAD - 7, 0))
    fixed(slice(INNER + STATE, INNER + 2 * STATE), pltpu.roll(common, PAD - 13, 0))

    def acts(b, cols):
        if b:
            return act_ref[b * SPAN : (b + 1) * SPAN, cols]
        return jnp.concatenate([first_ref[:, cols], act_ref[TAIL:SPAN, cols]], axis=0)

    first_tokens = lax.broadcasted_iota(jnp.int32, (TAIL, HEADS), 0) < CONV - 1
    early_scale = split(jnp.where(first_tokens, edge_ref[...], 0.0) * start)
    early_map = first_ref[:, INNER : INNER + STATE]
    spans = rows // SPAN
    out_maps = [acts(b, slice(INNER + STATE, INNER + 2 * STATE)) for b in range(spans)]
    out_map = jnp.concatenate(out_maps, axis=0)
    decayed = [jnp.ones((1, INNER), F32)]
    for b in range(1, spans - 1):
        end = (b + 1) * SPAN - 1
        decayed.append(decayed[-1] * spread_row(jnp.exp(cum_ref[end : end + 1, :]), sel))
    chunk = 256
    for c in range(0, INNER, chunk):
        cols = slice(c, c + chunk)
        entering = jnp.concatenate(
            [enter_ref[h, 0:HEAD_DIM, :] for h in range(c // HEAD_DIM, (c + chunk) // HEAD_DIM)],
            axis=0,
        )
        y_ref[:, cols] = dot(out_map, entering, ((1,), (1,))) * wide_ref[:, cols]
    early = (first_ref[:, 0:INNER].astype(F32) * dot(early_scale, sel)).astype(BF16)
    late = dot(early_map, early, ((0,), (0,)))
    for b in range(1, spans):
        r, own = slice(b * SPAN, (b + 1) * SPAN), slice((b - 1) * SPAN, b * SPAN)
        state = late if b == 1 else decayed[b - 1] * late
        state = state_ref[(b - 1) * STATE : b * STATE, :] + state
        within = later_ref[own, :] + dot(out_maps[b], state.astype(BF16)) * decay_ref[own, :]
        y_ref[r, :] = (y_ref[r, :] + within) * gate_ref[r, :]

    skip = spread_row(skip_ref[layer : layer + 1, :], sel)
    r = slice(0, SPAN)
    affinity = dot(out_maps[0], acts(0, slice(INNER, INNER + STATE)), ((1,), (1,)))
    cum, shifted = cum_ref[r, :], shifted_ref[:, r]
    for pair in range(HEADS // 2):
        cols = slice(pair * LANES, (pair + 1) * LANES)
        y = mixed_values(affinity, cum, shifted, acts(0, cols), skip[:, cols], pair)
        y_ref[r, cols] = (y + y_ref[r, cols]) * gate_ref[r, cols]

    row = lax.broadcasted_iota(jnp.int32, (chunk, chunk), 0) // HEAD_DIM
    col = lax.broadcasted_iota(jnp.int32, (chunk, chunk), 1) // HEAD_DIM
    same = jnp.where(row == col, 1.0 / HEAD_DIM, 0.0).astype(BF16)
    for c in range(0, INNER, chunk):
        cols = slice(c, c + chunk)
        total = y_ref[:, cols]
        square = total * total
        high = square.astype(BF16)
        low = (square - high.astype(F32)).astype(BF16)
        mean = dot(high, same) + dot(low, same)
        gain = gain_ref[layer : layer + 1, cols]
        normed_ref[:, cols] = (total * lax.rsqrt(mean + HEAD_EPS) * gain).astype(BF16)
    hidden = resid_ref[...].astype(F32) + dot(normed_ref[...], wo_ref[layer])
    hidden_ref[...] = hidden
    a_ref[...] = rms_mod(hidden, mods_ref[layer, 2:3, :], mods_ref[layer, 3:4, :])


def partial_attention(q_ref, seen, kv, half, r, k_rows, done):
    left = lax.broadcasted_iota(jnp.int32, (half, LANES), 1) < HEAD_DIM
    one = jnp.ones((k_rows.stop - k_rows.start, LANES), BF16)
    zero = jnp.zeros((half, LANES), BF16)
    seen = jnp.concatenate([seen, seen], axis=0)
    together = 4
    for group in range(0, ATT_HEADS // 2, together):
        columns = [slice(p * LANES, (p + 1) * LANES) for p in range(group, group + together)]
        scores = []
        for cols in columns:
            query = q_ref[r, cols]
            sides = jnp.concatenate(
                [jnp.where(left, query, zero), jnp.where(left, zero, query)], axis=0
            )
            scores.append(dot(sides, kv[k_rows, cols], ((1,), (1,))) + seen)
        tops = [jnp.max(s, axis=-1, keepdims=True) for s in scores]
        weights = [jnp.exp(s - t).astype(BF16) for s, t in zip(scores, tops)]
        for cols, weight, top in zip(columns, weights, tops):
            values = kv[k_rows, ATTN + cols.start : ATTN + cols.stop]
            both = dot(weight, jnp.concatenate([values, one], axis=1))
            number = jnp.where(left, both[:half, :LANES], both[half:, :LANES])
            total = jnp.where(left, both[:half, LANES:], both[half:, LANES:])
            done(cols, number, total, jnp.where(left, top[:half], top[half:]))


def memory_kernel(
    layer, reach_ref, a_ref, wq_ref, wm_ref, q_ref, number_ref, total_ref, top_ref, seen_ref, kv_ref
):
    rows = a_ref.shape[0]
    half = rows // 2
    a = a_ref[...]
    tok_frame = rows // WINDOW
    key_frame = lax.broadcasted_iota(jnp.int32, (tok_frame, 2 * rows), 1) // tok_frame
    first = WINDOW - lax.axis_index("frames") * WINDOW
    for f in range(WINDOW):
        low = jnp.maximum(first, f + WINDOW - reach_ref[f])
        seen = (key_frame >= low) & (key_frame <= f + WINDOW)
        seen_ref[f * tok_frame : (f + 1) * tok_frame, :] = jnp.where(seen, 0.0, -1e30)
    q_ref[...] = (dot(a, wq_ref[layer]).astype(BF16).astype(F32) * HEAD_DIM**-0.5).astype(BF16)
    kv_ref[...] = dot(a, wm_ref[layer]).astype(BF16)
    for part in range(2):
        r = slice(part * half, (part + 1) * half)
        k_rows = slice(0, (part + 1) * half)

        def done(cols, number, total, top):
            number_ref[r, cols] = number
            total_ref[r, cols] = total
            top_ref[r, cols] = top

        seen = seen_ref[r, rows : rows + k_rows.stop]
        partial_attention(q_ref, seen, kv_ref, half, r, k_rows, done)


def attend_half(part, q_ref, own_refs, seen_ref, kv_ref, first_key, out_ref):
    number_ref, total_ref, top_ref = own_refs
    rows = q_ref.shape[0]
    half = rows // 2
    r = slice(part * half, (part + 1) * half)
    keys = slice(part * half, rows)

    def done(cols, number, total, top):
        top_own = top_ref[r, cols]
        highest = jnp.maximum(top, top_own)
        mine, own = jnp.exp(top - highest), jnp.exp(top_own - highest)
        number = number * mine + number_ref[r, cols] * own
        total = total * mine + total_ref[r, cols] * own
        out_ref[r, cols] = (number / total).astype(BF16)

    k_rows = slice(keys.start - first_key, keys.stop - first_key)
    partial_attention(q_ref, seen_ref[r, keys], kv_ref, half, r, k_rows, done)
    return r


def last_rows_kernel(
    layer,
    q_ref,
    number_ref,
    total_ref,
    top_ref,
    seen_ref,
    prev_ref,
    wm_ref,
    merge_ref,
    hidden_ref,
    mods_ref,
    resid_ref,
    u_ref,
    tail_ref,
    kv_ref,
    out_ref,
):
    half = q_ref.shape[0] // 2
    kv_ref[...] = dot(prev_ref[half:, :], wm_ref[layer]).astype(BF16)
    r = attend_half(1, q_ref, (number_ref, total_ref, top_ref), seen_ref, kv_ref, half, out_ref)
    resid = hidden_ref[r, :] + dot(out_ref[r, :], merge_ref[layer])
    resid_ref[...] = resid
    u = rms_mod(resid, mods_ref[layer + 1, 0:1, :], mods_ref[layer + 1, 1:2, :])
    u_ref[...] = u
    tail_ref[...] = u[half - TAIL :]


def first_rows_kernel(
    layer,
    q_ref,
    number_ref,
    total_ref,
    top_ref,
    seen_ref,
    prev_ref,
    wm_ref,
    merge_ref,
    hidden_ref,
    mods_ref,
    late_resid_ref,
    late_u_ref,
    late_kv_ref,
    resid_ref,
    u_ref,
    kv_ref,
    out_ref,
):
    half = q_ref.shape[0] // 2
    kv_ref[0:half, :] = dot(prev_ref[0:half, :], wm_ref[layer]).astype(BF16)
    kv_ref[half:, :] = late_kv_ref[...]
    r = attend_half(0, q_ref, (number_ref, total_ref, top_ref), seen_ref, kv_ref, 0, out_ref)
    resid = hidden_ref[r, :] + dot(out_ref[r, :], merge_ref[layer])
    resid_ref[r, :] = resid
    resid_ref[half:, :] = late_resid_ref[...]
    u_ref[r, :] = rms_mod(resid, mods_ref[layer + 1, 0:1, :], mods_ref[layer + 1, 1:2, :])
    u_ref[half:, :] = late_u_ref[...]


def closing_kernel(
    layer,
    q_ref,
    number_ref,
    total_ref,
    top_ref,
    seen_ref,
    prev_ref,
    wm_ref,
    merge_ref,
    hidden_ref,
    resid_ref,
    kv_ref,
    out_ref,
):
    kv_ref[...] = dot(prev_ref[...], wm_ref[layer]).astype(BF16)
    for part in range(2):
        own_refs = (number_ref, total_ref, top_ref)
        attend_half(part, q_ref, own_refs, seen_ref, kv_ref, 0, out_ref)
    resid_ref[...] = hidden_ref[...] + dot(out_ref[...], merge_ref[layer])


WHOLE = pl.BlockSpec(memory_space=pltpu.VMEM)
SCALARS = pl.BlockSpec(memory_space=pltpu.SMEM)


def run(kernel, operands, outs, scratch=(), name=None, flops=0, scalars=()):
    moved = sum(o.size * o.dtype.itemsize for o in list(operands) + list(outs))
    return pl.pallas_call(
        kernel,
        in_specs=[SCALARS] * len(scalars) + [WHOLE] * len(operands),
        out_specs=[WHOLE] * len(outs),
        out_shape=list(outs),
        scratch_shapes=list(scratch),
        compiler_params=pltpu.CompilerParams(vmem_limit_bytes=20 * 1024 * 1024),
        cost_estimate=pl.CostEstimate(flops=flops, bytes_accessed=moved, transcendentals=0),
        name=name,
    )(*scalars, *operands)


def shape(dims, dtype):
    return jax.ShapeDtypeStruct(dims, dtype)


def swapped(value, axis):
    count = lax.axis_size(axis)
    return lax.ppermute(value, axis, [(i, i ^ 1) for i in range(count)])


def over_chips(value, axis):
    count = lax.axis_size(axis)
    groups = [list(range(core, count, 2)) for core in range(2)]
    return lax.all_to_all(value, axis, 0, 0, axis_index_groups=groups)


def from_behind(value, axis):
    count = lax.axis_size(axis)
    return lax.ppermute(value, axis, [(i, i + 1) for i in range(count - 1)])


def shards(
    latents,
    timestep,
    lookback,
    modulation,
    input_weight,
    step_weight,
    conv_weight,
    step_bias,
    decay_log,
    skip_gain,
    norm_gain,
    output_weight,
    query_weight,
    memory_weight,
    merge_weight,
):
    frames_dev, tok_frame, width = latents.shape
    rows = frames_dev * tok_frame
    spans = rows // SPAN
    parts = lax.axis_size("frames") // 2
    part_rows = HALF * HEAD_DIM // parts
    mixed = INNER + 2 * STATE
    step_weight = jnp.swapaxes(step_weight, 1, 2)
    step_bias = jnp.swapaxes(step_bias, 1, 2)
    resid = latents.reshape(rows, width)
    (sel,) = run(
        select_kernel, (), [shape((2 * HEADS, INNER), BF16)], name="select", flops=OPENING
    )
    u, tail, mods, bias = run(
        first_kernel,
        (sel, resid, modulation, step_bias),
        [
            shape((rows, width), BF16),
            shape((TAIL, width), BF16),
            shape((LAYERS,) + modulation.shape[2:], F32),
            shape((LAYERS, 8, HEADS), F32),
        ],
        name="first",
        flops=OPENING,
        scalars=(timestep,),
    )
    for layer in range(LAYERS):
        before = swapped(tail, "frames")
        act, own, cum, shifted, edge, state, keep, give = run(
            functools.partial(local_kernel, layer),
            (u, before, input_weight, step_weight, conv_weight, bias, decay_log, sel),
            [
                shape((rows, mixed), BF16),
                shape((8, mixed), F32),
                shape((rows, HEADS), F32),
                shape((HEADS, rows), F32),
                shape((TAIL, HEADS), F32),
                shape((max(spans - 1, 1) * STATE, INNER), F32),
                shape((HALF, BLOCK, LANES), BF16),
                shape((HALF, BLOCK, LANES), BF16),
            ],
            [
                pltpu.VMEM((2, rows + 2 * TAIL, 256), F32),
                pltpu.VMEM((8, mixed), F32),
                pltpu.VMEM((HEADS, PAD, LANES), F32),
                pltpu.VMEM((HEADS, BLOCK, LANES), BF16),
                pltpu.VMEM((rows, INNER), BF16),
            ],
            name="local",
            flops=2 * rows * width * mixed,
        )
        got = swapped(give, "frames")
        later, decays = run(
            functools.partial(later_kernel, layer),
            (act, cum, shifted, skip_gain, sel),
            [shape((max(spans - 1, 1) * SPAN, INNER), F32)] * 2,
            name="later",
            flops=2 * rows * SPAN * INNER,
        )
        got, later, decays = lax.optimization_barrier((got, later, decays))
        (send,) = run(
            chip_kernel,
            (keep, got),
            [shape((parts, part_rows + PAD, LANES), BF16)],
            [pltpu.VMEM((2, HALF, BLOCK, LANES), BF16)],
            name="chip",
        )
        (back,) = run(
            scan_kernel,
            (over_chips(send, "frames"),)
            + (() if layer else (output_weight, norm_gain, query_weight, memory_weight, merge_weight)),
            [shape(send.shape, BF16)],
            [pltpu.VMEM(((parts + 1) * PAD + 8, LANES), F32)],
            name="scan",
        )
        mine, give = run(
            enter_kernel,
            (keep, got, over_chips(back, "frames")),
            [shape(keep.shape, BF16)] * 2,
            [
                pltpu.VMEM((2, HALF, BLOCK, LANES), BF16),
                pltpu.VMEM((2, HALF, BLOCK, LANES), BF16),
                pltpu.VMEM((HEADS, PAD, LANES), F32),
            ],
            name="enter",
        )
        give, u = lax.optimization_barrier((give, u))
        other = swapped(give, "frames")
        gate, wide = run(
            functools.partial(gate_kernel, layer),
            (u, input_weight, cum, sel),
            [shape((rows, INNER), F32)] * 2,
            name="gate",
            flops=2 * rows * width * INNER,
        )
        hidden, a = run(
            functools.partial(finish_kernel, layer),
            (gate, wide, later, decays, act, own, cum, shifted, edge, state, skip_gain, sel)
            + (mine, other, resid, output_weight, norm_gain, mods),
            [shape((rows, width), F32), shape((rows, width), BF16)],
            [
                pltpu.VMEM((TAIL, mixed), BF16),
                pltpu.VMEM((rows, INNER), F32),
                pltpu.VMEM((rows, INNER), BF16),
                pltpu.VMEM((HEADS, BLOCK, LANES), BF16),
            ],
            name="finish",
        )
        prev = from_behind(a, "frames")
        q, number, total, top, seen = run(
            functools.partial(memory_kernel, layer),
            (a, query_weight, memory_weight),
            [shape((rows, ATTN), BF16)]
            + [shape((rows, ATTN), F32)] * 3
            + [shape((rows, 2 * rows), F32)],
            [pltpu.VMEM((rows, 2 * ATTN), BF16)],
            name="memory",
            scalars=(lookback,),
            flops=2 * rows * width * 3 * ATTN,
        )
        half = rows // 2
        attention = (q, number, total, top, seen, prev, memory_weight, merge_weight, hidden)
        if layer == LAYERS - 1:
            (resid,) = run(
                functools.partial(closing_kernel, layer),
                attention,
                [shape((rows, width), F32)],
                [pltpu.VMEM((rows, 2 * ATTN), BF16), pltpu.VMEM((rows, ATTN), BF16)],
                name="closing",
            )
        else:
            late_resid, late_u, tail, late_kv = run(
                functools.partial(last_rows_kernel, layer),
                attention + (mods,),
                [
                    shape((half, width), F32),
                    shape((half, width), BF16),
                    shape((TAIL, width), BF16),
                    shape((half, 2 * ATTN), BF16),
                ],
                [pltpu.VMEM((rows, ATTN), BF16)],
                name="last_rows",
            )
            resid, u = run(
                functools.partial(first_rows_kernel, layer),
                attention + (mods, late_resid, late_u, late_kv),
                [shape((rows, width), F32), shape((rows, width), BF16)],
                [pltpu.VMEM((rows, 2 * ATTN), BF16), pltpu.VMEM((rows, ATTN), BF16)],
                name="first_rows",
                flops=2 * half * width * 4 * ATTN,
            )
    return resid.reshape(latents.shape)


def solution(mesh):
    sharded = P(("groups", "frames"))
    return jax.shard_map(
        shards,
        mesh=mesh,
        in_specs=(P(("groups", "frames"), None, None), sharded, sharded) + (P(),) * 12,
        out_specs=P(("groups", "frames"), None, None),
        check_vma=False,
    )
```

```python
import functools

import jax
import jax.numpy as jnp
from jax import lax
from jax.experimental import pallas as pl
from jax.experimental.pallas import tpu as pltpu
from jax.sharding import PartitionSpec as P

HEADS = 16
HEAD_DIM = 64
STATE = 128
ATT_HEADS = 8
LAYERS = 2
CONV = 4
SPAN = 128
WINDOW = 8
EPS = 1e-06
HEAD_EPS = 1e-05
INNER = HEADS * HEAD_DIM
ATTN = ATT_HEADS * HEAD_DIM
PAD = 16
BLOCK = HEAD_DIM + PAD
HALF = HEADS // 2
LANES = 128
TAIL = 16
F32 = jnp.float32
OPENING = 4 * 10**9
BF16 = jnp.bfloat16


def dot(a, b, dims=((1,), (0,)), precision=None):
    return lax.dot_general(a, b, (dims, ((), ())), precision=precision, preferred_element_type=F32)


def rms_mod(x, shift, scale):
    normed = x * lax.rsqrt(jnp.mean(x * x, axis=-1, keepdims=True) + EPS)
    return (normed * (1.0 + scale) + shift).astype(BF16)


def split(per_head):
    high = per_head.astype(BF16)
    low = (per_head - high.astype(F32)).astype(BF16)
    return jnp.concatenate([high, low], axis=1)


def spread(per_head, sel):
    return dot(split(per_head), sel)


def spread_row(per_head, sel):
    return spread(jnp.broadcast_to(per_head, (16, HEADS)), sel)[0:1, :]


def select_kernel(sel_ref):
    row = lax.broadcasted_iota(jnp.int32, sel_ref.shape, 0) % HEADS
    head = lax.broadcasted_iota(jnp.int32, sel_ref.shape, 1) // HEAD_DIM
    sel_ref[...] = jnp.where(row == head, 1.0, 0.0).astype(BF16)


def first_kernel(
    step_ref,
    sel_ref,
    x_ref,
    all_mods_ref,
    all_bias_ref,
    u_ref,
    tail_ref,
    mods_ref,
    bias_ref,
):
    rows, width = u_ref.shape
    step = step_ref[0]
    for layer in range(LAYERS):
        mods_ref[layer] = all_mods_ref[layer, step].astype(F32)
    u = rms_mod(x_ref[...].astype(F32), mods_ref[0, 0:1, :], mods_ref[0, 1:2, :])
    u_ref[...] = u
    tail_ref[...] = u[rows - TAIL :]
    chosen = lax.broadcasted_iota(jnp.int32, (8, all_bias_ref.shape[-1]), 1) == step
    chosen = jnp.where(chosen, 1.0, 0.0).astype(F32)
    for layer in range(LAYERS):
        bias_ref[layer] = dot(
            chosen, all_bias_ref[layer], ((1,), (1,)), precision=lax.Precision.HIGHEST
        )


def core_index():
    return lax.axis_index("frames") % 2


def local_kernel(
    layer,
    u_ref,
    before_ref,
    w_ref,
    sw_ref,
    conv_ref,
    bias_ref,
    decay_ref,
    sel_ref,
    act_ref,
    own_ref,
    cum_ref,
    shifted_ref,
    edge_ref,
    state_ref,
    keep_ref,
    give_ref,
    ext_ref,
    tail_ref,
    pad_ref,
    send_ref,
    scaled_ref,
):
    rows = u_ref.shape[0]
    u = u_ref[...]
    sel = sel_ref[...]
    core = core_index()
    tail_rows = before_ref[...].astype(F32) * core.astype(F32)
    with_tail = jnp.concatenate([tail_rows.astype(BF16), u], axis=0)
    raw = dot(u, sw_ref[layer], ((1,), (1,))) + bias_ref[layer, 0:1, :]
    step = jnp.maximum(raw, 0.0) + jnp.log1p(jnp.exp(-jnp.abs(raw)))
    log_decay = -jnp.exp(decay_ref[layer : layer + 1, :]) * step
    log_step = jnp.log(step)
    q_pos = lax.broadcasted_iota(jnp.int32, (SPAN, SPAN), 0)
    s_pos = lax.broadcasted_iota(jnp.int32, (SPAN, SPAN), 1)
    lower = jnp.where(q_pos >= s_pos, 1.0, 0.0).astype(F32)
    whole_tokens = lax.broadcasted_iota(jnp.int32, (SPAN, HEADS), 0) >= (CONV - 1) * (1 - core)
    ends, edges = [], []
    for b in range(rows // SPAN):
        r = slice(b * SPAN, (b + 1) * SPAN)
        cum = dot(lower, log_decay[r], precision=lax.Precision.HIGHEST)
        end = cum[SPAN - 1 : SPAN, :]
        cum_ref[r, :] = cum
        shifted_ref[:, r] = (cum - log_step[r]).T
        edge = jnp.exp(end - cum) * step[r]
        if b == 0:
            edge_ref[...] = edge[0:TAIL, :]
            edge = jnp.where(whole_tokens, edge, 0.0)
        ends.append(end)
        edges.append(edge)

    edges = split(jnp.concatenate(edges, axis=0))
    chunk = 256
    for slot in range(2):
        ext_ref[slot, TAIL + rows :, :] = jnp.zeros((TAIL, chunk), F32)
    for c in [INNER] + list(range(0, INNER, chunk)):
        w = w_ref[layer, :, INNER + c : INNER + c + chunk]
        slot = c // chunk % 2
        ext_ref[slot, 0 : TAIL + rows, :] = dot(with_tail, w).astype(BF16).astype(F32)
        total, after = None, None
        for k in range(CONV):
            start = TAIL - (CONV - 1) + k
            taps = conv_ref[layer, k : k + 1, c : c + chunk]
            term = taps * ext_ref[slot, start : start + rows, :]
            next_term = taps * ext_ref[slot, start + rows : start + rows + 8, :]
            total = term if total is None else total + term
            after = next_term if after is None else after + next_term
        act = (total * jax.nn.sigmoid(total)).astype(BF16)
        act_ref[:, c : c + chunk] = act
        if c < INNER:
            scale = dot(edges, sel_ref[:, c : c + chunk])
            scaled_ref[:, c : c + chunk] = (act.astype(F32) * scale).astype(BF16)
        own_ref[:, c : c + chunk] = total[0:8, :]
        tail_ref[:, c : c + chunk] = after

    state = None
    for b in range(rows // SPAN):
        r = slice(b * SPAN, (b + 1) * SPAN)
        in_map = act_ref[r, INNER : INNER + STATE]
        term = dot(in_map, scaled_ref[r, :], ((0,), (0,)))
        if state is None:
            state = term
        else:
            state_ref[(b - 1) * STATE : b * STATE, :] = state
            state = spread_row(jnp.exp(ends[b]), sel) * state + term

    for pair in range(HEADS // 2):
        turned = state[:, pair * LANES : (pair + 1) * LANES].T.astype(BF16)
        for side in range(2):
            send_ref[2 * pair + side, 0:HEAD_DIM, :] = turned[side * HEAD_DIM : (side + 1) * HEAD_DIM, :]
    over = sum(ends[1:], ends[0])
    edge = jnp.exp(over - cum_ref[0:8, :]) * step[0:8, :]
    left = lax.broadcasted_iota(jnp.int32, (8, LANES), 1) < HEAD_DIM
    few = CONV - 1
    for h in range(HEADS):
        cols = slice(h // 2 * LANES, (h // 2 + 1) * LANES)
        own, tail = own_ref[:, cols], tail_ref[:, cols]
        if h % 2:
            own = pltpu.roll(own, HEAD_DIM, 1)
        else:
            tail = pltpu.roll(tail, HEAD_DIM, 1)
        pad_ref[h, 0:1, :] = halves(jnp.broadcast_to(over[:, h : h + 1], (8, LANES)))[0:1, :]
        pad_ref[h, 1 : 1 + few, :] = jnp.where(left, own, tail)[0:few, :]
        pad_ref[h, 4 : 4 + few, :] = own_ref[0:few, INNER : INNER + STATE]
        pad_ref[h, 7 : 7 + few, :] = tail_ref[0:few, INNER : INNER + STATE]
        broad = jnp.broadcast_to(edge[:, h : h + 1], (8, LANES))
        pad_ref[h, 10 : 10 + few, :] = halves(broad)[0:few, :]
        pad_ref[h, 13 : 13 + few, :] = tail_ref[0:few, INNER + STATE :]
        send_ref[h, HEAD_DIM:, :] = pad_ref[h].astype(BF16)
    keep_ref[...] = send_ref[pl.ds(core * HALF, HALF)]
    give_ref[...] = send_ref[pl.ds((1 - core) * HALF, HALF)]


def halves(value):
    left = lax.broadcasted_iota(jnp.int32, value.shape, 1) < HEAD_DIM
    high = value.astype(BF16).astype(F32)
    return jnp.where(left, high, value - high)


def joined(value):
    return value + pltpu.roll(value, HEAD_DIM, 1)


def chip_kernel(keep_ref, got_ref, send_ref, pair_ref):
    parts, padded, _ = send_ref.shape
    part_rows = padded - PAD
    core = core_index()
    pair_ref[core] = keep_ref[...]
    pair_ref[1 - core] = got_ref[...]
    row = lax.broadcasted_iota(jnp.int32, (PAD, LANES), 0)
    left = lax.broadcasted_iota(jnp.int32, (PAD, LANES), 1) < HEAD_DIM
    for h in range(HALF):
        one = pair_ref[0, h, HEAD_DIM:, :].astype(F32)
        two = pair_ref[1, h, HEAD_DIM:, :].astype(F32)
        one_sum, two_sum = joined(one), joined(two)
        decay = jnp.exp(two_sum[0:1, :])
        state = decay * pair_ref[0, h, 0:HEAD_DIM, :].astype(F32) + pair_ref[
            1, h, 0:HEAD_DIM, :
        ].astype(F32)
        state = state.astype(BF16)
        exact = halves(jnp.where(row == 0, one_sum + two_sum, one_sum * decay))
        for k in range(HEAD_DIM // part_rows):
            at = k * part_rows
            own = pltpu.roll(jnp.where(left, one, 0.0), LANES - at, 1) if at else one
            pad = jnp.where(row < 4, jnp.where(left, own, two), jnp.where(row < 7, one, two))
            pad = jnp.where((row == 0) | ((row >= 10) & (row < 13)), exact, pad)
            part = h * (HEAD_DIM // part_rows) + k
            send_ref[part, 0:part_rows, :] = state[at : at + part_rows, :]
            send_ref[part, part_rows:, :] = pad.astype(BF16)


def enter_kernel(keep_ref, got_ref, back_ref, mine_ref, give_ref, pair_ref, enter_ref, pad_ref):
    parts, padded, _ = back_ref.shape
    part_rows = padded - PAD
    each = HEAD_DIM // part_rows
    core = core_index()
    pair_ref[core] = keep_ref[...]
    pair_ref[1 - core] = got_ref[...]
    few = lax.broadcasted_iota(jnp.int32, (8, LANES), 0) < CONV - 1
    for h in range(HALF):
        pad = back_ref[h * each, part_rows:, :]
        pad_ref[2 * h] = pad.astype(F32)
        pad_ref[2 * h + 1] = pair_ref[0, h, HEAD_DIM:, :].astype(F32)
    for h in range(HALF):
        last, mine = 2 * h, 2 * h + 1
        entering = jnp.concatenate(
            [back_ref[h * each + k, 0:part_rows, :] for k in range(each)], axis=0
        )
        values = silu(pad_ref[mine, 1:9, :] + pltpu.roll(pad_ref[last, 1:9, :], HEAD_DIM, 1))
        in_map = silu(pad_ref[mine, 4:12, :] + pad_ref[last, 7:15, :])
        edge = joined(pad_ref[mine, 8:16, :])
        edge = pltpu.roll(edge, 6, 0)
        scaled = jnp.where(few, values.astype(BF16).astype(F32) * edge, 0.0)
        added = dot(scaled, jnp.where(few, in_map, 0.0), ((0,), (0,)))[0:HEAD_DIM, :]
        decay = jnp.exp(joined(pad_ref[mine, 0:8, :])[0:1, :])
        after = decay * entering.astype(F32) + pair_ref[0, h, 0:HEAD_DIM, :].astype(F32) + added
        pad = back_ref[h * each, part_rows:, :]
        enter_ref[0, h, 0:HEAD_DIM, :] = entering
        enter_ref[1, h, 0:HEAD_DIM, :] = after.astype(BF16)
        enter_ref[0, h, HEAD_DIM:, :] = pad
        enter_ref[1, h, HEAD_DIM:, :] = pad
    mine_ref[...] = enter_ref[core]
    give_ref[...] = enter_ref[1 - core]


def silu(x):
    return x * jax.nn.sigmoid(x)


def scan_kernel(got_ref, *rest):
    back_ref, pad_ref = rest[-2:]
    parts, padded, _ = got_ref.shape
    part_rows = padded - PAD
    rows = slice(0, part_rows)
    offset = lax.axis_index("frames") // 2 * part_rows % HEAD_DIM
    few = lax.broadcasted_iota(jnp.int32, (8, LANES), 0) < CONV - 1
    left = lax.broadcasted_iota(jnp.int32, (8, LANES), 1) < HEAD_DIM
    pad_ref[0:PAD, :] = jnp.zeros((PAD, LANES), F32)
    pad_ref[(parts + 1) * PAD :, :] = jnp.zeros((8, LANES), F32)
    for d in range(parts):
        pad_ref[(d + 1) * PAD : (d + 2) * PAD, :] = got_ref[d, part_rows:, :].astype(F32)
    carry = jnp.zeros((part_rows, LANES), F32)
    for d in range(parts):
        back_ref[d, rows, :] = carry.astype(BF16)
        back_ref[d, part_rows:, :] = pad_ref[d * PAD : (d + 1) * PAD, :].astype(BF16)
        last, mine = d * PAD, (d + 1) * PAD
        decay = pad_ref[mine : mine + 1, :]
        decay = jnp.exp(decay + pltpu.roll(decay, HEAD_DIM, 1))
        from_tail = pltpu.roll(pad_ref[last + 1 : last + 9, :], HEAD_DIM, 1)
        if part_rows < HEAD_DIM:
            from_tail = pltpu.roll(jnp.where(left, from_tail, 0.0), (LANES - offset) % LANES, 1)
        values = silu(pad_ref[mine + 1 : mine + 9, :] + from_tail)
        in_map = silu(pad_ref[mine + 4 : mine + 12, :] + pad_ref[last + 7 : last + 15, :])
        edge = pad_ref[mine + 10 : mine + 18, :]
        edge = edge + pltpu.roll(edge, HEAD_DIM, 1)
        scaled = jnp.where(few, values.astype(BF16).astype(F32) * edge, 0.0)
        in_map = jnp.where(few, in_map, 0.0)
        added = dot(scaled, in_map, ((0,), (0,)))
        carry = decay * carry + (got_ref[d, rows, :].astype(F32) + added[rows, :])


def mixed_values(affinity, cum, shifted, values, skip, pair):
    q_pos = lax.broadcasted_iota(jnp.int32, (SPAN, SPAN), 0)
    s_pos = lax.broadcasted_iota(jnp.int32, (SPAN, SPAN), 1)
    lower = q_pos >= s_pos
    left = lax.broadcasted_iota(jnp.int32, (SPAN, LANES), 1) < HEAD_DIM
    zero = jnp.zeros((SPAN, LANES), BF16)
    mixing = []
    for h in (2 * pair, 2 * pair + 1):
        gap = cum[:, h : h + 1] - shifted[h : h + 1, :]
        mixing.append(jnp.where(lower, affinity * jnp.exp(gap), 0.0).astype(BF16))
    both = jnp.concatenate(mixing, axis=1)
    stacked = jnp.concatenate([jnp.where(left, values, zero), jnp.where(left, zero, values)], axis=0)
    return dot(both, stacked) + skip * values.astype(F32)


def later_kernel(layer, act_ref, cum_ref, shifted_ref, skip_ref, sel_ref, y_ref, decay_ref):
    skip = spread_row(skip_ref[layer : layer + 1, :], sel_ref[...])
    for b in range(1, act_ref.shape[0] // SPAN):
        r = slice(b * SPAN, (b + 1) * SPAN)
        maps = act_ref[r, INNER:]
        affinity = dot(maps[:, STATE:], maps[:, :STATE], ((1,), (1,)))
        cum, shifted = cum_ref[r, :], shifted_ref[:, r]
        decays = split(jnp.exp(cum))
        for c in range(0, INNER, 256):
            decay_ref[(b - 1) * SPAN : b * SPAN, c : c + 256] = dot(decays, sel_ref[:, c : c + 256])
        for pair in range(HEADS // 2):
            cols = slice(pair * LANES, (pair + 1) * LANES)
            y_ref[(b - 1) * SPAN : b * SPAN, cols] = mixed_values(
                affinity, cum, shifted, act_ref[r, cols], skip[:, cols], pair
            )


def gate_kernel(layer, u_ref, w_ref, cum_ref, sel_ref, gate_ref, wide_ref):
    chunk = 256
    before = jnp.zeros((1, HEADS), F32)
    scales = []
    for b in range(u_ref.shape[0] // SPAN):
        cum = cum_ref[b * SPAN : (b + 1) * SPAN, :]
        scales.append(jnp.exp(cum + before))
        before = before + cum[SPAN - 1 : SPAN, :]
    scales = split(jnp.concatenate(scales, axis=0))
    for c in range(0, INNER, chunk):
        cols = slice(c, c + chunk)
        wide_ref[:, cols] = dot(scales, sel_ref[:, cols])
        gate_ref[:, cols] = silu(dot(u_ref[...], w_ref[layer, :, cols]).astype(BF16).astype(F32))


def finish_kernel(
    layer,
    gate_ref,
    wide_ref,
    later_ref,
    decay_ref,
    act_ref,
    own_ref,
    cum_ref,
    shifted_ref,
    edge_ref,
    state_ref,
    skip_ref,
    sel_ref,
    mine_ref,
    other_ref,
    resid_ref,
    wo_ref,
    gain_ref,
    mods_ref,
    *rest,
):
    hidden_ref, a_ref, first_ref, y_ref, normed_ref, enter_ref = rest[-6:]
    rows = gate_ref.shape[0]
    core = core_index()
    enter_ref[pl.ds(core * HALF, HALF)] = mine_ref[...]
    enter_ref[pl.ds((1 - core) * HALF, HALF)] = other_ref[...]
    start = (1 - core).astype(F32)
    sel = sel_ref[...]
    lane = lax.broadcasted_iota(jnp.int32, (SPAN, LANES), 1)
    left = lane < HEAD_DIM
    few = lax.broadcasted_iota(jnp.int32, (TAIL, LANES), 0) < CONV - 1
    nothing = jnp.zeros((TAIL - 8, LANES), F32)

    def fixed(cols, tail):
        total = jnp.concatenate([own_ref[:, cols] + start * tail[0:8, :], nothing], axis=0)
        first_ref[:, cols] = jnp.where(
            few, silu(total), act_ref[0:TAIL, cols].astype(F32)
        ).astype(BF16)

    for pair in range(HEADS // 2):
        pads = [
            enter_ref[h, HEAD_DIM:, :].astype(F32)
            for h in (2 * pair, 2 * pair + 1)
        ]
        tail = jnp.where(left[0:PAD], pltpu.roll(pads[0], HEAD_DIM, 1), pads[1])
        fixed(slice(pair * LANES, (pair + 1) * LANES), pltpu.roll(tail, PAD - 1, 0))
    common = enter_ref[0, HEAD_DIM:, :].astype(F32)
    fixed(slice(INNER, INNER + STATE), pltpu.roll(common, PAD - 7, 0))
    fixed(slice(INNER + STATE, INNER + 2 * STATE), pltpu.roll(common, PAD - 13, 0))

    def acts(b, cols):
        if b:
            return act_ref[b * SPAN : (b + 1) * SPAN, cols]
        return jnp.concatenate([first_ref[:, cols], act_ref[TAIL:SPAN, cols]], axis=0)

    first_tokens = lax.broadcasted_iota(jnp.int32, (TAIL, HEADS), 0) < CONV - 1
    early_scale = split(jnp.where(first_tokens, edge_ref[...], 0.0) * start)
    early_map = first_ref[:, INNER : INNER + STATE]
    spans = rows // SPAN
    out_maps = [acts(b, slice(INNER + STATE, INNER + 2 * STATE)) for b in range(spans)]
    out_map = jnp.concatenate(out_maps, axis=0)
    decayed = [jnp.ones((1, INNER), F32)]
    for b in range(1, spans - 1):
        end = (b + 1) * SPAN - 1
        decayed.append(decayed[-1] * spread_row(jnp.exp(cum_ref[end : end + 1, :]), sel))
    chunk = 256
    for c in range(0, INNER, chunk):
        cols = slice(c, c + chunk)
        entering = jnp.concatenate(
            [enter_ref[h, 0:HEAD_DIM, :] for h in range(c // HEAD_DIM, (c + chunk) // HEAD_DIM)],
            axis=0,
        )
        y_ref[:, cols] = dot(out_map, entering, ((1,), (1,))) * wide_ref[:, cols]
    early = (first_ref[:, 0:INNER].astype(F32) * dot(early_scale, sel)).astype(BF16)
    late = dot(early_map, early, ((0,), (0,)))
    for b in range(1, spans):
        r, own = slice(b * SPAN, (b + 1) * SPAN), slice((b - 1) * SPAN, b * SPAN)
        state = late if b == 1 else decayed[b - 1] * late
        state = state_ref[(b - 1) * STATE : b * STATE, :] + state
        within = later_ref[own, :] + dot(out_maps[b], state.astype(BF16)) * decay_ref[own, :]
        y_ref[r, :] = (y_ref[r, :] + within) * gate_ref[r, :]

    skip = spread_row(skip_ref[layer : layer + 1, :], sel)
    r = slice(0, SPAN)
    affinity = dot(out_maps[0], acts(0, slice(INNER, INNER + STATE)), ((1,), (1,)))
    cum, shifted = cum_ref[r, :], shifted_ref[:, r]
    for pair in range(HEADS // 2):
        cols = slice(pair * LANES, (pair + 1) * LANES)
        y = mixed_values(affinity, cum, shifted, acts(0, cols), skip[:, cols], pair)
        y_ref[r, cols] = (y + y_ref[r, cols]) * gate_ref[r, cols]

    row = lax.broadcasted_iota(jnp.int32, (chunk, chunk), 0) // HEAD_DIM
    col = lax.broadcasted_iota(jnp.int32, (chunk, chunk), 1) // HEAD_DIM
    same = jnp.where(row == col, 1.0 / HEAD_DIM, 0.0).astype(BF16)
    for c in range(0, INNER, chunk):
        cols = slice(c, c + chunk)
        total = y_ref[:, cols]
        square = total * total
        high = square.astype(BF16)
        low = (square - high.astype(F32)).astype(BF16)
        mean = dot(high, same) + dot(low, same)
        gain = gain_ref[layer : layer + 1, cols]
        normed_ref[:, cols] = (total * lax.rsqrt(mean + HEAD_EPS) * gain).astype(BF16)
    hidden = resid_ref[...].astype(F32) + dot(normed_ref[...], wo_ref[layer])
    hidden_ref[...] = hidden
    a_ref[...] = rms_mod(hidden, mods_ref[layer, 2:3, :], mods_ref[layer, 3:4, :])


def partial_attention(q_ref, seen, kv, half, r, k_rows, done):
    left = lax.broadcasted_iota(jnp.int32, (half, LANES), 1) < HEAD_DIM
    one = jnp.ones((k_rows.stop - k_rows.start, LANES), BF16)
    zero = jnp.zeros((half, LANES), BF16)
    seen = jnp.concatenate([seen, seen], axis=0)
    together = 4
    for group in range(0, ATT_HEADS // 2, together):
        columns = [slice(p * LANES, (p + 1) * LANES) for p in range(group, group + together)]
        scores = []
        for cols in columns:
            query = q_ref[r, cols]
            sides = jnp.concatenate(
                [jnp.where(left, query, zero), jnp.where(left, zero, query)], axis=0
            )
            scores.append(dot(sides, kv[k_rows, cols], ((1,), (1,))) + seen)
        tops = [jnp.max(s, axis=-1, keepdims=True) for s in scores]
        weights = [jnp.exp(s - t).astype(BF16) for s, t in zip(scores, tops)]
        for cols, weight, top in zip(columns, weights, tops):
            values = kv[k_rows, ATTN + cols.start : ATTN + cols.stop]
            both = dot(weight, jnp.concatenate([values, one], axis=1))
            number = jnp.where(left, both[:half, :LANES], both[half:, :LANES])
            total = jnp.where(left, both[:half, LANES:], both[half:, LANES:])
            done(cols, number, total, jnp.where(left, top[:half], top[half:]))


def memory_kernel(
    layer, reach_ref, a_ref, wq_ref, wm_ref, q_ref, number_ref, total_ref, top_ref, seen_ref, kv_ref
):
    rows = a_ref.shape[0]
    half = rows // 2
    a = a_ref[...]
    tok_frame = rows // WINDOW
    key_frame = lax.broadcasted_iota(jnp.int32, (tok_frame, 2 * rows), 1) // tok_frame
    first = WINDOW - lax.axis_index("frames") * WINDOW
    for f in range(WINDOW):
        low = jnp.maximum(first, f + WINDOW - reach_ref[f])
        seen = (key_frame >= low) & (key_frame <= f + WINDOW)
        seen_ref[f * tok_frame : (f + 1) * tok_frame, :] = jnp.where(seen, 0.0, -1e30)
    q_ref[...] = (dot(a, wq_ref[layer]).astype(BF16).astype(F32) * HEAD_DIM**-0.5).astype(BF16)
    kv_ref[...] = dot(a, wm_ref[layer]).astype(BF16)
    for part in range(2):
        r = slice(part * half, (part + 1) * half)
        k_rows = slice(0, (part + 1) * half)

        def done(cols, number, total, top):
            number_ref[r, cols] = number
            total_ref[r, cols] = total
            top_ref[r, cols] = top

        seen = seen_ref[r, rows : rows + k_rows.stop]
        partial_attention(q_ref, seen, kv_ref, half, r, k_rows, done)


def attend_kernel(
    layer,
    last,
    q_ref,
    number_ref,
    total_ref,
    top_ref,
    seen_ref,
    prev_ref,
    wm_ref,
    merge_ref,
    hidden_ref,
    mods_ref,
    *rest,
):
    if last:
        resid_ref, kv_ref, out_ref = rest
    else:
        resid_ref, u_ref, tail_ref, kv_ref, out_ref = rest
    rows = q_ref.shape[0]
    half = rows // 2
    kv_ref[...] = dot(prev_ref[...], wm_ref[layer]).astype(BF16)
    for part in range(2):
        r = slice(part * half, (part + 1) * half)
        k_rows = slice(part * half, rows)

        def done(cols, number, total, top):
            top_own = top_ref[r, cols]
            highest = jnp.maximum(top, top_own)
            mine, own = jnp.exp(top - highest), jnp.exp(top_own - highest)
            number = number * mine + number_ref[r, cols] * own
            total = total * mine + total_ref[r, cols] * own
            out_ref[r, cols] = (number / total).astype(BF16)

        partial_attention(q_ref, seen_ref[r, k_rows], kv_ref, half, r, k_rows, done)
    resid = hidden_ref[...] + dot(out_ref[...], merge_ref[layer])
    resid_ref[...] = resid
    if not last:
        u = rms_mod(resid, mods_ref[layer + 1, 0:1, :], mods_ref[layer + 1, 1:2, :])
        u_ref[...] = u
        tail_ref[...] = u[rows - TAIL :]


WHOLE = pl.BlockSpec(memory_space=pltpu.VMEM)
SCALARS = pl.BlockSpec(memory_space=pltpu.SMEM)


def run(kernel, operands, outs, scratch=(), name=None, flops=0, scalars=()):
    moved = sum(o.size * o.dtype.itemsize for o in list(operands) + list(outs))
    return pl.pallas_call(
        kernel,
        in_specs=[SCALARS] * len(scalars) + [WHOLE] * len(operands),
        out_specs=[WHOLE] * len(outs),
        out_shape=list(outs),
        scratch_shapes=list(scratch),
        compiler_params=pltpu.CompilerParams(vmem_limit_bytes=20 * 1024 * 1024),
        cost_estimate=pl.CostEstimate(flops=flops, bytes_accessed=moved, transcendentals=0),
        name=name,
    )(*scalars, *operands)


def shape(dims, dtype):
    return jax.ShapeDtypeStruct(dims, dtype)


def swapped(value, axis):
    count = lax.axis_size(axis)
    return lax.ppermute(value, axis, [(i, i ^ 1) for i in range(count)])


def over_chips(value, axis):
    count = lax.axis_size(axis)
    groups = [list(range(core, count, 2)) for core in range(2)]
    return lax.all_to_all(value, axis, 0, 0, axis_index_groups=groups)


def from_behind(value, axis):
    count = lax.axis_size(axis)
    return lax.ppermute(value, axis, [(i, i + 1) for i in range(count - 1)])


def shards(
    latents,
    timestep,
    lookback,
    modulation,
    input_weight,
    step_weight,
    conv_weight,
    step_bias,
    decay_log,
    skip_gain,
    norm_gain,
    output_weight,
    query_weight,
    memory_weight,
    merge_weight,
):
    frames_dev, tok_frame, width = latents.shape
    rows = frames_dev * tok_frame
    spans = rows // SPAN
    parts = lax.axis_size("frames") // 2
    part_rows = HALF * HEAD_DIM // parts
    mixed = INNER + 2 * STATE
    step_weight = jnp.swapaxes(step_weight, 1, 2)
    step_bias = jnp.swapaxes(step_bias, 1, 2)
    resid = latents.reshape(rows, width)
    (sel,) = run(
        select_kernel, (), [shape((2 * HEADS, INNER), BF16)], name="select", flops=OPENING
    )
    u, tail, mods, bias = run(
        first_kernel,
        (sel, resid, modulation, step_bias),
        [
            shape((rows, width), BF16),
            shape((TAIL, width), BF16),
            shape((LAYERS,) + modulation.shape[2:], F32),
            shape((LAYERS, 8, HEADS), F32),
        ],
        name="first",
        flops=OPENING,
        scalars=(timestep,),
    )
    for layer in range(LAYERS):
        before = swapped(tail, "frames")
        act, own, cum, shifted, edge, state, keep, give = run(
            functools.partial(local_kernel, layer),
            (u, before, input_weight, step_weight, conv_weight, bias, decay_log, sel),
            [
                shape((rows, mixed), BF16),
                shape((8, mixed), F32),
                shape((rows, HEADS), F32),
                shape((HEADS, rows), F32),
                shape((TAIL, HEADS), F32),
                shape((max(spans - 1, 1) * STATE, INNER), F32),
                shape((HALF, BLOCK, LANES), BF16),
                shape((HALF, BLOCK, LANES), BF16),
            ],
            [
                pltpu.VMEM((2, rows + 2 * TAIL, 256), F32),
                pltpu.VMEM((8, mixed), F32),
                pltpu.VMEM((HEADS, PAD, LANES), F32),
                pltpu.VMEM((HEADS, BLOCK, LANES), BF16),
                pltpu.VMEM((rows, INNER), BF16),
            ],
            name="local",
            flops=2 * rows * width * mixed,
        )
        got = swapped(give, "frames")
        later, decays = run(
            functools.partial(later_kernel, layer),
            (act, cum, shifted, skip_gain, sel),
            [shape((max(spans - 1, 1) * SPAN, INNER), F32)] * 2,
            name="later",
            flops=2 * rows * SPAN * INNER,
        )
        got, later, decays = lax.optimization_barrier((got, later, decays))
        (send,) = run(
            chip_kernel,
            (keep, got),
            [shape((parts, part_rows + PAD, LANES), BF16)],
            [pltpu.VMEM((2, HALF, BLOCK, LANES), BF16)],
            name="chip",
        )
        (back,) = run(
            scan_kernel,
            (over_chips(send, "frames"),)
            + (() if layer else (output_weight, norm_gain, query_weight, memory_weight, merge_weight)),
            [shape(send.shape, BF16)],
            [pltpu.VMEM(((parts + 1) * PAD + 8, LANES), F32)],
            name="scan",
        )
        mine, give = run(
            enter_kernel,
            (keep, got, over_chips(back, "frames")),
            [shape(keep.shape, BF16)] * 2,
            [
                pltpu.VMEM((2, HALF, BLOCK, LANES), BF16),
                pltpu.VMEM((2, HALF, BLOCK, LANES), BF16),
                pltpu.VMEM((HEADS, PAD, LANES), F32),
            ],
            name="enter",
        )
        give, u = lax.optimization_barrier((give, u))
        other = swapped(give, "frames")
        gate, wide = run(
            functools.partial(gate_kernel, layer),
            (u, input_weight, cum, sel),
            [shape((rows, INNER), F32)] * 2,
            name="gate",
            flops=2 * rows * width * INNER,
        )
        hidden, a = run(
            functools.partial(finish_kernel, layer),
            (gate, wide, later, decays, act, own, cum, shifted, edge, state, skip_gain, sel)
            + (mine, other, resid, output_weight, norm_gain, mods),
            [shape((rows, width), F32), shape((rows, width), BF16)],
            [
                pltpu.VMEM((TAIL, mixed), BF16),
                pltpu.VMEM((rows, INNER), F32),
                pltpu.VMEM((rows, INNER), BF16),
                pltpu.VMEM((HEADS, BLOCK, LANES), BF16),
            ],
            name="finish",
        )
        prev = from_behind(a, "frames")
        q, number, total, top, seen = run(
            functools.partial(memory_kernel, layer),
            (a, query_weight, memory_weight),
            [shape((rows, ATTN), BF16)]
            + [shape((rows, ATTN), F32)] * 3
            + [shape((rows, 2 * rows), F32)],
            [pltpu.VMEM((rows, 2 * ATTN), BF16)],
            name="memory",
            scalars=(lookback,),
            flops=2 * rows * width * 3 * ATTN,
        )
        last = layer == LAYERS - 1
        outs = [shape((rows, width), F32)]
        if not last:
            outs += [shape((rows, width), BF16), shape((TAIL, width), BF16)]
        result = run(
            functools.partial(attend_kernel, layer, last),
            (q, number, total, top, seen, prev, memory_weight, merge_weight, hidden, mods),
            outs,
            [pltpu.VMEM((rows, 2 * ATTN), BF16), pltpu.VMEM((rows, ATTN), BF16)],
            name="attend",
        )
        resid = result[0]
        if not last:
            u, tail = result[1:]
    return resid.reshape(latents.shape)


def solution(mesh):
    sharded = P(("groups", "frames"))
    return jax.shard_map(
        shards,
        mesh=mesh,
        in_specs=(P(("groups", "frames"), None, None), sharded, sharded) + (P(),) * 12,
        out_specs=P(("groups", "frames"), None, None),
        check_vma=False,
    )
```

```python
import functools

import jax
import jax.numpy as jnp
from jax import lax
from jax.experimental import pallas as pl
from jax.experimental.pallas import tpu as pltpu
from jax.sharding import PartitionSpec as P

HEADS = 16
HEAD_DIM = 64
STATE = 128
ATT_HEADS = 8
LAYERS = 2
CONV = 4
SPAN = 128
WINDOW = 8
EPS = 1e-06
HEAD_EPS = 1e-05
INNER = HEADS * HEAD_DIM
ATTN = ATT_HEADS * HEAD_DIM
PAD = 16
BLOCK = HEAD_DIM + PAD
HALF = HEADS // 2
LANES = 128
TAIL = 16
F32 = jnp.float32
OPENING = 4 * 10**9
BF16 = jnp.bfloat16


def dot(a, b, dims=((1,), (0,)), precision=None):
    return lax.dot_general(a, b, (dims, ((), ())), precision=precision, preferred_element_type=F32)


def rms_mod(x, shift, scale):
    normed = x * lax.rsqrt(jnp.mean(x * x, axis=-1, keepdims=True) + EPS)
    return (normed * (1.0 + scale) + shift).astype(BF16)


def split(per_head):
    high = per_head.astype(BF16)
    low = (per_head - high.astype(F32)).astype(BF16)
    return jnp.concatenate([high, low], axis=1)


def spread(per_head, sel):
    return dot(split(per_head), sel)


def spread_row(per_head, sel):
    return spread(jnp.broadcast_to(per_head, (16, HEADS)), sel)[0:1, :]


def select_kernel(sel_ref):
    row = lax.broadcasted_iota(jnp.int32, sel_ref.shape, 0) % HEADS
    head = lax.broadcasted_iota(jnp.int32, sel_ref.shape, 1) // HEAD_DIM
    sel_ref[...] = jnp.where(row == head, 1.0, 0.0).astype(BF16)


def first_kernel(
    step_ref,
    sel_ref,
    x_ref,
    all_mods_ref,
    all_bias_ref,
    u_ref,
    tail_ref,
    mods_ref,
    bias_ref,
):
    rows, width = u_ref.shape
    step = step_ref[0]
    for layer in range(LAYERS):
        mods_ref[layer] = all_mods_ref[layer, step].astype(F32)
    u = rms_mod(x_ref[...].astype(F32), mods_ref[0, 0:1, :], mods_ref[0, 1:2, :])
    u_ref[...] = u
    tail_ref[...] = u[rows - TAIL :]
    chosen = lax.broadcasted_iota(jnp.int32, (8, all_bias_ref.shape[-1]), 1) == step
    chosen = jnp.where(chosen, 1.0, 0.0).astype(F32)
    for layer in range(LAYERS):
        bias_ref[layer] = dot(
            chosen, all_bias_ref[layer], ((1,), (1,)), precision=lax.Precision.HIGHEST
        )


def core_index():
    return lax.axis_index("frames") % 2


def local_kernel(
    layer,
    u_ref,
    before_ref,
    w_ref,
    sw_ref,
    conv_ref,
    bias_ref,
    decay_ref,
    sel_ref,
    act_ref,
    own_ref,
    cum_ref,
    shifted_ref,
    edge_ref,
    state_ref,
    keep_ref,
    give_ref,
    ext_ref,
    tail_ref,
    pad_ref,
    send_ref,
    scaled_ref,
):
    rows = u_ref.shape[0]
    u = u_ref[...]
    sel = sel_ref[...]
    core = core_index()
    tail_rows = before_ref[...].astype(F32) * core.astype(F32)
    tail_rows = tail_rows.astype(BF16)
    raw = dot(u, sw_ref[layer], ((1,), (1,))) + bias_ref[layer, 0:1, :]
    step = jnp.maximum(raw, 0.0) + jnp.log1p(jnp.exp(-jnp.abs(raw)))
    log_decay = -jnp.exp(decay_ref[layer : layer + 1, :]) * step
    log_step = jnp.log(step)
    q_pos = lax.broadcasted_iota(jnp.int32, (SPAN, SPAN), 0)
    s_pos = lax.broadcasted_iota(jnp.int32, (SPAN, SPAN), 1)
    lower = jnp.where(q_pos >= s_pos, 1.0, 0.0).astype(F32)
    whole_tokens = lax.broadcasted_iota(jnp.int32, (SPAN, HEADS), 0) >= (CONV - 1) * (1 - core)
    ends, edges = [], []
    for b in range(rows // SPAN):
        r = slice(b * SPAN, (b + 1) * SPAN)
        cum = dot(lower, log_decay[r], precision=lax.Precision.HIGHEST)
        end = cum[SPAN - 1 : SPAN, :]
        cum_ref[r, :] = cum
        shifted_ref[:, r] = (cum - log_step[r]).T
        edge = jnp.exp(end - cum) * step[r]
        if b == 0:
            edge_ref[...] = edge[0:TAIL, :]
            edge = jnp.where(whole_tokens, edge, 0.0)
        ends.append(end)
        edges.append(edge)

    edges = split(jnp.concatenate(edges, axis=0))
    chunk = 256
    for slot in range(2):
        ext_ref[slot, TAIL + rows :, :] = jnp.zeros((TAIL, chunk), F32)
    for c in [INNER] + list(range(0, INNER, chunk)):
        w = w_ref[layer, :, INNER + c : INNER + c + chunk]
        slot = c // chunk % 2
        ext_ref[slot, 0:TAIL, :] = dot(tail_rows, w).astype(BF16).astype(F32)
        ext_ref[slot, TAIL : TAIL + rows, :] = dot(u, w).astype(BF16).astype(F32)
        total, after = None, None
        for k in range(CONV):
            start = TAIL - (CONV - 1) + k
            taps = conv_ref[layer, k : k + 1, c : c + chunk]
            term = taps * ext_ref[slot, start : start + rows, :]
            next_term = taps * ext_ref[slot, start + rows : start + rows + 8, :]
            total = term if total is None else total + term
            after = next_term if after is None else after + next_term
        act = (total * jax.nn.sigmoid(total)).astype(BF16)
        act_ref[:, c : c + chunk] = act
        if c < INNER:
            scale = dot(edges, sel_ref[:, c : c + chunk])
            scaled_ref[:, c : c + chunk] = (act.astype(F32) * scale).astype(BF16)
        own_ref[:, c : c + chunk] = total[0:8, :]
        tail_ref[:, c : c + chunk] = after

    state = None
    for b in range(rows // SPAN):
        r = slice(b * SPAN, (b + 1) * SPAN)
        in_map = act_ref[r, INNER : INNER + STATE]
        term = dot(in_map, scaled_ref[r, :], ((0,), (0,)))
        if state is None:
            state = term
        else:
            state_ref[(b - 1) * STATE : b * STATE, :] = state
            state = spread_row(jnp.exp(ends[b]), sel) * state + term

    for pair in range(HEADS // 2):
        turned = state[:, pair * LANES : (pair + 1) * LANES].T.astype(BF16)
        for side in range(2):
            send_ref[2 * pair + side, 0:HEAD_DIM, :] = turned[side * HEAD_DIM : (side + 1) * HEAD_DIM, :]
    over = sum(ends[1:], ends[0])
    edge = jnp.exp(over - cum_ref[0:8, :]) * step[0:8, :]
    left = lax.broadcasted_iota(jnp.int32, (8, LANES), 1) < HEAD_DIM
    few = CONV - 1
    for h in range(HEADS):
        cols = slice(h // 2 * LANES, (h // 2 + 1) * LANES)
        own, tail = own_ref[:, cols], tail_ref[:, cols]
        if h % 2:
            own = pltpu.roll(own, HEAD_DIM, 1)
        else:
            tail = pltpu.roll(tail, HEAD_DIM, 1)
        pad_ref[h, 0:1, :] = halves(jnp.broadcast_to(over[:, h : h + 1], (8, LANES)))[0:1, :]
        pad_ref[h, 1 : 1 + few, :] = jnp.where(left, own, tail)[0:few, :]
        pad_ref[h, 4 : 4 + few, :] = own_ref[0:few, INNER : INNER + STATE]
        pad_ref[h, 7 : 7 + few, :] = tail_ref[0:few, INNER : INNER + STATE]
        broad = jnp.broadcast_to(edge[:, h : h + 1], (8, LANES))
        pad_ref[h, 10 : 10 + few, :] = halves(broad)[0:few, :]
        pad_ref[h, 13 : 13 + few, :] = tail_ref[0:few, INNER + STATE :]
        send_ref[h, HEAD_DIM:, :] = pad_ref[h].astype(BF16)
    keep_ref[...] = send_ref[pl.ds(core * HALF, HALF)]
    give_ref[...] = send_ref[pl.ds((1 - core) * HALF, HALF)]


def halves(value):
    left = lax.broadcasted_iota(jnp.int32, value.shape, 1) < HEAD_DIM
    high = value.astype(BF16).astype(F32)
    return jnp.where(left, high, value - high)


def joined(value):
    return value + pltpu.roll(value, HEAD_DIM, 1)


def chip_kernel(keep_ref, got_ref, send_ref, pair_ref):
    parts, padded, _ = send_ref.shape
    part_rows = padded - PAD
    core = core_index()
    pair_ref[core] = keep_ref[...]
    pair_ref[1 - core] = got_ref[...]
    row = lax.broadcasted_iota(jnp.int32, (PAD, LANES), 0)
    left = lax.broadcasted_iota(jnp.int32, (PAD, LANES), 1) < HEAD_DIM
    for h in range(HALF):
        one = pair_ref[0, h, HEAD_DIM:, :].astype(F32)
        two = pair_ref[1, h, HEAD_DIM:, :].astype(F32)
        one_sum, two_sum = joined(one), joined(two)
        decay = jnp.exp(two_sum[0:1, :])
        state = decay * pair_ref[0, h, 0:HEAD_DIM, :].astype(F32) + pair_ref[
            1, h, 0:HEAD_DIM, :
        ].astype(F32)
        state = state.astype(BF16)
        exact = halves(jnp.where(row == 0, one_sum + two_sum, one_sum * decay))
        for k in range(HEAD_DIM // part_rows):
            at = k * part_rows
            own = pltpu.roll(jnp.where(left, one, 0.0), LANES - at, 1) if at else one
            pad = jnp.where(row < 4, jnp.where(left, own, two), jnp.where(row < 7, one, two))
            pad = jnp.where((row == 0) | ((row >= 10) & (row < 13)), exact, pad)
            part = h * (HEAD_DIM // part_rows) + k
            send_ref[part, 0:part_rows, :] = state[at : at + part_rows, :]
            send_ref[part, part_rows:, :] = pad.astype(BF16)


def enter_kernel(keep_ref, got_ref, back_ref, mine_ref, give_ref, pair_ref, enter_ref, pad_ref):
    parts, padded, _ = back_ref.shape
    part_rows = padded - PAD
    each = HEAD_DIM // part_rows
    core = core_index()
    pair_ref[core] = keep_ref[...]
    pair_ref[1 - core] = got_ref[...]
    few = lax.broadcasted_iota(jnp.int32, (8, LANES), 0) < CONV - 1
    for h in range(HALF):
        pad = back_ref[h * each, part_rows:, :]
        pad_ref[2 * h] = pad.astype(F32)
        pad_ref[2 * h + 1] = pair_ref[0, h, HEAD_DIM:, :].astype(F32)
    for h in range(HALF):
        last, mine = 2 * h, 2 * h + 1
        entering = jnp.concatenate(
            [back_ref[h * each + k, 0:part_rows, :] for k in range(each)], axis=0
        )
        values = silu(pad_ref[mine, 1:9, :] + pltpu.roll(pad_ref[last, 1:9, :], HEAD_DIM, 1))
        in_map = silu(pad_ref[mine, 4:12, :] + pad_ref[last, 7:15, :])
        edge = joined(pad_ref[mine, 8:16, :])
        edge = pltpu.roll(edge, 6, 0)
        scaled = jnp.where(few, values.astype(BF16).astype(F32) * edge, 0.0)
        added = dot(scaled, jnp.where(few, in_map, 0.0), ((0,), (0,)))[0:HEAD_DIM, :]
        decay = jnp.exp(joined(pad_ref[mine, 0:8, :])[0:1, :])
        after = decay * entering.astype(F32) + pair_ref[0, h, 0:HEAD_DIM, :].astype(F32) + added
        pad = back_ref[h * each, part_rows:, :]
        enter_ref[0, h, 0:HEAD_DIM, :] = entering
        enter_ref[1, h, 0:HEAD_DIM, :] = after.astype(BF16)
        enter_ref[0, h, HEAD_DIM:, :] = pad
        enter_ref[1, h, HEAD_DIM:, :] = pad
    mine_ref[...] = enter_ref[core]
    give_ref[...] = enter_ref[1 - core]


def silu(x):
    return x * jax.nn.sigmoid(x)


def scan_kernel(got_ref, *rest):
    back_ref, pad_ref = rest[-2:]
    parts, padded, _ = got_ref.shape
    part_rows = padded - PAD
    rows = slice(0, part_rows)
    offset = lax.axis_index("frames") // 2 * part_rows % HEAD_DIM
    few = lax.broadcasted_iota(jnp.int32, (8, LANES), 0) < CONV - 1
    left = lax.broadcasted_iota(jnp.int32, (8, LANES), 1) < HEAD_DIM
    pad_ref[0:PAD, :] = jnp.zeros((PAD, LANES), F32)
    pad_ref[(parts + 1) * PAD :, :] = jnp.zeros((8, LANES), F32)
    for d in range(parts):
        pad_ref[(d + 1) * PAD : (d + 2) * PAD, :] = got_ref[d, part_rows:, :].astype(F32)
    carry = jnp.zeros((part_rows, LANES), F32)
    for d in range(parts):
        back_ref[d, rows, :] = carry.astype(BF16)
        back_ref[d, part_rows:, :] = pad_ref[d * PAD : (d + 1) * PAD, :].astype(BF16)
        last, mine = d * PAD, (d + 1) * PAD
        decay = pad_ref[mine : mine + 1, :]
        decay = jnp.exp(decay + pltpu.roll(decay, HEAD_DIM, 1))
        from_tail = pltpu.roll(pad_ref[last + 1 : last + 9, :], HEAD_DIM, 1)
        if part_rows < HEAD_DIM:
            from_tail = pltpu.roll(jnp.where(left, from_tail, 0.0), (LANES - offset) % LANES, 1)
        values = silu(pad_ref[mine + 1 : mine + 9, :] + from_tail)
        in_map = silu(pad_ref[mine + 4 : mine + 12, :] + pad_ref[last + 7 : last + 15, :])
        edge = pad_ref[mine + 10 : mine + 18, :]
        edge = edge + pltpu.roll(edge, HEAD_DIM, 1)
        scaled = jnp.where(few, values.astype(BF16).astype(F32) * edge, 0.0)
        in_map = jnp.where(few, in_map, 0.0)
        added = dot(scaled, in_map, ((0,), (0,)))
        carry = decay * carry + (got_ref[d, rows, :].astype(F32) + added[rows, :])


def mixed_values(affinity, cum, shifted, values, skip, pair):
    q_pos = lax.broadcasted_iota(jnp.int32, (SPAN, SPAN), 0)
    s_pos = lax.broadcasted_iota(jnp.int32, (SPAN, SPAN), 1)
    lower = q_pos >= s_pos
    left = lax.broadcasted_iota(jnp.int32, (SPAN, LANES), 1) < HEAD_DIM
    zero = jnp.zeros((SPAN, LANES), BF16)
    mixing = []
    for h in (2 * pair, 2 * pair + 1):
        gap = cum[:, h : h + 1] - shifted[h : h + 1, :]
        mixing.append(jnp.where(lower, affinity * jnp.exp(gap), 0.0).astype(BF16))
    both = jnp.concatenate(mixing, axis=1)
    stacked = jnp.concatenate([jnp.where(left, values, zero), jnp.where(left, zero, values)], axis=0)
    return dot(both, stacked) + skip * values.astype(F32)


def later_kernel(layer, act_ref, cum_ref, shifted_ref, skip_ref, sel_ref, y_ref, decay_ref):
    skip = spread_row(skip_ref[layer : layer + 1, :], sel_ref[...])
    for b in range(1, act_ref.shape[0] // SPAN):
        r = slice(b * SPAN, (b + 1) * SPAN)
        maps = act_ref[r, INNER:]
        affinity = dot(maps[:, STATE:], maps[:, :STATE], ((1,), (1,)))
        cum, shifted = cum_ref[r, :], shifted_ref[:, r]
        decays = split(jnp.exp(cum))
        for c in range(0, INNER, 256):
            decay_ref[(b - 1) * SPAN : b * SPAN, c : c + 256] = dot(decays, sel_ref[:, c : c + 256])
        for pair in range(HEADS // 2):
            cols = slice(pair * LANES, (pair + 1) * LANES)
            y_ref[(b - 1) * SPAN : b * SPAN, cols] = mixed_values(
                affinity, cum, shifted, act_ref[r, cols], skip[:, cols], pair
            )


def gate_kernel(layer, u_ref, w_ref, cum_ref, sel_ref, gate_ref, wide_ref):
    chunk = 256
    before = jnp.zeros((1, HEADS), F32)
    scales = []
    for b in range(u_ref.shape[0] // SPAN):
        cum = cum_ref[b * SPAN : (b + 1) * SPAN, :]
        scales.append(jnp.exp(cum + before))
        before = before + cum[SPAN - 1 : SPAN, :]
    scales = split(jnp.concatenate(scales, axis=0))
    for c in range(0, INNER, chunk):
        cols = slice(c, c + chunk)
        wide_ref[:, cols] = dot(scales, sel_ref[:, cols])
        gate_ref[:, cols] = silu(dot(u_ref[...], w_ref[layer, :, cols]).astype(BF16).astype(F32))


def finish_kernel(
    layer,
    gate_ref,
    wide_ref,
    later_ref,
    decay_ref,
    act_ref,
    own_ref,
    cum_ref,
    shifted_ref,
    edge_ref,
    state_ref,
    skip_ref,
    sel_ref,
    mine_ref,
    other_ref,
    resid_ref,
    wo_ref,
    gain_ref,
    mods_ref,
    *rest,
):
    hidden_ref, a_ref, first_ref, y_ref, normed_ref, enter_ref = rest[-6:]
    rows = gate_ref.shape[0]
    core = core_index()
    enter_ref[pl.ds(core * HALF, HALF)] = mine_ref[...]
    enter_ref[pl.ds((1 - core) * HALF, HALF)] = other_ref[...]
    start = (1 - core).astype(F32)
    sel = sel_ref[...]
    lane = lax.broadcasted_iota(jnp.int32, (SPAN, LANES), 1)
    left = lane < HEAD_DIM
    few = lax.broadcasted_iota(jnp.int32, (TAIL, LANES), 0) < CONV - 1
    nothing = jnp.zeros((TAIL - 8, LANES), F32)

    def fixed(cols, tail):
        total = jnp.concatenate([own_ref[:, cols] + start * tail[0:8, :], nothing], axis=0)
        first_ref[:, cols] = jnp.where(
            few, silu(total), act_ref[0:TAIL, cols].astype(F32)
        ).astype(BF16)

    for pair in range(HEADS // 2):
        pads = [
            enter_ref[h, HEAD_DIM:, :].astype(F32)
            for h in (2 * pair, 2 * pair + 1)
        ]
        tail = jnp.where(left[0:PAD], pltpu.roll(pads[0], HEAD_DIM, 1), pads[1])
        fixed(slice(pair * LANES, (pair + 1) * LANES), pltpu.roll(tail, PAD - 1, 0))
    common = enter_ref[0, HEAD_DIM:, :].astype(F32)
    fixed(slice(INNER, INNER + STATE), pltpu.roll(common, PAD - 7, 0))
    fixed(slice(INNER + STATE, INNER + 2 * STATE), pltpu.roll(common, PAD - 13, 0))

    def acts(b, cols):
        if b:
            return act_ref[b * SPAN : (b + 1) * SPAN, cols]
        return jnp.concatenate([first_ref[:, cols], act_ref[TAIL:SPAN, cols]], axis=0)

    first_tokens = lax.broadcasted_iota(jnp.int32, (TAIL, HEADS), 0) < CONV - 1
    early_scale = split(jnp.where(first_tokens, edge_ref[...], 0.0) * start)
    early_map = first_ref[:, INNER : INNER + STATE]
    spans = rows // SPAN
    out_maps = [acts(b, slice(INNER + STATE, INNER + 2 * STATE)) for b in range(spans)]
    out_map = jnp.concatenate(out_maps, axis=0)
    decayed = [jnp.ones((1, INNER), F32)]
    for b in range(1, spans - 1):
        end = (b + 1) * SPAN - 1
        decayed.append(decayed[-1] * spread_row(jnp.exp(cum_ref[end : end + 1, :]), sel))
    chunk = 256
    for c in range(0, INNER, chunk):
        cols = slice(c, c + chunk)
        entering = jnp.concatenate(
            [enter_ref[h, 0:HEAD_DIM, :] for h in range(c // HEAD_DIM, (c + chunk) // HEAD_DIM)],
            axis=0,
        )
        y_ref[:, cols] = dot(out_map, entering, ((1,), (1,))) * wide_ref[:, cols]
    early = (first_ref[:, 0:INNER].astype(F32) * dot(early_scale, sel)).astype(BF16)
    late = dot(early_map, early, ((0,), (0,)))
    for b in range(1, spans):
        r, own = slice(b * SPAN, (b + 1) * SPAN), slice((b - 1) * SPAN, b * SPAN)
        state = late if b == 1 else decayed[b - 1] * late
        state = state_ref[(b - 1) * STATE : b * STATE, :] + state
        within = later_ref[own, :] + dot(out_maps[b], state.astype(BF16)) * decay_ref[own, :]
        y_ref[r, :] = (y_ref[r, :] + within) * gate_ref[r, :]

    skip = spread_row(skip_ref[layer : layer + 1, :], sel)
    r = slice(0, SPAN)
    affinity = dot(out_maps[0], acts(0, slice(INNER, INNER + STATE)), ((1,), (1,)))
    cum, shifted = cum_ref[r, :], shifted_ref[:, r]
    for pair in range(HEADS // 2):
        cols = slice(pair * LANES, (pair + 1) * LANES)
        y = mixed_values(affinity, cum, shifted, acts(0, cols), skip[:, cols], pair)
        y_ref[r, cols] = (y + y_ref[r, cols]) * gate_ref[r, cols]

    row = lax.broadcasted_iota(jnp.int32, (chunk, chunk), 0) // HEAD_DIM
    col = lax.broadcasted_iota(jnp.int32, (chunk, chunk), 1) // HEAD_DIM
    same = jnp.where(row == col, 1.0 / HEAD_DIM, 0.0).astype(BF16)
    for c in range(0, INNER, chunk):
        cols = slice(c, c + chunk)
        total = y_ref[:, cols]
        square = total * total
        mean = dot(square.astype(BF16), same)
        gain = gain_ref[layer : layer + 1, cols]
        normed_ref[:, cols] = (total * lax.rsqrt(mean + HEAD_EPS) * gain).astype(BF16)
    hidden = resid_ref[...].astype(F32) + dot(normed_ref[...], wo_ref[layer])
    hidden_ref[...] = hidden
    a_ref[...] = rms_mod(hidden, mods_ref[layer, 2:3, :], mods_ref[layer, 3:4, :])


def partial_attention(q_ref, seen, kv, half, r, k_rows, done):
    left = lax.broadcasted_iota(jnp.int32, (half, LANES), 1) < HEAD_DIM
    one = jnp.ones((k_rows.stop - k_rows.start, LANES), BF16)
    zero = jnp.zeros((half, LANES), BF16)
    seen = jnp.concatenate([seen, seen], axis=0)
    together = 4
    for group in range(0, ATT_HEADS // 2, together):
        columns = [slice(p * LANES, (p + 1) * LANES) for p in range(group, group + together)]
        scores = []
        for cols in columns:
            query = q_ref[r, cols]
            sides = jnp.concatenate(
                [jnp.where(left, query, zero), jnp.where(left, zero, query)], axis=0
            )
            scores.append(dot(sides, kv[k_rows, cols], ((1,), (1,))) + seen)
        tops = [jnp.max(s, axis=-1, keepdims=True) for s in scores]
        weights = [jnp.exp(s - t).astype(BF16) for s, t in zip(scores, tops)]
        for cols, weight, top in zip(columns, weights, tops):
            values = kv[k_rows, ATTN + cols.start : ATTN + cols.stop]
            both = dot(weight, jnp.concatenate([values, one], axis=1))
            number = jnp.where(left, both[:half, :LANES], both[half:, :LANES])
            total = jnp.where(left, both[:half, LANES:], both[half:, LANES:])
            done(cols, number, total, jnp.where(left, top[:half], top[half:]))


def memory_kernel(
    layer, reach_ref, a_ref, wq_ref, wm_ref, q_ref, number_ref, total_ref, top_ref, seen_ref, kv_ref
):
    rows = a_ref.shape[0]
    half = rows // 2
    a = a_ref[...]
    tok_frame = rows // WINDOW
    key_frame = lax.broadcasted_iota(jnp.int32, (tok_frame, 2 * rows), 1) // tok_frame
    first = WINDOW - lax.axis_index("frames") * WINDOW
    for f in range(WINDOW):
        low = jnp.maximum(first, f + WINDOW - reach_ref[f])
        seen = (key_frame >= low) & (key_frame <= f + WINDOW)
        seen_ref[f * tok_frame : (f + 1) * tok_frame, :] = jnp.where(seen, 0.0, -1e30)
    q_ref[...] = (dot(a, wq_ref[layer]).astype(BF16).astype(F32) * HEAD_DIM**-0.5).astype(BF16)
    kv_ref[...] = dot(a, wm_ref[layer]).astype(BF16)
    for part in range(2):
        r = slice(part * half, (part + 1) * half)
        k_rows = slice(0, (part + 1) * half)

        def done(cols, number, total, top):
            number_ref[r, cols] = number
            total_ref[r, cols] = total
            top_ref[r, cols] = top

        seen = seen_ref[r, rows : rows + k_rows.stop]
        partial_attention(q_ref, seen, kv_ref, half, r, k_rows, done)


def attend_kernel(
    layer,
    last,
    q_ref,
    number_ref,
    total_ref,
    top_ref,
    seen_ref,
    prev_ref,
    wm_ref,
    merge_ref,
    hidden_ref,
    mods_ref,
    *rest,
):
    if last:
        resid_ref, kv_ref, out_ref = rest
    else:
        resid_ref, u_ref, tail_ref, kv_ref, out_ref = rest
    rows = q_ref.shape[0]
    half = rows // 2
    kv_ref[...] = dot(prev_ref[...], wm_ref[layer]).astype(BF16)
    for part in range(2):
        r = slice(part * half, (part + 1) * half)
        k_rows = slice(part * half, rows)

        def done(cols, number, total, top):
            top_own = top_ref[r, cols]
            highest = jnp.maximum(top, top_own)
            mine, own = jnp.exp(top - highest), jnp.exp(top_own - highest)
            number = number * mine + number_ref[r, cols] * own
            total = total * mine + total_ref[r, cols] * own
            out_ref[r, cols] = (number / total).astype(BF16)

        partial_attention(q_ref, seen_ref[r, k_rows], kv_ref, half, r, k_rows, done)
    resid = hidden_ref[...] + dot(out_ref[...], merge_ref[layer])
    resid_ref[...] = resid
    if not last:
        u = rms_mod(resid, mods_ref[layer + 1, 0:1, :], mods_ref[layer + 1, 1:2, :])
        u_ref[...] = u
        tail_ref[...] = u[rows - TAIL :]


WHOLE = pl.BlockSpec(memory_space=pltpu.VMEM)
SCALARS = pl.BlockSpec(memory_space=pltpu.SMEM)


def run(kernel, operands, outs, scratch=(), name=None, flops=0, scalars=()):
    moved = sum(o.size * o.dtype.itemsize for o in list(operands) + list(outs))
    return pl.pallas_call(
        kernel,
        in_specs=[SCALARS] * len(scalars) + [WHOLE] * len(operands),
        out_specs=[WHOLE] * len(outs),
        out_shape=list(outs),
        scratch_shapes=list(scratch),
        compiler_params=pltpu.CompilerParams(vmem_limit_bytes=20 * 1024 * 1024),
        cost_estimate=pl.CostEstimate(flops=flops, bytes_accessed=moved, transcendentals=0),
        name=name,
    )(*scalars, *operands)


def shape(dims, dtype):
    return jax.ShapeDtypeStruct(dims, dtype)


def swapped(value, axis):
    count = lax.axis_size(axis)
    return lax.ppermute(value, axis, [(i, i ^ 1) for i in range(count)])


def over_chips(value, axis):
    count = lax.axis_size(axis)
    groups = [list(range(core, count, 2)) for core in range(2)]
    return lax.all_to_all(value, axis, 0, 0, axis_index_groups=groups)


def from_behind(value, axis):
    count = lax.axis_size(axis)
    return lax.ppermute(value, axis, [(i, i + 1) for i in range(count - 1)])


def shards(
    latents,
    timestep,
    lookback,
    modulation,
    input_weight,
    step_weight,
    conv_weight,
    step_bias,
    decay_log,
    skip_gain,
    norm_gain,
    output_weight,
    query_weight,
    memory_weight,
    merge_weight,
):
    frames_dev, tok_frame, width = latents.shape
    rows = frames_dev * tok_frame
    spans = rows // SPAN
    parts = lax.axis_size("frames") // 2
    part_rows = HALF * HEAD_DIM // parts
    mixed = INNER + 2 * STATE
    step_weight = jnp.swapaxes(step_weight, 1, 2)
    step_bias = jnp.swapaxes(step_bias, 1, 2)
    resid = latents.reshape(rows, width)
    (sel,) = run(
        select_kernel, (), [shape((2 * HEADS, INNER), BF16)], name="select", flops=OPENING
    )
    u, tail, mods, bias = run(
        first_kernel,
        (sel, resid, modulation, step_bias),
        [
            shape((rows, width), BF16),
            shape((TAIL, width), BF16),
            shape((LAYERS,) + modulation.shape[2:], F32),
            shape((LAYERS, 8, HEADS), F32),
        ],
        name="first",
        flops=OPENING,
        scalars=(timestep,),
    )
    for layer in range(LAYERS):
        before = swapped(tail, "frames")
        act, own, cum, shifted, edge, state, keep, give = run(
            functools.partial(local_kernel, layer),
            (u, before, input_weight, step_weight, conv_weight, bias, decay_log, sel),
            [
                shape((rows, mixed), BF16),
                shape((8, mixed), F32),
                shape((rows, HEADS), F32),
                shape((HEADS, rows), F32),
                shape((TAIL, HEADS), F32),
                shape((max(spans - 1, 1) * STATE, INNER), F32),
                shape((HALF, BLOCK, LANES), BF16),
                shape((HALF, BLOCK, LANES), BF16),
            ],
            [
                pltpu.VMEM((2, rows + 2 * TAIL, 256), F32),
                pltpu.VMEM((8, mixed), F32),
                pltpu.VMEM((HEADS, PAD, LANES), F32),
                pltpu.VMEM((HEADS, BLOCK, LANES), BF16),
                pltpu.VMEM((rows, INNER), BF16),
            ],
            name="local",
            flops=2 * rows * width * mixed,
        )
        got = swapped(give, "frames")
        later, decays = run(
            functools.partial(later_kernel, layer),
            (act, cum, shifted, skip_gain, sel),
            [shape((max(spans - 1, 1) * SPAN, INNER), F32)] * 2,
            name="later",
            flops=2 * rows * SPAN * INNER,
        )
        got, later, decays = lax.optimization_barrier((got, later, decays))
        (send,) = run(
            chip_kernel,
            (keep, got),
            [shape((parts, part_rows + PAD, LANES), BF16)],
            [pltpu.VMEM((2, HALF, BLOCK, LANES), BF16)],
            name="chip",
        )
        (back,) = run(
            scan_kernel,
            (over_chips(send, "frames"),)
            + (() if layer else (output_weight, norm_gain, query_weight, memory_weight, merge_weight)),
            [shape(send.shape, BF16)],
            [pltpu.VMEM(((parts + 1) * PAD + 8, LANES), F32)],
            name="scan",
        )
        mine, give = run(
            enter_kernel,
            (keep, got, over_chips(back, "frames")),
            [shape(keep.shape, BF16)] * 2,
            [
                pltpu.VMEM((2, HALF, BLOCK, LANES), BF16),
                pltpu.VMEM((2, HALF, BLOCK, LANES), BF16),
                pltpu.VMEM((HEADS, PAD, LANES), F32),
            ],
            name="enter",
        )
        give, u = lax.optimization_barrier((give, u))
        other = swapped(give, "frames")
        gate, wide = run(
            functools.partial(gate_kernel, layer),
            (u, input_weight, cum, sel),
            [shape((rows, INNER), F32)] * 2,
            name="gate",
            flops=2 * rows * width * INNER,
        )
        hidden, a = run(
            functools.partial(finish_kernel, layer),
            (gate, wide, later, decays, act, own, cum, shifted, edge, state, skip_gain, sel)
            + (mine, other, resid, output_weight, norm_gain, mods),
            [shape((rows, width), F32), shape((rows, width), BF16)],
            [
                pltpu.VMEM((TAIL, mixed), BF16),
                pltpu.VMEM((rows, INNER), F32),
                pltpu.VMEM((rows, INNER), BF16),
                pltpu.VMEM((HEADS, BLOCK, LANES), BF16),
            ],
            name="finish",
        )
        prev = from_behind(a, "frames")
        q, number, total, top, seen = run(
            functools.partial(memory_kernel, layer),
            (a, query_weight, memory_weight),
            [shape((rows, ATTN), BF16)]
            + [shape((rows, ATTN), F32)] * 3
            + [shape((rows, 2 * rows), F32)],
            [pltpu.VMEM((rows, 2 * ATTN), BF16)],
            name="memory",
            scalars=(lookback,),
            flops=2 * rows * width * 3 * ATTN,
        )
        last = layer == LAYERS - 1
        outs = [shape((rows, width), F32)]
        if not last:
            outs += [shape((rows, width), BF16), shape((TAIL, width), BF16)]
        result = run(
            functools.partial(attend_kernel, layer, last),
            (q, number, total, top, seen, prev, memory_weight, merge_weight, hidden, mods),
            outs,
            [pltpu.VMEM((rows, 2 * ATTN), BF16), pltpu.VMEM((rows, ATTN), BF16)],
            name="attend",
        )
        resid = result[0]
        if not last:
            u, tail = result[1:]
    return resid.reshape(latents.shape)


def solution(mesh):
    sharded = P(("groups", "frames"))
    return jax.shard_map(
        shards,
        mesh=mesh,
        in_specs=(P(("groups", "frames"), None, None), sharded, sharded) + (P(),) * 12,
        out_specs=P(("groups", "frames"), None, None),
        check_vma=False,
    )
```
